32 devices in a mesh: front: 4 (over x, core), grp: 8 (over z, y).
Axes of the slice: x: 2, y: 2, z: 4, core: 2. Of those that a mesh axis runs over, the one named last changes fastest.
Arguments:
- front_in: bfloat16 [4, 8192, 8192], P('front', None, 'grp'), may hold values from -6 to 6
- panel_inverse: float32 [4, 2, 256, 256], P('front'), may hold values from -2 to 2, as said below
- tile_mask: int32 [4, 32, 32], P('front', None, 'grp'), may hold values 0 or 1
- tile_map: int32 [4, 8, 4], P('front', 'grp'), may hold values from 0 to 127, as said below
Outputs:
- front_out: bfloat16 [4, 8192, 8192], P('front', None, 'grp')
- parent_tiles: float32 [128, 256, 256], P(('front', 'grp'))
The draws below stay inside these ranges and needn't reach their ends.
Inputs may be any that keep to these rules, and one draw needn't show every extreme that they name: `panel_inverse`: lower triangular, with a positive diagonal. `tile_map`: entry s names device s // 4 of the mesh (front slowest), parent front s // 32. The 4 tiles of one front and one index of grp go to exactly 2 tiles each of 2 distinct parent fronts. Of all tiles from fronts' devices with the same grp index that go to one parent front, no two go to the same device of that parent's group.
All inputs are finite; a program needn't handle non-finite values. No bound on the sum of `tile_mask` on one device may be relied on, other than what follows from the above.
Results may differ from the reference program's by a relative error of at most 0.006.
Values may be sent and summed in bfloat16 or wider, within the bound.
No kernel may reach another device: no remote copies, remote signals or barrier semaphores. Data moves between devices by JAX's collectives and lax.ppermute only.
A program may use at most 192 MiB of HBM per device.

```python
import math
import jax
import jax.numpy as jnp
from jax import lax

TILE = 256
ORDER = 8192
FRONTS = 4
TILES = 32
COLS_DEV = 4
CONTRIB = 4
ROWS_OUT = 1
PER_PARENT = 2
SLOTS = 4
N_GRP = 8


def draw_panel_inverse(key, part):
    first_key, second_key = jax.random.split(jax.random.fold_in(key, 11))
    shape = (FRONTS, 2, TILE, TILE)
    lower_part = jax.random.normal(first_key, shape, jnp.float32) * (0.25 / math.sqrt(TILE))
    diagonal = jax.random.uniform(second_key, shape[:-1], jnp.float32, 0.15, 0.45)
    rows = jax.lax.broadcasted_iota(jnp.int32, (TILE, TILE), 0)
    cols = jax.lax.broadcasted_iota(jnp.int32, (TILE, TILE), 1)
    result = jnp.where(rows > cols, lower_part, 0.0) + jnp.where(rows == cols, diagonal[..., None], 0.0)
    return result.astype(jnp.float32)


def draw_tile_map(key, part):
    front_key, owner_key, slot_key = jax.random.split(jax.random.fold_in(key, 23), 3)
    front_keys = jax.random.split(front_key, FRONTS * N_GRP)
    front_perm = jax.vmap(lambda single: jax.random.permutation(single, FRONTS))(front_keys)
    front_perm = front_perm.reshape(FRONTS, N_GRP, FRONTS).astype(jnp.int32)
    owner_keys = jax.random.split(owner_key, FRONTS * N_GRP)
    owner_perm = jax.vmap(lambda single: jax.random.permutation(single, N_GRP))(owner_keys)
    owner_perm = owner_perm.reshape(FRONTS, N_GRP, N_GRP).astype(jnp.int32)
    number = jnp.arange(CONTRIB, dtype=jnp.int32)
    parent = front_perm[:, :, number // PER_PARENT]
    within = (number % PER_PARENT)[None, None, :]
    source = jnp.arange(FRONTS, dtype=jnp.int32)[:, None, None]
    column = jnp.arange(N_GRP, dtype=jnp.int32)[None, :, None]
    position = source * PER_PARENT + within
    owner = owner_perm[parent, column, position]
    slot = jax.random.randint(slot_key, (FRONTS, N_GRP, CONTRIB), 0, SLOTS, jnp.int32)
    return ((parent * N_GRP + owner) * SLOTS + slot).astype(jnp.int32)


def place_ends(entries, own_key, low, high):
    longest = entries.shape.index(max(entries.shape))
    spots = []
    for shift in (0, 1):
        where = [jax.random.randint(jax.random.fold_in(own_key, axis), (), 0, length) for axis, length in enumerate(entries.shape)]
        where[longest] = (where[longest] + shift) % entries.shape[longest]
        spots.append(tuple(where))
    return entries.at[spots[0]].set(low).at[spots[1]].set(high)


def steps_of(key, dims, cuts, low, top_value):
    gain, own = 1.0, jax.random.fold_in(key, 6)
    for dim, parts in cuts:
        heights = jnp.exp(jax.random.uniform(jax.random.fold_in(own, dim), (parts,), jnp.float32, low / len(cuts), top_value / len(cuts)))
        gain = gain * jnp.repeat(heights, dims[dim] // parts).reshape([-1 if axis == dim else 1 for axis in range(len(dims))])
    return gain


def scatter_about(rng, extent, deviation, bound, shards=(), kind=jnp.bfloat16):
    values = deviation * jax.random.normal(rng, extent, jnp.float32)
    if shards:
        values = values * steps_of(rng, extent, shards, -0.22, 0.18)
    return jnp.clip(values, -bound, bound).astype(kind)


def setup_inputs(seed: int = 0) -> dict:
    splits = jax.random.split(jax.random.key(seed), 5)
    return {
        "front_in": scatter_about(splits[0], (FRONTS, ORDER, ORDER), 1.0, 6.0, ((0, 4), (2, 8))),
        "panel_inverse": draw_panel_inverse(jax.random.fold_in(splits[4], 71), 0),
        "tile_mask": place_ends((jax.random.randint(splits[2], (FRONTS, TILES, TILES), 0, 4) < 3).astype(jnp.int32), jax.random.fold_in(splits[2], 1), 0, 1),
        "tile_map": draw_tile_map(jax.random.fold_in(splits[4], 71), 0),
    }


def one_front(items):
    front, inverse, mask = items
    working = front.astype(jnp.float32)
    row_tiles = (jnp.arange(ORDER, dtype=jnp.int32) // TILE)[:, None]
    tile_index = jnp.arange(TILES, dtype=jnp.int32)
    keep_mask = mask.astype(jnp.float32)

    def factor(block, which):
        product = jnp.dot(block, inverse[which].T, precision=lax.Precision.HIGHEST, preferred_element_type=jnp.float32)
        return jnp.where(row_tiles > which, product, 0.0).astype(jnp.bfloat16)

    def trailing(working, panel, which):
        update = jnp.dot(panel, panel.T, preferred_element_type=jnp.float32)
        inside = (tile_index[:, None] > which) & (tile_index[None, :] > which)
        keep = keep_mask * inside.astype(jnp.float32)
        update = update.reshape(TILES, TILE, TILES, TILE) * keep[:, None, :, None]
        return working - update.reshape(ORDER, ORDER)

    first = factor(working[:, :TILE], 0)
    working = trailing(working, first, 0)
    second = factor(working[:, TILE:2 * TILE], 1)
    working = trailing(working, second, 1)
    result = working.astype(jnp.bfloat16)
    result = result.at[:, :TILE].set(jnp.where(row_tiles > 0, first, result[:, :TILE]))
    result = result.at[:, TILE:2 * TILE].set(jnp.where(row_tiles > 1, second, result[:, TILE:2 * TILE]))
    return result


def reference(front_in, panel_inverse, tile_mask, tile_map):
    front_out = lax.map(one_front, (front_in, panel_inverse, tile_mask))
    bottom = front_out[:, (TILES - ROWS_OUT) * TILE:, :]
    bottom = bottom.reshape(FRONTS, ROWS_OUT, TILE, N_GRP, COLS_DEV, TILE)
    bottom = jnp.transpose(bottom, (0, 3, 4, 1, 2, 5)).reshape(FRONTS * N_GRP * CONTRIB, TILE, TILE)
    parent_tiles = jax.ops.segment_sum(bottom.astype(jnp.float32), tile_map.reshape(-1), num_segments=FRONTS * N_GRP * SLOTS)
    return front_out, parent_tiles
```

```python
import functools

import jax
import jax.numpy as jnp
from jax import lax
from jax.experimental import pallas as pl
from jax.experimental.pallas import tpu as pltpu
from jax.sharding import PartitionSpec as P

TILE = 256
VMEM_LIMIT = 40 * 1024 * 1024


def ring_order(n_grp):
    depth = 4 if n_grp % 4 == 0 and n_grp >= 8 else 1
    width = n_grp // depth
    if depth == 1:
        return list(range(n_grp))
    order = [z * width for z in range(depth)]
    for number, z in enumerate(reversed(range(depth))):
        ys = range(1, width) if number % 2 == 0 else range(width - 1, 0, -1)
        order += [z * width + y for y in ys]
    return order


def stream_plan(n_grp, tiles, cols_dev, rows_out):
    cycle = ring_order(n_grp)
    paths = [cycle, [cycle[0]] + cycle[:0:-1]]
    place = [{g: d for d, g in enumerate(path)} for path in paths]
    lists = [[], []]
    bottom = [tiles - 1 - r for r in range(rows_out)]
    rest = []
    for g in range(n_grp):
        for c in range(cols_dev):
            tile = g * cols_dev + c
            if tile and tile not in bottom:
                rest.append((g, tile))
    for number, tile in enumerate(bottom):
        lists[number % 2].append(tile)
    rest.sort(key=lambda item: (-min(place[0][item[0]], place[1][item[0]]), item[1]))
    for g, tile in rest:
        near = [place[s][g] for s in (0, 1)]
        if near[0] == near[1] or g == 0:
            which = 0 if len(lists[0]) <= len(lists[1]) else 1
        else:
            which = 0 if near[0] < near[1] else 1
        lists[which].append(tile)
    return paths, place, lists


def split3(x):
    hi = x.astype(jnp.bfloat16)
    rest = x - hi.astype(jnp.float32)
    mid = rest.astype(jnp.bfloat16)
    low = (rest - mid.astype(jnp.float32)).astype(jnp.bfloat16)
    return hi, mid, low


def dot_t(a, b):
    return lax.dot_general(a, b, (((1,), (1,)), ((), ())), preferred_element_type=jnp.float32)


def factor_kernel(rows, mask, block, top, inverse, out, first_one):
    step = pl.program_id(0)
    row = rows[step]

    def first_of(x):
        return sum(dot_t(x, part) for part in reversed(split3(inverse[0]))).astype(jnp.bfloat16)

    @pl.when(step == 0)
    def _():
        first_one[...] = first_of(top[...])

    first = first_of(block[:, :TILE])
    first = jnp.where(row > 0, first, jnp.zeros_like(first))
    update = dot_t(first, first_one[...])
    keep = mask[row, 1] > 0
    work = block[:, TILE:].astype(jnp.float32) - jnp.where(keep, update, 0.0)
    ah, am, al = split3(work)
    bh, bm, bl = split3(inverse[1])
    small = dot_t(al, bh) + dot_t(ah, bl) + dot_t(am, bm)
    second = (small + (dot_t(am, bh) + dot_t(ah, bm)) + dot_t(ah, bh)).astype(jnp.bfloat16)
    second = jnp.where(row > 1, second, jnp.zeros_like(second))
    out[0, :, :TILE] = first
    out[0, :, TILE:] = second


def factor(front, inverse, mask, rows):
    count = len(rows)
    return pl.pallas_call(
        factor_kernel,
        out_shape=jax.ShapeDtypeStruct((count, TILE, 2 * TILE), jnp.bfloat16),
        grid_spec=pltpu.PrefetchScalarGridSpec(
            num_scalar_prefetch=2,
            grid=(count,),
            in_specs=[
                pl.BlockSpec((TILE, 2 * TILE), lambda s, rows, mask: (rows[s], 0)),
                pl.BlockSpec((TILE, TILE), lambda s, rows, mask: (1, 0)),
                pl.BlockSpec((2, TILE, TILE), lambda s, rows, mask: (0, 0, 0)),
            ],
            out_specs=pl.BlockSpec((1, TILE, 2 * TILE), lambda s, rows, mask: (s, 0, 0)),
            scratch_shapes=[pltpu.VMEM((TILE, TILE), jnp.bfloat16)],
        ),
        compiler_params=pltpu.CompilerParams(vmem_limit_bytes=VMEM_LIMIT),
        cost_estimate=pl.CostEstimate(
            flops=20 * count * TILE**3, bytes_accessed=4 * count * TILE * 2 * TILE, transcendentals=0
        ),
        name="factor",
    )(jnp.asarray(rows, jnp.int32), mask, front, front, inverse)


def gather_kernel(choices, sources, me, *refs):
    blocks, (out, sem) = refs[:sources], refs[sources:]
    for part, options in enumerate(choices):
        for g, (source, index) in enumerate(options):
            block = blocks[source] if index is None else blocks[source].at[index]

            @pl.when(me[0] == g)
            def _():
                pltpu.make_async_copy(block, out.at[pl.ds(part * TILE, TILE)], sem.at[part]).start()

    for part, options in enumerate(choices):
        source, index = options[0]
        block = blocks[source] if index is None else blocks[source].at[index]
        pltpu.make_async_copy(block, out.at[pl.ds(part * TILE, TILE)], sem.at[part]).wait()


def gather(me, blocks, choices):
    parts = len(choices)
    return pl.pallas_call(
        functools.partial(gather_kernel, choices, len(blocks)),
        out_shape=jax.ShapeDtypeStruct((parts * TILE, 2 * TILE), jnp.bfloat16),
        in_specs=[pl.BlockSpec(memory_space=pltpu.SMEM)] + [pl.BlockSpec(memory_space=pl.ANY)] * len(blocks),
        out_specs=pl.BlockSpec(memory_space=pl.ANY),
        scratch_shapes=[pltpu.SemaphoreType.DMA((parts,))],
        cost_estimate=pl.CostEstimate(flops=0, bytes_accessed=4 * parts * TILE * 2 * TILE, transcendentals=0),
        name="gather_own",
    )(me, *blocks)


def update_kernel(count, cols_dev, stacked, rows, mask, me, block, own, *refs):
    panels, out = refs[:-1] if stacked else refs[:count], refs[-1]
    step = pl.program_id(0)
    row = rows[step]

    def run(panel):
        for c in range(cols_dev):
            span = slice(c * TILE, (c + 1) * TILE)
            update = dot_t(panel[...], own[span, :])
            keep = (mask[row, c] > 0) & (row > 0)
            old = block[:, span].astype(jnp.float32)
            out[:, span] = (old - jnp.where(keep, update, 0.0)).astype(jnp.bfloat16)

        @pl.when((me[0] == 0) & (row > 0))
        def _():
            out[:, :TILE] = panel[:, :TILE]

        @pl.when((me[0] == 0) & (row > 1))
        def _():
            out[:, TILE : 2 * TILE] = panel[:, TILE:]

    if stacked:
        run(panels[0])
    else:
        for number in range(count):
            pl.when(step == number)(functools.partial(run, panels[number]))


def update(me, mask, front, own, rows, panels, base=None, out_rows=None):
    width = front.shape[1]
    cols_dev = width // TILE
    count = rows.shape[0]
    stacked = not isinstance(panels, (list, tuple))
    if out_rows is None:
        out_shape = jax.ShapeDtypeStruct(front.shape, jnp.bfloat16)
        out_spec = pl.BlockSpec((TILE, width), lambda s, rows, mask, me: (rows[s], 0))
    else:
        out_shape = jax.ShapeDtypeStruct((out_rows * TILE, width), jnp.bfloat16)
        out_spec = pl.BlockSpec((TILE, width), lambda s, rows, mask, me: (s, 0))
    in_specs = [
        pl.BlockSpec((TILE, width), lambda s, rows, mask, me: (rows[s], 0)),
        pl.BlockSpec((width, 2 * TILE), lambda s, rows, mask, me: (0, 0)),
    ]
    if stacked:
        in_specs.append(pl.BlockSpec((TILE, 2 * TILE), lambda s, rows, mask, me: (s, 0)))
        operands = [front, own, panels]
    else:
        in_specs += [pl.BlockSpec((TILE, 2 * TILE), lambda s, rows, mask, me: (0, 0))] * count
        operands = [front, own, *panels]
    aliases = {}
    if base is not None:
        in_specs.append(pl.BlockSpec(memory_space=pl.ANY))
        operands.append(base)
        aliases = {3 + len(operands) - 1: 0}
    return pl.pallas_call(
        functools.partial(update_kernel, count, cols_dev, stacked),
        out_shape=out_shape,
        grid_spec=pltpu.PrefetchScalarGridSpec(
            num_scalar_prefetch=3, grid=(count,), in_specs=in_specs, out_specs=out_spec
        ),
        input_output_aliases=aliases,
        compiler_params=pltpu.CompilerParams(vmem_limit_bytes=VMEM_LIMIT),
        cost_estimate=pl.CostEstimate(
            flops=2 * count * TILE * width * 2 * TILE, bytes_accessed=4 * count * TILE * width, transcendentals=0
        ),
        name="update",
    )(rows, mask, me, *operands)


def shards(front_in, panel_inverse, tile_mask, tile_map):
    front = front_in[0]
    width = front.shape[1]
    tiles = front.shape[0] // TILE
    cols_dev = width // TILE
    inverse = panel_inverse[0]
    mask = tile_mask[0]
    targets = tile_map[0, 0]
    contrib = targets.shape[0]
    rows_out = contrib // cols_dev
    n_grp = lax.axis_size("grp")
    n_front = lax.axis_size("front")
    n_dev = n_grp * n_front
    slots_dev = n_grp // 2
    g = lax.axis_index("grp")
    me = jnp.reshape(g, (1,)).astype(jnp.int32)
    root = g == 0

    labels = lax.all_to_all(
        jnp.broadcast_to(targets[None], (n_dev, contrib)), ("front", "grp"), split_axis=0, concat_axis=0, tiled=True
    )

    paths, place, lists = stream_plan(n_grp, tiles, cols_dev, rows_out)
    head = [lists[0][0], lists[1][0]]
    others = [tile for pair in zip(lists[0][1:], lists[1][1:]) for tile in pair]
    others += [tile for tile in lists[0] + lists[1] if tile not in head + others] + [0]
    made_head = factor(front, inverse, mask, head)
    made = factor(front, inverse, mask, others)
    where_made = {tile: (0, n) for n, tile in enumerate(head)}
    where_made.update({tile: (1, n) for n, tile in enumerate(others)})

    def made_block(tile):
        which, n = where_made[tile]
        return (made_head, made)[which][n]

    rounds = [len(lists[s]) + n_grp - 1 for s in (0, 1)]
    held = [[], []]
    for t in range(max(rounds)):
        for s in (0, 1):
            count = len(lists[s])
            if t >= rounds[s]:
                continue
            if t == 0:
                value = made_block(lists[s][0])
            else:
                pairs = [
                    (paths[s][d], paths[s][d + 1]) for d in range(n_grp - 1) if 0 <= t - 1 - d < count
                ]
                value = lax.ppermute(held[s][t - 1], "grp", pairs)
                if t < count:
                    value = jnp.where(root, made_block(lists[s][t]), value)
            held[s].append(value)

    distance = [jnp.asarray([place[s][n] for n in range(n_grp)], jnp.int32)[g] for s in (0, 1)]
    padded = [jnp.asarray(lists[s] + [0], jnp.int32) for s in (0, 1)]

    def rows_of(slots):
        result = []
        for s, t in slots:
            index = t - distance[s]
            inside = (index >= 0) & (index < len(lists[s]))
            result.append(padded[s][jnp.where(inside, index, len(lists[s]))])
        return jnp.stack(result)

    spot = {tile: (s, n) for s in (0, 1) for n, tile in enumerate(lists[s])}
    blocks, names = [made_head, made], {}

    def choice(tile, n):
        if n == 0:
            which, index = where_made[tile]
            return (which, index)
        s, number = spot[tile]
        slot = (s, number + place[s][n])
        if slot not in names:
            names[slot] = len(blocks)
            blocks.append(held[s][slot[1]])
        return (names[slot], None)

    choices = [[choice(n * cols_dev + c, n) for n in range(n_grp)] for c in range(cols_dev)]
    choices += [[choice(tiles - rows_out + r, n) for n in range(n_grp)] for r in range(rows_out)]
    gathered = gather(me, blocks, choices)
    own, ends = gathered[:width], gathered[width:]
    ready = max(slot[1] for slot in names)

    bottom_rows = jnp.arange(tiles - rows_out, tiles, dtype=jnp.int32)
    bottom = update(me, mask, front, own, bottom_rows, ends, out_rows=rows_out)

    piece = TILE // n_dev
    pieces = bottom.reshape(rows_out, n_dev, piece, cols_dev, TILE)
    pieces = jnp.transpose(pieces, (1, 3, 0, 2, 4)).reshape(n_dev, contrib, piece, TILE)
    arrived = lax.all_to_all(pieces, ("front", "grp"), split_axis=0, concat_axis=0, tiled=True)
    picker = labels.reshape(-1)[None, :] == jnp.arange(n_dev * slots_dev, dtype=jnp.int32)[:, None]
    sums = jnp.dot(
        picker.astype(jnp.bfloat16),
        arrived.reshape(n_dev * contrib, piece * TILE),
        preferred_element_type=jnp.float32,
    ).astype(jnp.bfloat16)
    sums = lax.all_to_all(
        sums.reshape(n_dev, slots_dev, piece, TILE), ("front", "grp"), split_axis=0, concat_axis=0, tiled=True
    )
    parent_tiles = jnp.transpose(sums, (1, 0, 2, 3)).reshape(slots_dev, TILE, TILE).astype(jnp.float32)

    result = None
    backlog = [(s, t) for t in range(ready + 1) for s in (0, 1) if t < rounds[s]]
    for t in range(ready + 1, max(rounds)):
        backlog += [(s, t) for s in (0, 1) if t < rounds[s]]
        take = min(len(backlog), 8)
        if t == max(rounds) - 1:
            take = len(backlog)
        slots, backlog = backlog[:take], backlog[take:]
        result = update(me, mask, front, own, rows_of(slots), [held[s][n] for s, n in slots], base=result)
    return (result[None], parent_tiles)


def solution(mesh):
    in_specs = (
        P("front", None, "grp"),
        P("front", None, None, None),
        P("front", None, "grp"),
        P("front", "grp", None),
    )
    out_specs = (P("front", None, "grp"), P(("front", "grp"), None, None))
    return jax.shard_map(shards, mesh=mesh, in_specs=in_specs, out_specs=out_specs, check_vma=False)
```

```python
import functools

import jax
import jax.numpy as jnp
from jax import lax
from jax.experimental import pallas as pl
from jax.experimental.pallas import tpu as pltpu
from jax.sharding import PartitionSpec as P

TILE = 256
HALF = 128
VMEM_LIMIT = 40 * 1024 * 1024


def ring_order(n_grp):
    depth = 4 if n_grp % 4 == 0 and n_grp >= 8 else 1
    width = n_grp // depth
    if depth == 1:
        return list(range(n_grp))
    order = [z * width for z in range(depth)]
    for number, z in enumerate(reversed(range(depth))):
        ys = range(1, width) if number % 2 == 0 else range(width - 1, 0, -1)
        order += [z * width + y for y in ys]
    return order


def stream_plan(n_grp, tiles, cols_dev, rows_out):
    cycle = ring_order(n_grp)
    paths = [cycle, [cycle[0]] + cycle[:0:-1]]
    place = [{g: d for d, g in enumerate(path)} for path in paths]
    lists = [[], []]
    bottom = [tiles - 1 - r for r in range(rows_out)]
    rest = []
    for g in range(n_grp):
        for c in range(cols_dev):
            tile = g * cols_dev + c
            if tile and tile not in bottom:
                rest.append((g, tile))
    for number, tile in enumerate(bottom):
        lists[number % 2].append(tile)
    rest.sort(key=lambda item: (-min(place[0][item[0]], place[1][item[0]]), item[1]))
    for g, tile in rest:
        near = [place[s][g] for s in (0, 1)]
        if near[0] == near[1] or g == 0:
            which = 0 if len(lists[0]) <= len(lists[1]) else 1
        else:
            which = 0 if near[0] < near[1] else 1
        lists[which].append(tile)
    return paths, place, lists


def split2(x):
    hi = x.astype(jnp.bfloat16)
    return hi, (x - hi.astype(jnp.float32)).astype(jnp.bfloat16)


def dot(a, b):
    return jnp.dot(a, b, preferred_element_type=jnp.float32)


def factor_kernel(per_step, rows, mask, *refs):
    blocks, (top, inverse, out, parts, one) = refs[:per_step], refs[per_step:]
    step = pl.program_id(0)

    def first_of(x):
        return (dot(x, parts[1]) + dot(x, parts[0])).astype(jnp.bfloat16)

    @pl.when(step == 0)
    def _():
        for which in range(2):
            hi, low = split2(inverse[which].T)
            parts[2 * which] = hi
            parts[2 * which + 1] = low
        one[...] = first_of(top[...]).astype(jnp.float32).T.astype(jnp.bfloat16)

    stack = [block[...] for block in blocks]
    firsts = first_of(jnp.concatenate([block[:, :TILE] for block in stack], axis=0))
    updates = dot(firsts, one[...])
    works = []
    for n, block in enumerate(stack):
        keep = mask[rows[step * per_step + n], 1] > 0
        works.append(
            block[:, TILE:].astype(jnp.float32) - jnp.where(keep, updates[n * TILE : (n + 1) * TILE], 0.0)
        )
    high, low = split2(jnp.concatenate(works, axis=0))
    seconds = (dot(low, parts[2]) + dot(high, parts[3]) + dot(high, parts[2])).astype(jnp.bfloat16)
    for n in range(per_step):
        row = rows[step * per_step + n]
        first, second = firsts[n * TILE : (n + 1) * TILE], seconds[n * TILE : (n + 1) * TILE]
        out[n, :, :TILE] = jnp.where(row > 0, first, jnp.zeros_like(first))
        out[n, :, TILE:] = jnp.where(row > 1, second, jnp.zeros_like(second))


def factor(front, inverse, mask, rows):
    count = len(rows)
    per_step = 2 if count % 2 == 0 else 1

    def block_spec(n):
        return pl.BlockSpec((TILE, 2 * TILE), lambda s, rows, mask: (rows[s * per_step + n], 0))

    return pl.pallas_call(
        functools.partial(factor_kernel, per_step),
        out_shape=jax.ShapeDtypeStruct((count, TILE, 2 * TILE), jnp.bfloat16),
        grid_spec=pltpu.PrefetchScalarGridSpec(
            num_scalar_prefetch=2,
            grid=(count // per_step,),
            in_specs=[block_spec(n) for n in range(per_step)]
            + [
                pl.BlockSpec((TILE, TILE), lambda s, rows, mask: (1, 0)),
                pl.BlockSpec((2, TILE, TILE), lambda s, rows, mask: (0, 0, 0)),
            ],
            out_specs=pl.BlockSpec((per_step, TILE, 2 * TILE), lambda s, rows, mask: (s, 0, 0)),
            scratch_shapes=[pltpu.VMEM((4, TILE, TILE), jnp.bfloat16), pltpu.VMEM((TILE, TILE), jnp.bfloat16)],
        ),
        compiler_params=pltpu.CompilerParams(vmem_limit_bytes=VMEM_LIMIT),
        cost_estimate=pl.CostEstimate(
            flops=12 * count * TILE**3, bytes_accessed=4 * count * TILE * 2 * TILE, transcendentals=0
        ),
        name="factor",
    )(jnp.asarray(rows, jnp.int32), mask, *([front] * (per_step + 1)), inverse)


def gather_kernel(choices, sources, me, *refs):
    blocks, (out, sem) = refs[:sources], refs[sources:]

    def copy(part, option):
        source, index, offset = option
        block = blocks[source] if index is None else blocks[source].at[index, pl.ds(offset, HALF)]
        return pltpu.make_async_copy(block, out.at[pl.ds(part * HALF, HALF)], sem.at[part])

    for part, options in enumerate(choices):
        for g, option in enumerate(options):
            pl.when(me[0] == g)(lambda part=part, option=option: copy(part, option).start())
    for part, options in enumerate(choices):
        copy(part, options[0]).wait()


def gather(me, blocks, choices):
    parts = len(choices)
    return pl.pallas_call(
        functools.partial(gather_kernel, choices, len(blocks)),
        out_shape=jax.ShapeDtypeStruct((parts * HALF, 2 * TILE), jnp.bfloat16),
        in_specs=[pl.BlockSpec(memory_space=pltpu.SMEM)] + [pl.BlockSpec(memory_space=pl.ANY)] * len(blocks),
        out_specs=pl.BlockSpec(memory_space=pltpu.VMEM),
        scratch_shapes=[pltpu.SemaphoreType.DMA((parts,))],
        cost_estimate=pl.CostEstimate(flops=0, bytes_accessed=4 * parts * HALF * 2 * TILE, transcendentals=0),
        name="gather_own",
    )(me, *blocks)


def update_kernel(numbers, cols_dev, rows, mask, me, block, own, *refs):
    panels, out = refs[: 2 * len(numbers)], refs[-1]
    step = pl.program_id(0)

    def run(place, number):
        row = rows[number]
        panel = jnp.concatenate([panels[2 * place][...], panels[2 * place + 1][...]], axis=0)
        for c in range(cols_dev):
            span = slice(c * TILE, (c + 1) * TILE)
            update = dot(panel, own[:, span])
            keep = (mask[row, c] > 0) & (row > 0)
            old = block[:, span].astype(jnp.float32)
            out[:, span] = (old - jnp.where(keep, update, 0.0)).astype(jnp.bfloat16)

        @pl.when((me[0] == 0) & (row > 0))
        def _():
            out[:, :TILE] = panel[:, :TILE]

        @pl.when((me[0] == 0) & (row > 1))
        def _():
            out[:, TILE : 2 * TILE] = panel[:, TILE:]

    for place, number in enumerate(numbers):
        pl.when(step == place)(functools.partial(run, place, number))


def update(me, mask, front, own, rows, numbers, panels, base=None, fresh=False):
    width = front.shape[1]
    cols_dev = width // TILE
    count = len(numbers)
    start = numbers[0]

    def front_rows(s, rows, mask, me):
        return (rows[start + s], 0)

    if fresh:
        out_shape = jax.ShapeDtypeStruct((count * TILE, width), jnp.bfloat16)
        out_spec = pl.BlockSpec((TILE, width), lambda s, rows, mask, me: (s, 0))
    else:
        out_shape = jax.ShapeDtypeStruct(front.shape, jnp.bfloat16)
        out_spec = pl.BlockSpec((TILE, width), front_rows)
    in_specs = [
        pl.BlockSpec((TILE, width), front_rows),
        pl.BlockSpec((2 * TILE, width), lambda s, rows, mask, me: (0, 0)),
    ]
    in_specs += [pl.BlockSpec((HALF, 2 * TILE), lambda s, rows, mask, me: (0, 0))] * len(panels)
    operands = [front, own, *panels]
    aliases = {}
    if base is not None:
        in_specs.append(pl.BlockSpec(memory_space=pl.ANY))
        operands.append(base)
        aliases = {3 + len(operands) - 1: 0}
    return pl.pallas_call(
        functools.partial(update_kernel, numbers, cols_dev),
        out_shape=out_shape,
        grid_spec=pltpu.PrefetchScalarGridSpec(
            num_scalar_prefetch=3, grid=(count,), in_specs=in_specs, out_specs=out_spec
        ),
        input_output_aliases=aliases,
        compiler_params=pltpu.CompilerParams(vmem_limit_bytes=VMEM_LIMIT),
        cost_estimate=pl.CostEstimate(
            flops=2 * count * TILE * width * 2 * TILE, bytes_accessed=4 * count * TILE * width, transcendentals=0
        ),
        name="update",
    )(rows, mask, me, *operands)


def after(values, *others):
    return lax.optimization_barrier((tuple(values), others))[0]


def shards(front_in, panel_inverse, tile_mask, tile_map):
    front = front_in[0]
    width = front.shape[1]
    tiles = front.shape[0] // TILE
    cols_dev = width // TILE
    inverse = panel_inverse[0]
    mask = tile_mask[0]
    targets = tile_map[0, 0]
    contrib = targets.shape[0]
    rows_out = contrib // cols_dev
    n_grp = lax.axis_size("grp")
    n_front = lax.axis_size("front")
    n_dev = n_grp * n_front
    slots_dev = n_grp // 2
    g = lax.axis_index("grp")
    me = jnp.reshape(g, (1,)).astype(jnp.int32)
    root = g == 0

    labels = lax.all_to_all(
        jnp.broadcast_to(targets[None], (n_dev, contrib)), ("front", "grp"), split_axis=0, concat_axis=0, tiled=True
    )

    paths, place, lists = stream_plan(n_grp, tiles, cols_dev, rows_out)
    longest = max(len(lists[0]), len(lists[1]))
    rounds = longest + n_grp - 1
    order = [lists[s][t] for t in range(longest) for s in (0, 1) if t < len(lists[s])] + [0]
    cuts = [0, 2] + list(range(6, len(order), 4)) + [len(order)]
    made, where_made = [], {}

    def make(ready_at=None):
        begin, end = cuts[len(made)], cuts[len(made) + 1]
        for n, tile in enumerate(order[begin:end]):
            where_made[tile] = (len(made), n)
        blocks = inverse if ready_at is None else after((inverse,), *ready_at)[0]
        made.append(factor(front, blocks, mask, order[begin:end]))

    make()

    def made_half(tile, half):
        which, n = where_made[tile]
        return made[which][n, half * HALF : (half + 1) * HALF]

    cycles = [[(path[d], path[(d + 1) % n_grp]) for d in range(n_grp)] for path in paths]
    held = []
    turn = ()
    for t in range(rounds):
        held.append([])
        for half in (0, 1):
            if t == 0:
                values = tuple(made_half(lists[s][0], half) for s in (0, 1))
            else:
                values = tuple(lax.ppermute(held[t - 1][half][s], "grp", cycles[s]) for s in (0, 1))
                values = after(values, *turn)
                values = tuple(
                    jnp.where(root, made_half(lists[s][t], half), values[s]) if t < len(lists[s]) else values[s]
                    for s in (0, 1)
                )
            values = after(values)
            turn = values
            held[t].append(values)
        while len(made) < len(cuts) - 1 and len(made) <= t // 2 + 1:
            make(turn)

    table = []
    for n in range(n_grp):
        line = []
        for t in range(rounds):
            for s in (0, 1):
                index = t - place[s][n]
                line.append(lists[s][index] if 0 <= index < len(lists[s]) else 0)
        table.append(line + list(range(tiles - rows_out, tiles)))
    rows = lax.dynamic_index_in_dim(jnp.asarray(table, jnp.int32), g, 0, keepdims=False)

    while len(made) < len(cuts) - 1:
        make(turn)
    spot = {tile: (s, n) for s in (0, 1) for n, tile in enumerate(lists[s])}
    blocks, names, ready = list(made), {}, 0

    def choice(tile, half, n):
        nonlocal ready
        if n == 0:
            which, index = where_made[tile]
            return (which, index, half * HALF)
        s, number = spot[tile]
        slot = (number + place[s][n], half, s)
        ready = max(ready, slot[0])
        if slot not in names:
            names[slot] = len(blocks)
            blocks.append(held[slot[0]][half][s])
        return (names[slot], None, 0)

    choices = [
        [choice(n * cols_dev + c, half, n) for n in range(n_grp)] for c in range(cols_dev) for half in (0, 1)
    ]
    choices += [
        [choice(tiles - rows_out + r, half, n) for n in range(n_grp)] for r in range(rows_out) for half in (0, 1)
    ]
    gathered = gather(me, blocks, choices)
    own = gathered[:width].T
    ends = [gathered[width + n * HALF : width + (n + 1) * HALF] for n in range(2 * rows_out)]
    numbers = list(range(2 * rounds, 2 * rounds + rows_out))
    bottom = update(me, mask, front, own, rows, numbers, ends, fresh=True)

    piece = TILE // n_dev
    pieces = bottom.reshape(rows_out, n_dev, piece, cols_dev, TILE)
    pieces = jnp.transpose(pieces, (1, 3, 0, 2, 4)).reshape(n_dev, contrib, piece, TILE)
    arrived = lax.all_to_all(pieces, ("front", "grp"), split_axis=0, concat_axis=0, tiled=True)
    picker = labels.reshape(-1)[None, :] == jnp.arange(n_dev * slots_dev, dtype=jnp.int32)[:, None]
    sums = jnp.dot(
        picker.astype(jnp.bfloat16),
        arrived.reshape(n_dev * contrib, piece * TILE),
        preferred_element_type=jnp.float32,
    ).astype(jnp.bfloat16)
    sums = lax.all_to_all(
        sums.reshape(n_dev, slots_dev, piece, TILE), ("front", "grp"), split_axis=0, concat_axis=0, tiled=True
    )
    parent_tiles = jnp.transpose(sums, (1, 0, 2, 3)).reshape(slots_dev, TILE, TILE).astype(jnp.float32)

    result, done = None, 0
    for t in range(ready + 1, rounds):
        last = 2 * (t + 1)
        take = last - done if t == rounds - 1 else min(last - done, 8)
        numbers = list(range(done, done + take))
        done += take
        panels = [held[n // 2][half][n % 2] for n in numbers for half in (0, 1)]
        result = update(me, mask, front, own, rows, numbers, panels, base=result)
    return (result[None], parent_tiles)


def solution(mesh):
    in_specs = (
        P("front", None, "grp"),
        P("front", None, None, None),
        P("front", None, "grp"),
        P("front", "grp", None),
    )
    out_specs = (P("front", None, "grp"), P(("front", "grp"), None, None))
    return jax.shard_map(shards, mesh=mesh, in_specs=in_specs, out_specs=out_specs, check_vma=False)
```

```python
import functools

import jax
import jax.numpy as jnp
from jax import lax
from jax.experimental import pallas as pl
from jax.experimental.pallas import tpu as pltpu
from jax.sharding import PartitionSpec as P

TILE = 256
CHAINS = 2
VMEM_LIMIT = 24 * 1024 * 1024
ANY = pl.BlockSpec(memory_space=pl.ANY)
VMEM = pl.BlockSpec(memory_space=pltpu.VMEM)
SMEM = pl.BlockSpec(memory_space=pltpu.SMEM)


def ring_order(n_grp):
    depth = 4 if n_grp % 4 == 0 and n_grp >= 8 else 1
    width = n_grp // depth
    if depth == 1:
        return list(range(n_grp))
    order = [z * width for z in range(depth)]
    for number, z in enumerate(reversed(range(depth))):
        ys = range(1, width) if number % 2 == 0 else range(width - 1, 0, -1)
        order += [z * width + y for y in ys]
    return order


def routes(n_grp):
    if n_grp == 8:
        climb = [(g, (g + 2) % n_grp) for g in range(n_grp)]
        cross = [(g, g ^ 1) for g in range(n_grp)]
        rules = [[0] * n_grp, [0] * n_grp]
        rules[0][1] = rules[0][n_grp - 1] = rules[1][1] = 1
        return [climb, cross], rules
    cycle = ring_order(n_grp)
    ring = [(g, cycle[(d + 1) % n_grp]) for d, g in enumerate(cycle)]
    return [ring, [(b, a) for a, b in ring]], [[0] * n_grp, [1] * n_grp]


def travel(perms, rules, lists, n_grp, tiles):
    got = []
    missing = {(g, tile) for g in range(n_grp) for tile in range(1, tiles)}
    while missing:
        e = len(got)
        now = []
        for s in (0, 1):
            arrival = [0] * n_grp
            for g, target in perms[s]:
                if g == 0 and e < len(lists[s]):
                    arrival[target] = lists[s][e]
                elif e >= CHAINS:
                    arrival[target] = got[e - CHAINS][rules[s][g]][g]
            now.append(arrival)
            missing -= set(enumerate(arrival))
        got.append(now)
    return got


def delays(perms, rules, n_grp):
    result = [[None] * n_grp, [None] * n_grp]
    for s in (0, 1):
        lists = [[], []]
        lists[s] = [1]
        for e, now in enumerate(travel(perms, rules, lists, n_grp, 2)):
            for arrival in now:
                for g in range(n_grp):
                    if arrival[g] and result[s][g] is None:
                        result[s][g] = e
    return result


def stream_plan(perms, rules, n_grp, tiles, cols_dev, rows_out):
    hops = delays(perms, rules, n_grp)
    lists = [[], []]
    bottom = [tiles - 1 - r for r in range(rows_out)]
    rest = []
    for g in range(n_grp):
        for c in range(cols_dev):
            tile = g * cols_dev + c
            if tile and tile not in bottom:
                rest.append((g, tile))
    for number, tile in enumerate(bottom):
        lists[number % 2].append(tile)

    def lateness(g):
        return -1 if g == 0 else min(hops[0][g], hops[1][g])

    rest.sort(key=lambda item: (-lateness(item[0]), item[1]))
    for g, tile in rest:
        if hops[0][g] == hops[1][g] or g == 0:
            which = 0 if len(lists[0]) <= len(lists[1]) else 1
        else:
            which = 0 if hops[0][g] < hops[1][g] else 1
        lists[which].append(tile)
    return lists


def split2(x):
    hi = x.astype(jnp.bfloat16)
    return hi, (x - hi.astype(jnp.float32)).astype(jnp.bfloat16)


def dot(a, b):
    return jnp.dot(a, b, preferred_element_type=jnp.float32)


def factor_kernel(tiles, head, mask, front, *refs):
    if head:
        inverse, out, parts, one, blocks, sems, top, top_sem = refs
    else:
        parts, one, out, blocks, sems = refs
    copies = [
        pltpu.make_async_copy(
            front.at[pl.ds(tile * TILE, TILE), pl.ds(0, 2 * TILE)], blocks.at[n], sems.at[n]
        )
        for n, tile in enumerate(tiles)
    ]
    if head:
        top_copy = pltpu.make_async_copy(front.at[pl.ds(TILE, TILE), pl.ds(0, TILE)], top, top_sem)
        top_copy.start()
    for copy in copies:
        copy.start()

    def first_of(x):
        return (dot(x, parts[1]) + dot(x, parts[0])).astype(jnp.bfloat16)

    if head:
        for which in range(2):
            hi, low = split2(inverse[which].T)
            parts[2 * which] = hi
            parts[2 * which + 1] = low
        top_copy.wait()
        one[...] = first_of(top[...]).astype(jnp.float32).T.astype(jnp.bfloat16)
    for begin in range(0, len(tiles), 2):
        group = list(range(begin, min(begin + 2, len(tiles))))
        for n in group:
            copies[n].wait()
        firsts = first_of(jnp.concatenate([blocks[n, :, :TILE] for n in group], axis=0))
        updates = dot(firsts, one[...])
        works = []
        for place, n in enumerate(group):
            keep = mask[tiles[n] : tiles[n] + 1, 1:2] > 0
            update = updates[place * TILE : (place + 1) * TILE]
            works.append(blocks[n, :, TILE:].astype(jnp.float32) - jnp.where(keep, update, 0.0))
        high, low = split2(jnp.concatenate(works, axis=0))
        seconds = (dot(low, parts[2]) + dot(high, parts[3]) + dot(high, parts[2])).astype(jnp.bfloat16)
        for place, n in enumerate(group):
            span = slice(place * TILE, (place + 1) * TILE)
            empty = jnp.zeros((TILE, TILE), jnp.bfloat16)
            out[n, :, :TILE] = firsts[span] if tiles[n] > 0 else empty
            out[n, :, TILE:] = seconds[span] if tiles[n] > 1 else empty


def factor(front, mask, tiles, inverse=None, parts=None):
    head = parts is None
    count = len(tiles)
    out_shape = [jax.ShapeDtypeStruct((count, TILE, 2 * TILE), jnp.bfloat16)]
    scratch = [pltpu.VMEM((count, TILE, 2 * TILE), jnp.bfloat16), pltpu.SemaphoreType.DMA((count,))]
    if head:
        out_shape += [
            jax.ShapeDtypeStruct((4, TILE, TILE), jnp.bfloat16),
            jax.ShapeDtypeStruct((TILE, TILE), jnp.bfloat16),
        ]
        scratch += [pltpu.VMEM((TILE, TILE), jnp.bfloat16), pltpu.SemaphoreType.DMA(())]
    operands = (inverse,) if head else parts
    return pl.pallas_call(
        functools.partial(factor_kernel, tuple(tiles), head),
        out_shape=out_shape,
        in_specs=[VMEM, ANY] + [VMEM] * len(operands),
        out_specs=[VMEM] * len(out_shape),
        scratch_shapes=scratch,
        compiler_params=pltpu.CompilerParams(vmem_limit_bytes=VMEM_LIMIT),
        cost_estimate=pl.CostEstimate(
            flops=12 * count * TILE**3, bytes_accessed=4 * count * TILE * 2 * TILE, transcendentals=0
        ),
        name="factor",
    )(mask, front, *operands)


def subtract(row, mask, me, panel, own, old, new, cols_dev):
    for c in range(cols_dev):
        span = slice(c * TILE, (c + 1) * TILE)
        update = dot(panel[...], own[:, span])
        keep = mask[row, c] > 0
        new[:, span] = (old[:, span].astype(jnp.float32) - jnp.where(keep, update, 0.0)).astype(jnp.bfloat16)

    @pl.when(me[0] == 0)
    def _():
        new[:, :TILE] = panel[:, :TILE]

    @pl.when((me[0] == 0) & (row > 1))
    def _():
        new[:, TILE : 2 * TILE] = panel[:, TILE:]


def own_kernel(choices, sources, cols_dev, rows_out, mask, me, front, *refs):
    blocks, (own, bottom, panels, old, sems, old_sem) = refs[:sources], refs[sources:]
    tiles = front.shape[0] // TILE

    def copy(part, option):
        source, index = option
        block = blocks[source] if index is None else blocks[source].at[index]
        return pltpu.make_async_copy(block, panels.at[part], sems.at[part])

    old_copy = pltpu.make_async_copy(front.at[pl.ds((tiles - rows_out) * TILE, rows_out * TILE)], old, old_sem)
    old_copy.start()
    for part, options in enumerate(choices):
        for g, option in enumerate(options):
            pl.when(me[0] == g)(lambda part=part, option=option: copy(part, option).start())
    for part, options in enumerate(choices):
        copy(part, options[0]).wait()
    for c in range(cols_dev):
        own[:, c * TILE : (c + 1) * TILE] = panels[c].astype(jnp.float32).T.astype(jnp.bfloat16)
    old_copy.wait()
    for r in range(rows_out):
        span = pl.ds(r * TILE, TILE)
        subtract(tiles - rows_out + r, mask, me, panels.at[cols_dev + r], own, old.at[span], bottom.at[span], cols_dev)


def own_panels(mask, me, front, blocks, choices, rows_out):
    width = front.shape[1]
    parts = len(choices)
    return pl.pallas_call(
        functools.partial(own_kernel, choices, len(blocks), width // TILE, rows_out),
        out_shape=[
            jax.ShapeDtypeStruct((2 * TILE, width), jnp.bfloat16),
            jax.ShapeDtypeStruct((rows_out * TILE, width), jnp.bfloat16),
        ],
        in_specs=[SMEM, SMEM, ANY] + [ANY] * len(blocks),
        out_specs=[VMEM, VMEM],
        scratch_shapes=[
            pltpu.VMEM((parts, TILE, 2 * TILE), jnp.bfloat16),
            pltpu.VMEM((rows_out * TILE, width), jnp.bfloat16),
            pltpu.SemaphoreType.DMA((parts,)),
            pltpu.SemaphoreType.DMA(()),
        ],
        compiler_params=pltpu.CompilerParams(vmem_limit_bytes=VMEM_LIMIT),
        cost_estimate=pl.CostEstimate(
            flops=2 * rows_out * TILE * width * 2 * TILE,
            bytes_accessed=4 * parts * TILE * 2 * TILE,
            transcendentals=0,
        ),
        name="own_panels",
    )(mask, me, front, *blocks)


def update_kernel(numbers, cols_dev, start, rows, mask, me, own, front, *refs):
    count = len(numbers)
    panels = refs[:count]
    out, old, new, in_sems, out_sems = refs[-5:]

    def span(n):
        return pl.ds(pl.multiple_of(rows[numbers[n]] * TILE, TILE), TILE)

    def fetch(n):
        return pltpu.make_async_copy(front.at[span(n)], old.at[n], in_sems.at[n])

    def store(n):
        return pltpu.make_async_copy(new.at[n], out.at[span(n)], out_sems.at[n])

    def each(act):
        for n in range(count):
            pl.when(rows[numbers[n]] > 0)(functools.partial(act, n))

    def work(n):
        fetch(n).wait()
        subtract(rows[numbers[n]], mask, me, panels[n], own, old.at[n], new.at[n], cols_dev)
        store(n).start()

    if start:
        here = pl.ds(0, TILE)
        top_in = pltpu.make_async_copy(front.at[here], new.at[count], in_sems.at[count])
        top_out = pltpu.make_async_copy(new.at[count], out.at[here], out_sems.at[count])
        top_in.start()
    each(lambda n: fetch(n).start())
    if start:
        top_in.wait()
        top_out.start()
    each(work)
    each(lambda n: store(n).wait())
    if start:
        top_out.wait()


def update(rows, mask, me, own, front, numbers, panels, base=None):
    width = front.shape[1]
    count = len(numbers)
    room = count + (base is None)
    operands = [rows, mask, me, own, front, *panels]
    in_specs = [SMEM, SMEM, SMEM, VMEM, ANY] + [VMEM] * count
    aliases = {}
    if base is not None:
        aliases = {len(operands): 0}
        operands.append(base)
        in_specs.append(ANY)
    return pl.pallas_call(
        functools.partial(update_kernel, tuple(numbers), width // TILE, base is None),
        out_shape=jax.ShapeDtypeStruct(front.shape, jnp.bfloat16),
        in_specs=in_specs,
        out_specs=ANY,
        scratch_shapes=[
            pltpu.VMEM((count, TILE, width), jnp.bfloat16),
            pltpu.VMEM((room, TILE, width), jnp.bfloat16),
            pltpu.SemaphoreType.DMA((room,)),
            pltpu.SemaphoreType.DMA((room,)),
        ],
        input_output_aliases=aliases,
        compiler_params=pltpu.CompilerParams(vmem_limit_bytes=VMEM_LIMIT),
        cost_estimate=pl.CostEstimate(
            flops=2 * count * TILE * width * 2 * TILE, bytes_accessed=4 * count * TILE * width, transcendentals=0
        ),
        name="update",
    )(*operands)


def after(values, *others):
    return lax.optimization_barrier((tuple(values), others))[0]


def one_of(g, members):
    result = g == members[0]
    for member in members[1:]:
        result = result | (g == member)
    return result


def shards(front_in, panel_inverse, tile_mask, tile_map):
    front = front_in[0]
    width = front.shape[1]
    tiles = front.shape[0] // TILE
    cols_dev = width // TILE
    inverse = panel_inverse[0]
    mask = tile_mask[0]
    targets = tile_map[0, 0]
    contrib = targets.shape[0]
    rows_out = contrib // cols_dev
    n_grp = lax.axis_size("grp")
    n_dev = n_grp * lax.axis_size("front")
    slots_dev = n_grp // 2
    g = lax.axis_index("grp")
    me = jnp.reshape(g, (1,)).astype(jnp.int32)
    root = g == 0

    perms, rules = routes(n_grp)
    lists = stream_plan(perms, rules, n_grp, tiles, cols_dev, rows_out)
    got = travel(perms, rules, lists, n_grp, tiles)
    events = len(got)
    longest = max(len(lists[0]), len(lists[1]))

    order = [(e, lists[s][e]) for e in range(longest) for s in (0, 1) if e < len(lists[s])] + [(longest, 0)]
    cuts = [0, 2, 6] + list(range(14, len(order) - 2, 8)) + [len(order)]
    made, parts, where_made = [], None, {}

    def make(e, turn):
        nonlocal parts
        while len(made) < len(cuts) - 1:
            begin, end = cuts[len(made)], cuts[len(made) + 1]
            if order[begin][0] > max(e + 1, e + 2 if begin > 2 else 0):
                break
            names = [tile for _, tile in order[begin:end]]
            for n, tile in enumerate(names):
                where_made[tile] = (len(made), n)
            if parts is None:
                block, *parts = factor(front, mask, names, inverse=inverse)
            else:
                (block,) = factor(front, mask, names, parts=after(parts, *turn))
            made.append(block)

    make(-2, ())
    held, turns, turn = [], [], ()
    for e in range(events):
        values = []
        for s in (0, 1):
            value = None
            if e >= CHAINS:
                others = [n for n in range(n_grp) if rules[s][n] != rules[s][0]]
                value = held[e - CHAINS][rules[s][0]]
                if others:
                    value = jnp.where(one_of(g, others), held[e - CHAINS][1 - rules[s][0]], value)
            if e < len(lists[s]):
                which, n = where_made[lists[s][e]]
                value = made[which][n] if value is None else jnp.where(root, made[which][n], value)
            values.append(value)
        turn = after(values, *turn, *([labels] if e == 4 else []))
        turns.append(turn)
        held.append([lax.ppermute(turn[s], "grp", perms[s]) for s in (0, 1)])
        make(e, turn)
        if e + 1 < events and e + 1 >= CHAINS:
            held[e + 1 - CHAINS] = list(after(held[e + 1 - CHAINS], *turn))
        if e == 1:
            labels = lax.all_to_all(
                after((jnp.broadcast_to(targets[None], (n_dev, contrib)),), *turn)[0],
                ("front", "grp"),
                split_axis=0,
                concat_axis=0,
                tiled=True,
            )

    table = []
    for n in range(n_grp):
        line = []
        for now in got:
            for arrival in now:
                line.append(arrival[n] if arrival[n] not in line else 0)
        table.append(line)
    rows = lax.dynamic_index_in_dim(jnp.asarray(table, jnp.int32), g, 0, keepdims=False)

    blocks, names, ready = list(made), {}, 0

    def choice(tile, n):
        nonlocal ready
        if n == 0:
            return where_made[tile]
        number = table[n].index(tile)
        ready = max(ready, number // 2)
        if number not in names:
            names[number] = len(blocks)
            blocks.append(held[number // 2][number % 2])
        return (names[number], None)

    choices = [[choice(n * cols_dev + c, n) for n in range(n_grp)] for c in range(cols_dev)]
    choices += [[choice(tiles - rows_out + r, n) for n in range(n_grp)] for r in range(rows_out)]
    own, bottom = own_panels(mask, me, front, blocks, choices, rows_out)

    piece = TILE // n_dev
    pieces = jnp.transpose(bottom.reshape(rows_out, n_dev, piece, width), (1, 0, 2, 3))
    arrived = lax.all_to_all(pieces, ("front", "grp"), split_axis=0, concat_axis=0, tiled=True)
    arrived = arrived.reshape(n_dev, rows_out, piece, cols_dev, TILE)
    arrived = jnp.transpose(arrived, (0, 3, 1, 2, 4)) if rows_out == 1 else jnp.transpose(arrived, (0, 1, 3, 2, 4))
    picker = labels.reshape(-1)[None, :] == jnp.arange(n_dev * slots_dev, dtype=jnp.int32)[:, None]
    sums = dot(picker.astype(jnp.bfloat16), arrived.reshape(n_dev * contrib, piece * TILE)).astype(jnp.bfloat16)
    sums = lax.all_to_all(
        sums.reshape(n_dev, slots_dev, piece, TILE), ("front", "grp"), split_axis=0, concat_axis=0, tiled=True
    )
    parent_tiles = jnp.transpose(sums, (1, 0, 2, 3)).reshape(slots_dev, TILE, TILE).astype(jnp.float32)

    result, done = None, 0
    for e in range(ready + CHAINS + 1, events + CHAINS):
        take = min(2 * (e - CHAINS + 1) - done, 8)
        if take < 4 and e < events + CHAINS - 1:
            continue
        numbers = list(range(done, done + take))
        done += take
        here = after((rows,), *turns[e])[0] if e < events else rows
        panels = [held[n // 2][n % 2] for n in numbers]
        result = update(here, mask, me, own, front, numbers, panels, base=result)
    while done < 2 * events:
        numbers = list(range(done, min(done + 8, 2 * events)))
        done += len(numbers)
        result = update(rows, mask, me, own, front, numbers, [held[n // 2][n % 2] for n in numbers], base=result)
    return (result[None], parent_tiles)


def solution(mesh):
    in_specs = (
        P("front", None, "grp"),
        P("front", None, None, None),
        P("front", None, "grp"),
        P("front", "grp", None),
    )
    out_specs = (P("front", None, "grp"), P(("front", "grp"), None, None))
    return jax.shard_map(shards, mesh=mesh, in_specs=in_specs, out_specs=out_specs, check_vma=False)
```

```python
import functools

import jax
import jax.numpy as jnp
from jax import lax
from jax.experimental import pallas as pl
from jax.experimental.pallas import tpu as pltpu
from jax.sharding import PartitionSpec as P

TILE = 256
CHAINS = 2
VMEM_LIMIT = 16 * 1024 * 1024
HBM = pl.BlockSpec(memory_space=pltpu.HBM)
VMEM = pl.BlockSpec(memory_space=pltpu.VMEM)
SMEM = pl.BlockSpec(memory_space=pltpu.SMEM)


def ring_order(n_grp):
    depth = 4 if n_grp % 4 == 0 and n_grp >= 8 else 1
    width = n_grp // depth
    if depth == 1:
        return list(range(n_grp))
    order = [z * width for z in range(depth)]
    for number, z in enumerate(reversed(range(depth))):
        ys = range(1, width) if number % 2 == 0 else range(width - 1, 0, -1)
        order += [z * width + y for y in ys]
    return order


def routes(n_grp):
    if n_grp == 8:
        climb = [(g, (g + 2) % n_grp) for g in range(n_grp)]
        cross = [(g, g ^ 1) for g in range(n_grp)]
        rules = [[0] * n_grp, [0] * n_grp]
        rules[0][1] = rules[0][n_grp - 1] = rules[1][1] = 1
        return [climb, cross], rules
    cycle = ring_order(n_grp)
    ring = [(g, cycle[(d + 1) % n_grp]) for d, g in enumerate(cycle)]
    return [ring, [(b, a) for a, b in ring]], [[0] * n_grp, [1] * n_grp]


def travel(perms, rules, lists, n_grp, tiles):
    got = []
    missing = {(g, tile) for g in range(n_grp) for tile in range(1, tiles)}
    while missing:
        e = len(got)
        now = []
        for s in (0, 1):
            arrival = [0] * n_grp
            for g, target in perms[s]:
                if g == 0 and e < len(lists[s]):
                    arrival[target] = lists[s][e]
                elif e >= CHAINS:
                    arrival[target] = got[e - CHAINS][rules[s][g]][g]
            now.append(arrival)
            missing -= set(enumerate(arrival))
        got.append(now)
    return got


def delays(perms, rules, n_grp):
    result = [[None] * n_grp, [None] * n_grp]
    for s in (0, 1):
        lists = [[], []]
        lists[s] = [1]
        for e, now in enumerate(travel(perms, rules, lists, n_grp, 2)):
            for arrival in now:
                for g in range(n_grp):
                    if arrival[g] and result[s][g] is None:
                        result[s][g] = e
    return result


def stream_plan(perms, rules, n_grp, tiles, cols_dev, rows_out):
    hops = delays(perms, rules, n_grp)
    lists = [[], []]
    bottom = [tiles - 1 - r for r in range(rows_out)]
    rest = []
    for g in range(n_grp):
        for c in range(cols_dev):
            tile = g * cols_dev + c
            if tile and tile not in bottom:
                rest.append((g, tile))
    for number, tile in enumerate(bottom):
        lists[number % 2].append(tile)

    def lateness(g):
        return -1 if g == 0 else min(hops[0][g], hops[1][g])

    rest.sort(key=lambda item: (-lateness(item[0]), item[1]))
    for g, tile in rest:
        if hops[0][g] == hops[1][g] or g == 0:
            which = 0 if len(lists[0]) <= len(lists[1]) else 1
        else:
            which = 0 if hops[0][g] < hops[1][g] else 1
        lists[which].append(tile)
    return lists


def in_hbm(x):
    return pltpu.with_memory_space_constraint(x, pltpu.HBM)


def split2(x):
    hi = x.astype(jnp.bfloat16)
    return hi, (x - hi.astype(jnp.float32)).astype(jnp.bfloat16)


def dot(a, b):
    return jnp.dot(a, b, preferred_element_type=jnp.float32)


def factor_kernel(tiles, head, mask, front, *refs):
    if head:
        inverse, out, parts, one, blocks, sems, top, top_sem = refs
    else:
        parts, one, out, blocks, sems = refs
    copies = [
        pltpu.make_async_copy(
            front.at[pl.ds(tile * TILE, TILE), pl.ds(0, 2 * TILE)], blocks.at[n], sems.at[n]
        )
        for n, tile in enumerate(tiles)
    ]
    if head:
        top_copy = pltpu.make_async_copy(front.at[pl.ds(TILE, TILE), pl.ds(0, TILE)], top, top_sem)
        top_copy.start()
    for copy in copies:
        copy.start()

    def first_of(x):
        return (dot(x, parts[1]) + dot(x, parts[0])).astype(jnp.bfloat16)

    if head:
        for which in range(2):
            hi, low = split2(inverse[which].T)
            parts[2 * which] = hi
            parts[2 * which + 1] = low
        top_copy.wait()
        one[...] = first_of(top[...]).astype(jnp.float32).T.astype(jnp.bfloat16)
    for begin in range(0, len(tiles), 2):
        group = list(range(begin, min(begin + 2, len(tiles))))
        for n in group:
            copies[n].wait()
        firsts = first_of(jnp.concatenate([blocks[n, :, :TILE] for n in group], axis=0))
        updates = dot(firsts, one[...])
        works = []
        for place, n in enumerate(group):
            keep = mask[tiles[n] : tiles[n] + 1, 1:2] > 0
            update = updates[place * TILE : (place + 1) * TILE]
            works.append(blocks[n, :, TILE:].astype(jnp.float32) - jnp.where(keep, update, 0.0))
        high, low = split2(jnp.concatenate(works, axis=0))
        seconds = (dot(low, parts[2]) + dot(high, parts[3]) + dot(high, parts[2])).astype(jnp.bfloat16)
        for place, n in enumerate(group):
            span = slice(place * TILE, (place + 1) * TILE)
            empty = jnp.zeros((TILE, TILE), jnp.bfloat16)
            out[n, :, :TILE] = firsts[span] if tiles[n] > 0 else empty
            out[n, :, TILE:] = seconds[span] if tiles[n] > 1 else empty


def factor(front, mask, tiles, inverse=None, parts=None):
    head = parts is None
    count = len(tiles)
    out_shape = [jax.ShapeDtypeStruct((count, TILE, 2 * TILE), jnp.bfloat16)]
    scratch = [pltpu.VMEM((count, TILE, 2 * TILE), jnp.bfloat16), pltpu.SemaphoreType.DMA((count,))]
    if head:
        out_shape += [
            jax.ShapeDtypeStruct((4, TILE, TILE), jnp.bfloat16),
            jax.ShapeDtypeStruct((TILE, TILE), jnp.bfloat16),
        ]
        scratch += [pltpu.VMEM((TILE, TILE), jnp.bfloat16), pltpu.SemaphoreType.DMA(())]
    operands = (inverse,) if head else parts
    return pl.pallas_call(
        functools.partial(factor_kernel, tuple(tiles), head),
        out_shape=out_shape,
        in_specs=[VMEM, HBM] + [VMEM] * len(operands),
        out_specs=[VMEM] * len(out_shape),
        scratch_shapes=scratch,
        compiler_params=pltpu.CompilerParams(vmem_limit_bytes=VMEM_LIMIT),
        cost_estimate=pl.CostEstimate(
            flops=12 * count * TILE**3, bytes_accessed=4 * count * TILE * 2 * TILE, transcendentals=0
        ),
        name="factor",
    )(mask, in_hbm(front), *operands)


def subtract(row, mask, me, panel, own, old, new, cols_dev):
    for c in range(cols_dev):
        span = slice(c * TILE, (c + 1) * TILE)
        update = dot(panel[...], own[:, span])
        keep = mask[row, c] > 0
        new[:, span] = (old[:, span].astype(jnp.float32) - jnp.where(keep, update, 0.0)).astype(jnp.bfloat16)

    @pl.when(me[0] == 0)
    def _():
        new[:, :TILE] = panel[:, :TILE]

    @pl.when((me[0] == 0) & (row > 1))
    def _():
        new[:, TILE : 2 * TILE] = panel[:, TILE:]


def own_kernel(choices, sources, cols_dev, rows_out, mask, me, front, *refs):
    blocks, (own, bottom, panels, old, sems, old_sem) = refs[:sources], refs[sources:]
    tiles = front.shape[0] // TILE

    def copy(part, option):
        source, index = option
        block = blocks[source] if index is None else blocks[source].at[index]
        return pltpu.make_async_copy(block, panels.at[part], sems.at[part])

    old_copy = pltpu.make_async_copy(front.at[pl.ds((tiles - rows_out) * TILE, rows_out * TILE)], old, old_sem)
    old_copy.start()
    for part, options in enumerate(choices):
        for g, option in enumerate(options):
            pl.when(me[0] == g)(lambda part=part, option=option: copy(part, option).start())
    for part, options in enumerate(choices):
        copy(part, options[0]).wait()
    for c in range(cols_dev):
        own[:, c * TILE : (c + 1) * TILE] = panels[c].astype(jnp.float32).T.astype(jnp.bfloat16)
    old_copy.wait()
    for r in range(rows_out):
        span = pl.ds(r * TILE, TILE)
        subtract(tiles - rows_out + r, mask, me, panels.at[cols_dev + r], own, old.at[span], bottom.at[span], cols_dev)


def own_panels(mask, me, front, blocks, choices, rows_out):
    width = front.shape[1]
    parts = len(choices)
    return pl.pallas_call(
        functools.partial(own_kernel, choices, len(blocks), width // TILE, rows_out),
        out_shape=[
            jax.ShapeDtypeStruct((2 * TILE, width), jnp.bfloat16),
            jax.ShapeDtypeStruct((rows_out * TILE, width), jnp.bfloat16),
        ],
        in_specs=[SMEM, SMEM, HBM] + [VMEM] * len(blocks),
        out_specs=[VMEM, VMEM],
        scratch_shapes=[
            pltpu.VMEM((parts, TILE, 2 * TILE), jnp.bfloat16),
            pltpu.VMEM((rows_out * TILE, width), jnp.bfloat16),
            pltpu.SemaphoreType.DMA((parts,)),
            pltpu.SemaphoreType.DMA(()),
        ],
        compiler_params=pltpu.CompilerParams(vmem_limit_bytes=VMEM_LIMIT),
        cost_estimate=pl.CostEstimate(
            flops=2 * rows_out * TILE * width * 2 * TILE,
            bytes_accessed=4 * parts * TILE * 2 * TILE,
            transcendentals=0,
        ),
        name="own_panels",
    )(mask, me, in_hbm(front), *blocks)


def update_kernel(numbers, cols_dev, start, rows, mask, me, own, front, *refs):
    count = len(numbers)
    panels = refs[:count]
    out, old, new, in_sems, out_sems = refs[-5:]

    def span(n):
        return pl.ds(pl.multiple_of(rows[numbers[n]] * TILE, TILE), TILE)

    def fetch(n):
        return pltpu.make_async_copy(front.at[span(n)], old.at[n], in_sems.at[n])

    def store(n):
        return pltpu.make_async_copy(new.at[n], out.at[span(n)], out_sems.at[n])

    def each(act):
        for n in range(count):
            pl.when(rows[numbers[n]] > 0)(functools.partial(act, n))

    def work(n):
        fetch(n).wait()
        subtract(rows[numbers[n]], mask, me, panels[n], own, old.at[n], new.at[n], cols_dev)
        store(n).start()

    if start:
        here = pl.ds(0, TILE)
        top_in = pltpu.make_async_copy(front.at[here], new.at[count], in_sems.at[count])
        top_out = pltpu.make_async_copy(new.at[count], out.at[here], out_sems.at[count])
        top_in.start()
    each(lambda n: fetch(n).start())
    if start:
        top_in.wait()
        top_out.start()
    each(work)
    each(lambda n: store(n).wait())
    if start:
        top_out.wait()


def update(rows, mask, me, own, front, numbers, panels, base=None):
    width = front.shape[1]
    count = len(numbers)
    room = count + (base is None)
    operands = [rows, mask, me, own, in_hbm(front), *panels]
    in_specs = [SMEM, SMEM, SMEM, VMEM, HBM] + [VMEM] * count
    aliases = {}
    if base is not None:
        aliases = {len(operands): 0}
        operands.append(in_hbm(base))
        in_specs.append(HBM)
    return pl.pallas_call(
        functools.partial(update_kernel, tuple(numbers), width // TILE, base is None),
        out_shape=jax.ShapeDtypeStruct(front.shape, jnp.bfloat16),
        in_specs=in_specs,
        out_specs=HBM,
        scratch_shapes=[
            pltpu.VMEM((count, TILE, width), jnp.bfloat16),
            pltpu.VMEM((room, TILE, width), jnp.bfloat16),
            pltpu.SemaphoreType.DMA((room,)),
            pltpu.SemaphoreType.DMA((room,)),
        ],
        input_output_aliases=aliases,
        compiler_params=pltpu.CompilerParams(vmem_limit_bytes=VMEM_LIMIT),
        cost_estimate=pl.CostEstimate(
            flops=2 * count * TILE * width * 2 * TILE, bytes_accessed=4 * count * TILE * width, transcendentals=0
        ),
        name="update",
    )(*operands)


def after(values, *others):
    return lax.optimization_barrier((tuple(values), others))[0]


def one_of(g, members):
    result = g == members[0]
    for member in members[1:]:
        result = result | (g == member)
    return result


def shards(front_in, panel_inverse, tile_mask, tile_map):
    front = front_in[0]
    width = front.shape[1]
    tiles = front.shape[0] // TILE
    cols_dev = width // TILE
    inverse = panel_inverse[0]
    mask = tile_mask[0]
    targets = tile_map[0, 0]
    contrib = targets.shape[0]
    rows_out = contrib // cols_dev
    n_grp = lax.axis_size("grp")
    n_dev = n_grp * lax.axis_size("front")
    slots_dev = n_grp // 2
    g = lax.axis_index("grp")
    me = jnp.reshape(g, (1,)).astype(jnp.int32)
    root = g == 0

    perms, rules = routes(n_grp)
    lists = stream_plan(perms, rules, n_grp, tiles, cols_dev, rows_out)
    got = travel(perms, rules, lists, n_grp, tiles)
    events = len(got)
    longest = max(len(lists[0]), len(lists[1]))

    order = [(e, lists[s][e]) for e in range(longest) for s in (0, 1) if e < len(lists[s])] + [(longest, 0)]
    cuts = [0, 2, 6] + list(range(14, len(order) - 2, 8)) + [len(order)]
    made, parts, where_made = [], None, {}

    def make(e, turn):
        nonlocal parts
        while len(made) < len(cuts) - 1:
            begin, end = cuts[len(made)], cuts[len(made) + 1]
            if order[begin][0] > max(e + 1, e + 2 if begin > 2 else 0):
                break
            names = [tile for _, tile in order[begin:end]]
            for n, tile in enumerate(names):
                where_made[tile] = (len(made), n)
            if parts is None:
                block, *parts = factor(front, mask, names, inverse=inverse)
            else:
                (block,) = factor(front, mask, names, parts=after(parts, *turn))
            made.append(block)

    make(-2, ())
    held, turns, turn = [], [], ()
    for e in range(events):
        values = []
        for s in (0, 1):
            value = None
            if e >= CHAINS:
                others = [n for n in range(n_grp) if rules[s][n] != rules[s][0]]
                value = held[e - CHAINS][rules[s][0]]
                if others:
                    value = jnp.where(one_of(g, others), held[e - CHAINS][1 - rules[s][0]], value)
            if e < len(lists[s]):
                which, n = where_made[lists[s][e]]
                value = made[which][n] if value is None else jnp.where(root, made[which][n], value)
            values.append(value)
        turn = after(values, *turn, *([labels] if e == 4 else []))
        turns.append(turn)
        held.append([lax.ppermute(turn[s], "grp", perms[s]) for s in (0, 1)])
        make(e, turn)
        if e + 1 < events and e + 1 >= CHAINS:
            held[e + 1 - CHAINS] = list(after(held[e + 1 - CHAINS], *turn))
        if e == 1:
            labels = lax.all_to_all(
                after((jnp.broadcast_to(targets[None], (n_dev, contrib)),), *turn)[0],
                ("front", "grp"),
                split_axis=0,
                concat_axis=0,
                tiled=True,
            )

    table = []
    for n in range(n_grp):
        line = []
        for now in got:
            for arrival in now:
                line.append(arrival[n] if arrival[n] not in line else 0)
        table.append(line)
    rows = lax.dynamic_index_in_dim(jnp.asarray(table, jnp.int32), g, 0, keepdims=False)

    blocks, names, ready = list(made), {}, 0

    def choice(tile, n):
        nonlocal ready
        if n == 0:
            return where_made[tile]
        number = table[n].index(tile)
        ready = max(ready, number // 2)
        if number not in names:
            names[number] = len(blocks)
            blocks.append(held[number // 2][number % 2])
        return (names[number], None)

    choices = [[choice(n * cols_dev + c, n) for n in range(n_grp)] for c in range(cols_dev)]
    choices += [[choice(tiles - rows_out + r, n) for n in range(n_grp)] for r in range(rows_out)]
    own, bottom = own_panels(mask, me, front, blocks, choices, rows_out)

    piece = TILE // n_dev
    pieces = jnp.transpose(bottom.reshape(rows_out, n_dev, piece, width), (1, 0, 2, 3))
    arrived = lax.all_to_all(pieces, ("front", "grp"), split_axis=0, concat_axis=0, tiled=True)
    arrived = arrived.reshape(n_dev, rows_out, piece, cols_dev, TILE)
    arrived = jnp.transpose(arrived, (0, 3, 1, 2, 4)) if rows_out == 1 else jnp.transpose(arrived, (0, 1, 3, 2, 4))
    picker = labels.reshape(-1)[None, :] == jnp.arange(n_dev * slots_dev, dtype=jnp.int32)[:, None]
    sums = dot(picker.astype(jnp.bfloat16), arrived.reshape(n_dev * contrib, piece * TILE)).astype(jnp.bfloat16)
    sums = lax.all_to_all(
        sums.reshape(n_dev, slots_dev, piece, TILE), ("front", "grp"), split_axis=0, concat_axis=0, tiled=True
    )
    parent_tiles = jnp.transpose(sums, (1, 0, 2, 3)).reshape(slots_dev, TILE, TILE).astype(jnp.float32)

    result, done = None, 0
    for e in range(ready + CHAINS + 1, events + CHAINS):
        take = min(2 * (e - CHAINS + 1) - done, 8)
        if take < 4 and e < events + CHAINS - 1:
            continue
        numbers = list(range(done, done + take))
        done += take
        here = after((rows,), *(turns[e] if e < events else (parent_tiles,)))[0]
        panels = [held[n // 2][n % 2] for n in numbers]
        result = update(here, mask, me, own, front, numbers, panels, base=result)
    while done < 2 * events:
        numbers = list(range(done, min(done + 8, 2 * events)))
        done += len(numbers)
        result = update(rows, mask, me, own, front, numbers, [held[n // 2][n % 2] for n in numbers], base=result)
    return (result[None], parent_tiles)


def solution(mesh):
    in_specs = (
        P("front", None, "grp"),
        P("front", None, None, None),
        P("front", None, "grp"),
        P("front", "grp", None),
    )
    out_specs = (P("front", None, "grp"), P(("front", "grp"), None, None))
    return jax.shard_map(shards, mesh=mesh, in_specs=in_specs, out_specs=out_specs, check_vma=False)
```

```python
import functools

import jax
import jax.numpy as jnp
from jax import lax
from jax.experimental import pallas as pl
from jax.experimental.pallas import tpu as pltpu
from jax.sharding import PartitionSpec as P

TILE = 256
CHAINS = 2
VMEM_LIMIT = 16 * 1024 * 1024
UPDATE_LIMIT = 32 * 1024 * 1024
HBM = pl.BlockSpec(memory_space=pltpu.HBM)
VMEM = pl.BlockSpec(memory_space=pltpu.VMEM)
SMEM = pl.BlockSpec(memory_space=pltpu.SMEM)


def ring_order(n_grp):
    depth = 4 if n_grp % 4 == 0 and n_grp >= 8 else 1
    width = n_grp // depth
    if depth == 1:
        return list(range(n_grp))
    order = [z * width for z in range(depth)]
    for number, z in enumerate(reversed(range(depth))):
        ys = range(1, width) if number % 2 == 0 else range(width - 1, 0, -1)
        order += [z * width + y for y in ys]
    return order


def routes(n_grp):
    if n_grp == 8:
        climb = [(g, (g + 2) % n_grp) for g in range(n_grp)]
        cross = [(g, g ^ 1) for g in range(n_grp)]
        rules = [[0] * n_grp, [0] * n_grp]
        rules[0][1] = rules[0][n_grp - 1] = rules[1][1] = 1
        return [climb, cross], rules
    cycle = ring_order(n_grp)
    ring = [(g, cycle[(d + 1) % n_grp]) for d, g in enumerate(cycle)]
    return [ring, [(b, a) for a, b in ring]], [[0] * n_grp, [1] * n_grp]


def travel(perms, rules, lists, n_grp, tiles):
    got = []
    missing = {(g, tile) for g in range(n_grp) for tile in range(1, tiles)}
    while missing:
        e = len(got)
        now = []
        for s in (0, 1):
            arrival = [0] * n_grp
            for g, target in perms[s]:
                if g == 0 and e < len(lists[s]):
                    arrival[target] = lists[s][e]
                elif e >= CHAINS:
                    arrival[target] = got[e - CHAINS][rules[s][g]][g]
            now.append(arrival)
            missing -= set(enumerate(arrival))
        got.append(now)
    return got


def delays(perms, rules, n_grp):
    result = [[None] * n_grp, [None] * n_grp]
    for s in (0, 1):
        lists = [[], []]
        lists[s] = [1]
        for e, now in enumerate(travel(perms, rules, lists, n_grp, 2)):
            for arrival in now:
                for g in range(n_grp):
                    if arrival[g] and result[s][g] is None:
                        result[s][g] = e
    return result


def stream_plan(perms, rules, n_grp, tiles, cols_dev, rows_out):
    hops = delays(perms, rules, n_grp)
    picks = [[], []]
    bottom = [tiles - 1 - r for r in range(rows_out)]
    heads = [bottom[0::2], bottom[1::2]]

    def shorter():
        return 0 if len(heads[0] + picks[0]) <= len(heads[1] + picks[1]) else 1

    rest = [(n // cols_dev, n) for n in range(1, tiles) if n not in bottom]
    for g, tile in rest:
        if g and hops[0][g] != hops[1][g]:
            picks[0 if hops[0][g] < hops[1][g] else 1].append((g, tile))
    for g, tile in rest:
        if g and hops[0][g] == hops[1][g]:
            picks[shorter()].append((g, tile))
    for s in (0, 1):
        picks[s].sort(key=lambda item: (-hops[s][item[0]], item[1]))
    for g, tile in rest:
        if g == 0:
            picks[shorter()].append((g, tile))
    return [heads[s] + [tile for _, tile in picks[s]] for s in (0, 1)]


def in_hbm(x):
    return pltpu.with_memory_space_constraint(x, pltpu.HBM)


def split2(x):
    hi = x.astype(jnp.bfloat16)
    return hi, (x - hi.astype(jnp.float32)).astype(jnp.bfloat16)


def dot(a, b):
    return jnp.dot(a, b, preferred_element_type=jnp.float32)


def factor_kernel(tiles, head, mask, front, *refs):
    count = len(tiles)
    if head:
        inverse, outs, (parts, one, blocks, sems, top, top_sem) = refs[0], refs[1 : count + 1], refs[count + 1 :]
    else:
        parts, one, outs, (blocks, sems) = refs[0], refs[1], refs[2 : count + 2], refs[count + 2 :]
    copies = [
        pltpu.make_async_copy(
            front.at[pl.ds(tile * TILE, TILE), pl.ds(0, 2 * TILE)], blocks.at[n], sems.at[n]
        )
        for n, tile in enumerate(tiles)
    ]
    if head:
        top_copy = pltpu.make_async_copy(front.at[pl.ds(TILE, TILE), pl.ds(0, TILE)], top, top_sem)
        top_copy.start()
    for copy in copies:
        copy.start()

    def first_of(x):
        return (dot(x, parts[1]) + dot(x, parts[0])).astype(jnp.bfloat16)

    if head:
        for which in range(2):
            hi, low = split2(inverse[which].T)
            parts[2 * which] = hi
            parts[2 * which + 1] = low
        top_copy.wait()
        one[...] = first_of(top[...]).astype(jnp.float32).T.astype(jnp.bfloat16)
    for begin in range(0, len(tiles), 2):
        group = list(range(begin, min(begin + 2, len(tiles))))
        for n in group:
            copies[n].wait()
        firsts = first_of(jnp.concatenate([blocks[n, :, :TILE] for n in group], axis=0))
        updates = dot(firsts, one[...])
        works = []
        for place, n in enumerate(group):
            keep = mask[tiles[n] : tiles[n] + 1, 1:2] > 0
            update = updates[place * TILE : (place + 1) * TILE]
            works.append(blocks[n, :, TILE:].astype(jnp.float32) - jnp.where(keep, update, 0.0))
        high, low = split2(jnp.concatenate(works, axis=0))
        seconds = (dot(low, parts[2]) + dot(high, parts[3]) + dot(high, parts[2])).astype(jnp.bfloat16)
        for place, n in enumerate(group):
            span = slice(place * TILE, (place + 1) * TILE)
            empty = jnp.zeros((TILE, TILE), jnp.bfloat16)
            outs[n][:, :TILE] = firsts[span] if tiles[n] > 0 else empty
            outs[n][:, TILE:] = seconds[span] if tiles[n] > 1 else empty


def factor(front, mask, tiles, inverse=None, parts=None):
    head = parts is None
    count = len(tiles)
    out_shape = [jax.ShapeDtypeStruct((TILE, 2 * TILE), jnp.bfloat16)] * count
    scratch = [pltpu.VMEM((count, TILE, 2 * TILE), jnp.bfloat16), pltpu.SemaphoreType.DMA((count,))]
    if head:
        out_shape += [
            jax.ShapeDtypeStruct((4, TILE, TILE), jnp.bfloat16),
            jax.ShapeDtypeStruct((TILE, TILE), jnp.bfloat16),
        ]
        scratch += [pltpu.VMEM((TILE, TILE), jnp.bfloat16), pltpu.SemaphoreType.DMA(())]
    operands = (inverse,) if head else parts
    return pl.pallas_call(
        functools.partial(factor_kernel, tuple(tiles), head),
        out_shape=out_shape,
        in_specs=[VMEM, HBM] + [VMEM] * len(operands),
        out_specs=[VMEM] * len(out_shape),
        scratch_shapes=scratch,
        compiler_params=pltpu.CompilerParams(vmem_limit_bytes=VMEM_LIMIT),
        cost_estimate=pl.CostEstimate(
            flops=12 * count * TILE**3, bytes_accessed=4 * count * TILE * 2 * TILE, transcendentals=0
        ),
        name="factor",
    )(mask, in_hbm(front), *operands)


def own_kernel(choices, sources, cols_dev, rows_out, mask, targets, me, front, *refs):
    blocks, (own, bottom, panels, old, sems, old_sem) = refs[:sources], refs[sources:]
    tiles = front.shape[0] // TILE
    width = front.shape[1]

    def copy(part, source):
        return pltpu.make_async_copy(blocks[source], panels.at[part], sems.at[part])

    old_copy = pltpu.make_async_copy(front.at[pl.ds((tiles - rows_out) * TILE, rows_out * TILE)], old, old_sem)
    old_copy.start()
    for part, options in enumerate(choices):
        for g, source in enumerate(options):
            pl.when(me[0] == g)(lambda part=part, source=source: copy(part, source).start())
    lane = lax.broadcasted_iota(jnp.int32, (rows_out * TILE, 128), 1)
    digits = jnp.zeros((rows_out * TILE, 128), jnp.int32)
    for number in range(cols_dev * rows_out):
        target = targets[number]
        digits = jnp.where(lane == 2 * number, target >> 5, digits)
        digits = jnp.where(lane == 2 * number + 1, target & 31, digits)
    bottom[:, width:] = digits.astype(jnp.float32).astype(jnp.bfloat16)
    for part, options in enumerate(choices):
        copy(part, options[0]).wait()
    for c in range(cols_dev):
        own[:, c * TILE : (c + 1) * TILE] = panels[c].astype(jnp.float32).T.astype(jnp.bfloat16)
    old_copy.wait()
    for r in range(rows_out):
        row, rows, panel = tiles - rows_out + r, slice(r * TILE, (r + 1) * TILE), panels.at[cols_dev + r]
        for c in range(cols_dev):
            span = slice(c * TILE, (c + 1) * TILE)
            change = jnp.where(mask[row, c] > 0, dot(panel[...], own[:, span]), 0.0)
            bottom[rows, span] = (old[rows, span].astype(jnp.float32) - change).astype(jnp.bfloat16)

        @pl.when(me[0] == 0)
        def _():
            bottom[rows, : 2 * TILE] = panel[...]


def own_panels(mask, targets, me, front, blocks, choices, rows_out):
    width = front.shape[1]
    parts = len(choices)
    return pl.pallas_call(
        functools.partial(own_kernel, choices, len(blocks), width // TILE, rows_out),
        out_shape=[
            jax.ShapeDtypeStruct((2 * TILE, width), jnp.bfloat16),
            jax.ShapeDtypeStruct((rows_out * TILE, width + 128), jnp.bfloat16),
        ],
        in_specs=[SMEM, SMEM, SMEM, HBM] + [HBM] * len(blocks),
        out_specs=[VMEM, VMEM],
        scratch_shapes=[
            pltpu.VMEM((parts, TILE, 2 * TILE), jnp.bfloat16),
            pltpu.VMEM((rows_out * TILE, width), jnp.bfloat16),
            pltpu.SemaphoreType.DMA((parts,)),
            pltpu.SemaphoreType.DMA(()),
        ],
        compiler_params=pltpu.CompilerParams(vmem_limit_bytes=VMEM_LIMIT),
        cost_estimate=pl.CostEstimate(
            flops=2 * rows_out * TILE * width * 2 * TILE,
            bytes_accessed=4 * parts * TILE * 2 * TILE,
            transcendentals=0,
        ),
        name="own_panels",
    )(mask, targets, me, in_hbm(front), *[in_hbm(block) for block in blocks])


def update_kernel(numbers, cols_dev, start, table, mask, me, own, front, *refs):
    count = len(numbers)
    blocks = refs[:count]
    out, panels, old, new, listed, panel_sems, in_sems, out_sems = refs[-8:]

    def place(row):
        return pl.ds(pl.multiple_of(row * TILE, TILE), TILE)

    def fetch(n, spot):
        return pltpu.make_async_copy(blocks[n], panels.at[spot], panel_sems.at[spot])

    def load(row, spot):
        return pltpu.make_async_copy(front.at[place(row)], old.at[spot], in_sems.at[spot])

    def store(row, spot):
        return pltpu.make_async_copy(new.at[spot], out.at[place(row)], out_sems.at[spot])

    spot = jnp.int32(0)
    for n, number in enumerate(numbers):
        row = table[me[0], number]

        def begin(n=n, row=row, spot=spot):
            listed[spot] = row
            fetch(n, spot).start()
            load(row, spot).start()

        pl.when(row > 0)(begin)
        spot = spot + (row > 0).astype(jnp.int32)
    total = spot
    listed[total] = 0
    if start:
        here = pl.ds(0, TILE)
        top_in = pltpu.make_async_copy(front.at[here], new.at[count], in_sems.at[count])
        top_out = pltpu.make_async_copy(new.at[count], out.at[here], out_sems.at[count])
        top_in.start()
        top_in.wait()
        top_out.start()

    @pl.loop(0, (total + 1) // 2)
    def _(pair):
        first = 2 * pair
        both = first + 1 < total

        def ready(spot):
            fetch(0, spot).wait()
            load(0, spot).wait()

        ready(first)
        pl.when(both)(lambda: ready(first + 1))
        panel = panels[pl.ds(first, 2)].reshape(2 * TILE, 2 * TILE)
        for c in range(cols_dev):
            span = slice(c * TILE, (c + 1) * TILE)
            change = dot(panel, own[:, span])
            for h in (0, 1):
                keep = mask[listed[first + h], c] > 0
                part = jnp.where(keep, change[h * TILE : (h + 1) * TILE], 0.0)
                before = old[first + h, :, span].astype(jnp.float32)
                new[first + h, :, span] = (before - part).astype(jnp.bfloat16)

        @pl.when(me[0] == 0)
        def _():
            for h in (0, 1):
                new[first + h, :, :TILE] = panels[first + h, :, :TILE]

                @pl.when(listed[first + h] > 1)
                def _():
                    new[first + h, :, TILE : 2 * TILE] = panels[first + h, :, TILE:]

        store(listed[first], first).start()
        pl.when(both)(lambda: store(listed[first + 1], first + 1).start())

    @pl.loop(0, total)
    def _(spot):
        store(0, spot).wait()

    if start:
        top_out.wait()


def update(table, mask, me, own, front, numbers, blocks, base=None):
    width = front.shape[1]
    count = len(numbers)
    room = count + count % 2
    operands = [table, mask, me, own, in_hbm(front), *[in_hbm(block) for block in blocks]]
    in_specs = [SMEM, SMEM, SMEM, VMEM, HBM] + [HBM] * count
    aliases = {}
    if base is not None:
        aliases = {len(operands): 0}
        operands.append(in_hbm(base))
        in_specs.append(HBM)
    return pl.pallas_call(
        functools.partial(update_kernel, tuple(numbers), width // TILE, base is None),
        out_shape=jax.ShapeDtypeStruct(front.shape, jnp.bfloat16),
        in_specs=in_specs,
        out_specs=HBM,
        scratch_shapes=[
            pltpu.VMEM((room, TILE, 2 * TILE), jnp.bfloat16),
            pltpu.VMEM((room, TILE, width), jnp.bfloat16),
            pltpu.VMEM((room + 1, TILE, width), jnp.bfloat16),
            pltpu.SMEM((room + 1,), jnp.int32),
            pltpu.SemaphoreType.DMA((room,)),
            pltpu.SemaphoreType.DMA((room + 1,)),
            pltpu.SemaphoreType.DMA((room + 1,)),
        ],
        input_output_aliases=aliases,
        compiler_params=pltpu.CompilerParams(vmem_limit_bytes=UPDATE_LIMIT),
        cost_estimate=pl.CostEstimate(
            flops=2 * count * TILE * width * 2 * TILE, bytes_accessed=4 * count * TILE * width, transcendentals=0
        ),
        name="update",
    )(*operands)


def after(values, *others):
    return lax.optimization_barrier((tuple(values), others))[0]


def one_of(g, members):
    result = g == members[0]
    for member in members[1:]:
        result = result | (g == member)
    return result


def shards(front_in, panel_inverse, tile_mask, tile_map):
    front = front_in[0]
    width = front.shape[1]
    tiles = front.shape[0] // TILE
    cols_dev = width // TILE
    inverse = panel_inverse[0]
    mask = tile_mask[0]
    targets = tile_map[0, 0]
    contrib = targets.shape[0]
    rows_out = contrib // cols_dev
    n_grp = lax.axis_size("grp")
    n_dev = n_grp * lax.axis_size("front")
    slots_dev = n_grp // 2
    g = lax.axis_index("grp")
    me = jnp.reshape(g, (1,)).astype(jnp.int32)
    root = g == 0

    perms, rules = routes(n_grp)
    lists = stream_plan(perms, rules, n_grp, tiles, cols_dev, rows_out)
    got = travel(perms, rules, lists, n_grp, tiles)
    events = len(got)
    longest = max(len(lists[0]), len(lists[1]))

    order = [(e, lists[s][e]) for e in range(longest) for s in (0, 1) if e < len(lists[s])] + [(longest, 0)]
    cuts = [0, 2, 6] + list(range(14, len(order) - 2, 8)) + [len(order)]
    made, parts, where_made = [], None, {}

    def make(e, turn):
        nonlocal parts
        while len(made) < len(cuts) - 1:
            begin, end = cuts[len(made)], cuts[len(made) + 1]
            if order[begin][0] > max(e + 1, e + 2 if begin > 2 else 0):
                break
            names = [tile for _, tile in order[begin:end]]
            for n, tile in enumerate(names):
                where_made[tile] = (len(made), n)
            if parts is None:
                *made_now, parts, one = factor(front, mask, names, inverse=inverse)
                parts = (parts, one)
            else:
                made_now = factor(front, mask, names, parts=after(parts, *turn))
            made.append(made_now)

    make(-2, ())
    odd = [[n for n in range(n_grp) if rules[s][n] != rules[s][0]] for s in (0, 1)]
    others = [one_of(g, odd[s]) if odd[s] else None for s in (0, 1)]
    scalars = [value for value in (root, *others) if value is not None]
    held, turns, turn = [], [], ()
    for e in range(events):
        values = []
        for s in (0, 1):
            value = None
            if e >= CHAINS:
                value = held[e - CHAINS][rules[s][0]]
                if others[s] is not None:
                    value = jnp.where(others[s], held[e - CHAINS][1 - rules[s][0]], value)
            if e < len(lists[s]):
                which, n = where_made[lists[s][e]]
                value = made[which][n] if value is None else jnp.where(root, made[which][n], value)
            values.append(value)
        turn = after(values, *turn, *(scalars if e == 0 else ()))
        turns.append(turn)
        held.append([lax.ppermute(turn[s], "grp", perms[s]) for s in (0, 1)])
        make(e, turn)
        if e + 1 < events and e + 1 >= CHAINS:
            held[e + 1 - CHAINS] = list(after(held[e + 1 - CHAINS], *turn))
    table = []
    for n in range(n_grp):
        line = []
        for now in got:
            for arrival in now:
                line.append(arrival[n] if arrival[n] not in line else 0)
        table.append(line)
    rows = jnp.asarray(table, jnp.int32)

    blocks, names, ready = [], {}, 0

    def choice(tile, n):
        nonlocal ready
        if n == 0:
            name = (-1, tile)
            which, place = where_made[tile]
            block = made[which][place]
        else:
            name = divmod(table[n].index(tile), 2)
            ready = max(ready, name[0])
            block = held[name[0]][name[1]]
        if name not in names:
            names[name] = len(blocks)
            blocks.append(block)
        return names[name]

    choices = [[choice(n * cols_dev + c, n) for n in range(n_grp)] for c in range(cols_dev)]
    choices += [[choice(tiles - rows_out + r, n) for n in range(n_grp)] for r in range(rows_out)]
    own, bottom = own_panels(mask, targets, me, front, blocks, choices, rows_out)

    piece = TILE // n_dev
    pieces = jnp.transpose(bottom.reshape(rows_out, n_dev, piece, width + 128), (1, 0, 2, 3))
    arrived = lax.all_to_all(pieces, ("front", "grp"), split_axis=0, concat_axis=0, tiled=True)

    def parents(arrived):
        digits = arrived[:, 0, 0, width : width + 2 * contrib].astype(jnp.int32).reshape(n_dev * contrib, 2)
        labels = digits[:, 0] * 32 + digits[:, 1]
        blocks = arrived[..., :width].reshape(n_dev, rows_out, piece, cols_dev, TILE)
        blocks = jnp.transpose(blocks, (0, 3, 1, 2, 4)).reshape(n_dev * contrib, piece * TILE)
        picker = labels[None, :] == jnp.arange(n_dev * slots_dev, dtype=jnp.int32)[:, None]
        sums = dot(picker.astype(jnp.bfloat16), blocks).astype(jnp.bfloat16)
        sums = lax.all_to_all(
            sums.reshape(n_dev, slots_dev, piece, TILE), ("front", "grp"), split_axis=0, concat_axis=0, tiled=True
        )
        return jnp.transpose(sums, (1, 0, 2, 3)).reshape(slots_dev, TILE, TILE).astype(jnp.float32)

    result, parent_tiles = None, None
    done, e = 0, ready + CHAINS + 1
    while done < 2 * events:
        at_hand = 2 * min(e - CHAINS + 1, events)
        take = min(at_hand - done, 16)
        if e < events - 1 and take < 16:
            e += 1
            continue
        numbers = list(range(done, done + take))
        done += take
        if e >= events - 1 and parent_tiles is None:
            parent_tiles = parents(after((arrived,), result)[0])
        here = after((me,), *(turns[e] if e < events else (parent_tiles,)))[0]
        result = update(rows, mask, here, own, front, numbers, [held[n // 2][n % 2] for n in numbers], base=result)
        e = min(e + 2, events - 1) if e < events - 1 else e + CHAINS
    return (result[None], parent_tiles)


def solution(mesh):
    in_specs = (
        P("front", None, "grp"),
        P("front", None, None, None),
        P("front", None, "grp"),
        P("front", "grp", None),
    )
    out_specs = (P("front", None, "grp"), P(("front", "grp"), None, None))
    return jax.shard_map(shards, mesh=mesh, in_specs=in_specs, out_specs=out_specs, check_vma=False)
```

```python
import functools

import jax
import jax.numpy as jnp
from jax import lax
from jax.experimental import pallas as pl
from jax.experimental.pallas import tpu as pltpu
from jax.sharding import PartitionSpec as P

TILE = 256
CHAINS = 2
SUM_AFTER = 3
VMEM_LIMIT = 16 * 1024 * 1024
UPDATE_LIMIT = 32 * 1024 * 1024
HBM = pl.BlockSpec(memory_space=pltpu.HBM)
VMEM = pl.BlockSpec(memory_space=pltpu.VMEM)
SMEM = pl.BlockSpec(memory_space=pltpu.SMEM)


def ring_order(n_grp):
    depth = 4 if n_grp % 4 == 0 and n_grp >= 8 else 1
    width = n_grp // depth
    if depth == 1:
        return list(range(n_grp))
    order = [z * width for z in range(depth)]
    for number, z in enumerate(reversed(range(depth))):
        ys = range(1, width) if number % 2 == 0 else range(width - 1, 0, -1)
        order += [z * width + y for y in ys]
    return order


def routes(n_grp):
    if n_grp == 8:
        climb = [(g, (g + 2) % n_grp) for g in range(n_grp)]
        cross = [(g, g ^ 1) for g in range(n_grp)]
        rules = [[0] * n_grp, [0] * n_grp]
        rules[0][1] = rules[0][n_grp - 1] = rules[1][1] = 1
        return [climb, cross], rules
    cycle = ring_order(n_grp)
    ring = [(g, cycle[(d + 1) % n_grp]) for d, g in enumerate(cycle)]
    return [ring, [(b, a) for a, b in ring]], [[0] * n_grp, [1] * n_grp]


def travel(perms, rules, lists, n_grp, tiles):
    got = []
    missing = {(g, tile) for g in range(n_grp) for tile in range(1, tiles)}
    while missing:
        e = len(got)
        now = []
        for s in (0, 1):
            arrival = [0] * n_grp
            for g, target in perms[s]:
                if g == 0 and e < len(lists[s]):
                    arrival[target] = lists[s][e]
                elif e >= CHAINS:
                    arrival[target] = got[e - CHAINS][rules[s][g]][g]
            now.append(arrival)
            missing -= set(enumerate(arrival))
        got.append(now)
    return got


def delays(perms, rules, n_grp):
    result = [[None] * n_grp, [None] * n_grp]
    for s in (0, 1):
        lists = [[], []]
        lists[s] = [1]
        for e, now in enumerate(travel(perms, rules, lists, n_grp, 2)):
            for arrival in now:
                for g in range(n_grp):
                    if arrival[g] and result[s][g] is None:
                        result[s][g] = e
    return result


def stream_plan(perms, rules, n_grp, tiles, cols_dev, rows_out):
    hops = delays(perms, rules, n_grp)
    picks = [[], []]
    bottom = [tiles - 1 - r for r in range(rows_out)]
    heads = [bottom[0::2], bottom[1::2]]

    def shorter():
        return 0 if len(heads[0] + picks[0]) <= len(heads[1] + picks[1]) else 1

    rest = [(n // cols_dev, n) for n in range(1, tiles) if n not in bottom]
    for g, tile in rest:
        if g and hops[0][g] != hops[1][g]:
            picks[0 if hops[0][g] < hops[1][g] else 1].append((g, tile))
    for g, tile in rest:
        if g and hops[0][g] == hops[1][g]:
            picks[shorter()].append((g, tile))
    for s in (0, 1):
        picks[s].sort(key=lambda item: (-hops[s][item[0]], item[1]))
    for g, tile in rest:
        if g == 0:
            picks[shorter()].append((g, tile))
    return [heads[s] + [tile for _, tile in picks[s]] for s in (0, 1)]


def in_hbm(x):
    return pltpu.with_memory_space_constraint(x, pltpu.HBM)


def split2(x):
    hi = x.astype(jnp.bfloat16)
    return hi, (x - hi.astype(jnp.float32)).astype(jnp.bfloat16)


def dot(a, b):
    return jnp.dot(a, b, preferred_element_type=jnp.float32)


def factor_kernel(tiles, head, mask, front, *refs):
    count = len(tiles)
    if head:
        source, outs, rest = refs[0], refs[1 : count + 1], refs[count + 1 :]
        parts, one, blocks, sems, top, top_sem, inverse, inverse_sem = rest
        inverse_copy = pltpu.make_async_copy(source, inverse, inverse_sem)
        inverse_copy.start()
    else:
        parts, one, outs, (blocks, sems) = refs[0], refs[1], refs[2 : count + 2], refs[count + 2 :]
    copies = [
        pltpu.make_async_copy(
            front.at[pl.ds(tile * TILE, TILE), pl.ds(0, 2 * TILE)], blocks.at[n], sems.at[n]
        )
        for n, tile in enumerate(tiles)
    ]
    if head:
        top_copy = pltpu.make_async_copy(front.at[pl.ds(TILE, TILE), pl.ds(0, TILE)], top, top_sem)
        top_copy.start()
    for copy in copies:
        copy.start()

    def first_of(x):
        return (dot(x, parts[1]) + dot(x, parts[0])).astype(jnp.bfloat16)

    if head:
        inverse_copy.wait()
        for which in range(2):
            hi, low = split2(inverse[which].T)
            parts[2 * which] = hi
            parts[2 * which + 1] = low
        top_copy.wait()
        one[...] = first_of(top[...]).astype(jnp.float32).T.astype(jnp.bfloat16)
    for begin in range(0, len(tiles), 2):
        group = list(range(begin, min(begin + 2, len(tiles))))
        for n in group:
            copies[n].wait()
        firsts = first_of(jnp.concatenate([blocks[n, :, :TILE] for n in group], axis=0))
        updates = dot(firsts, one[...])
        works = []
        for place, n in enumerate(group):
            keep = mask[tiles[n] : tiles[n] + 1, 1:2] > 0
            update = updates[place * TILE : (place + 1) * TILE]
            works.append(blocks[n, :, TILE:].astype(jnp.float32) - jnp.where(keep, update, 0.0))
        high, low = split2(jnp.concatenate(works, axis=0))
        seconds = (dot(low, parts[2]) + dot(high, parts[3]) + dot(high, parts[2])).astype(jnp.bfloat16)
        for place, n in enumerate(group):
            span = slice(place * TILE, (place + 1) * TILE)
            empty = jnp.zeros((TILE, TILE), jnp.bfloat16)
            outs[n][:, :TILE] = firsts[span] if tiles[n] > 0 else empty
            outs[n][:, TILE:] = seconds[span] if tiles[n] > 1 else empty


def factor(front, mask, tiles, inverse=None, parts=None):
    head = parts is None
    count = len(tiles)
    out_shape = [jax.ShapeDtypeStruct((TILE, 2 * TILE), jnp.bfloat16)] * count
    scratch = [pltpu.VMEM((count, TILE, 2 * TILE), jnp.bfloat16), pltpu.SemaphoreType.DMA((count,))]
    if head:
        out_shape += [
            jax.ShapeDtypeStruct((4, TILE, TILE), jnp.bfloat16),
            jax.ShapeDtypeStruct((TILE, TILE), jnp.bfloat16),
        ]
        scratch += [pltpu.VMEM((TILE, TILE), jnp.bfloat16), pltpu.SemaphoreType.DMA(())]
        scratch += [pltpu.VMEM((2, TILE, TILE), jnp.float32), pltpu.SemaphoreType.DMA(())]
    operands = (in_hbm(inverse),) if head else parts
    return pl.pallas_call(
        functools.partial(factor_kernel, tuple(tiles), head),
        out_shape=out_shape,
        in_specs=[VMEM, HBM] + [HBM if head else VMEM] * len(operands),
        out_specs=[VMEM] * len(out_shape),
        scratch_shapes=scratch,
        compiler_params=pltpu.CompilerParams(vmem_limit_bytes=VMEM_LIMIT),
        cost_estimate=pl.CostEstimate(
            flops=12 * count * TILE**3, bytes_accessed=4 * count * TILE * 2 * TILE, transcendentals=0
        ),
        name="factor",
    )(mask, in_hbm(front), *operands)


def own_kernel(choices, sources, cols_dev, rows_out, mask, targets, me, front, *refs):
    blocks, (own, bottom, panels, old, sems, old_sem) = refs[:sources], refs[sources:]
    tiles = front.shape[0] // TILE
    width = front.shape[1]

    def copy(part, source):
        return pltpu.make_async_copy(blocks[source], panels.at[part], sems.at[part])

    old_copy = pltpu.make_async_copy(front.at[pl.ds((tiles - rows_out) * TILE, rows_out * TILE)], old, old_sem)
    old_copy.start()
    for part, options in enumerate(choices):
        for g, source in enumerate(options):
            pl.when(me[0] == g)(lambda part=part, source=source: copy(part, source).start())
    lane = lax.broadcasted_iota(jnp.int32, (rows_out * TILE, 128), 1)
    digits = jnp.zeros((rows_out * TILE, 128), jnp.int32)
    for number in range(cols_dev * rows_out):
        target = targets[number]
        digits = jnp.where(lane == 2 * number, target >> 5, digits)
        digits = jnp.where(lane == 2 * number + 1, target & 31, digits)
    bottom[:, width:] = digits.astype(jnp.float32).astype(jnp.bfloat16)
    for part, options in enumerate(choices):
        copy(part, options[0]).wait()
    for c in range(cols_dev):
        own[:, c * TILE : (c + 1) * TILE] = panels[c].astype(jnp.float32).T.astype(jnp.bfloat16)
    old_copy.wait()
    for r in range(rows_out):
        row, rows, panel = tiles - rows_out + r, slice(r * TILE, (r + 1) * TILE), panels.at[cols_dev + r]
        for c in range(cols_dev):
            span = slice(c * TILE, (c + 1) * TILE)
            change = jnp.where(mask[row, c] > 0, dot(panel[...], own[:, span]), 0.0)
            bottom[rows, span] = (old[rows, span].astype(jnp.float32) - change).astype(jnp.bfloat16)

        @pl.when(me[0] == 0)
        def _():
            bottom[rows, : 2 * TILE] = panel[...]


def own_panels(mask, targets, me, front, blocks, choices, rows_out):
    width = front.shape[1]
    parts = len(choices)
    return pl.pallas_call(
        functools.partial(own_kernel, choices, len(blocks), width // TILE, rows_out),
        out_shape=[
            jax.ShapeDtypeStruct((2 * TILE, width), jnp.bfloat16),
            jax.ShapeDtypeStruct((rows_out * TILE, width + 128), jnp.bfloat16),
        ],
        in_specs=[SMEM, SMEM, SMEM, HBM] + [HBM] * len(blocks),
        out_specs=[VMEM, VMEM],
        scratch_shapes=[
            pltpu.VMEM((parts, TILE, 2 * TILE), jnp.bfloat16),
            pltpu.VMEM((rows_out * TILE, width), jnp.bfloat16),
            pltpu.SemaphoreType.DMA((parts,)),
            pltpu.SemaphoreType.DMA(()),
        ],
        compiler_params=pltpu.CompilerParams(vmem_limit_bytes=VMEM_LIMIT),
        cost_estimate=pl.CostEstimate(
            flops=2 * rows_out * TILE * width * 2 * TILE,
            bytes_accessed=4 * parts * TILE * 2 * TILE,
            transcendentals=0,
        ),
        name="own_panels",
    )(mask, targets, me, in_hbm(front), *[in_hbm(block) for block in blocks])


def update_kernel(numbers, cols_dev, start, table, mask, me, own, front, *refs):
    count = len(numbers)
    blocks = refs[:count]
    out, panels, old, new, listed, panel_sems, in_sems, out_sems = refs[-8:]

    def place(row):
        return pl.ds(pl.multiple_of(row * TILE, TILE), TILE)

    def fetch(n, spot):
        return pltpu.make_async_copy(blocks[n], panels.at[spot], panel_sems.at[spot])

    def load(row, spot):
        return pltpu.make_async_copy(front.at[place(row)], old.at[spot], in_sems.at[spot])

    def store(row, spot):
        return pltpu.make_async_copy(new.at[spot], out.at[place(row)], out_sems.at[spot])

    spot = jnp.int32(0)
    for n, number in enumerate(numbers):
        row = table[me[0], number]

        def begin(n=n, row=row, spot=spot):
            listed[spot] = row
            fetch(n, spot).start()
            pl.when(spot < 4)(lambda: load(row, spot).start())

        pl.when(row > 0)(begin)
        spot = spot + (row > 0).astype(jnp.int32)
    total = spot
    listed[total] = 0
    if start:
        here = pl.ds(0, TILE)
        top_in = pltpu.make_async_copy(front.at[here], new.at[count], in_sems.at[count])
        top_out = pltpu.make_async_copy(new.at[count], out.at[here], out_sems.at[count])
        top_in.start()
        top_in.wait()
        top_out.start()

    @pl.loop(0, (total + 1) // 2)
    def _(pair):
        first = 2 * pair
        both = first + 1 < total

        def ready(spot):
            fetch(0, spot).wait()
            load(0, spot).wait()

        for ahead in (first + 4, first + 5):
            pl.when(ahead < total)(lambda ahead=ahead: load(listed[ahead], ahead).start())
        ready(first)
        pl.when(both)(lambda: ready(first + 1))
        panel = panels[pl.ds(first, 2)].reshape(2 * TILE, 2 * TILE)
        for c in range(cols_dev):
            span = slice(c * TILE, (c + 1) * TILE)
            change = dot(panel, own[:, span])
            for h in (0, 1):
                keep = mask[listed[first + h], c] > 0
                part = jnp.where(keep, change[h * TILE : (h + 1) * TILE], 0.0)
                before = old[first + h, :, span].astype(jnp.float32)
                new[first + h, :, span] = (before - part).astype(jnp.bfloat16)

        @pl.when(me[0] == 0)
        def _():
            for h in (0, 1):
                new[first + h, :, :TILE] = panels[first + h, :, :TILE]

                @pl.when(listed[first + h] > 1)
                def _():
                    new[first + h, :, TILE : 2 * TILE] = panels[first + h, :, TILE:]

        store(listed[first], first).start()
        pl.when(both)(lambda: store(listed[first + 1], first + 1).start())

    @pl.loop(0, total)
    def _(spot):
        store(0, spot).wait()

    if start:
        top_out.wait()


def update(table, mask, me, own, front, numbers, blocks, base=None):
    width = front.shape[1]
    count = len(numbers)
    room = count + count % 2
    operands = [table, mask, me, own, in_hbm(front), *[in_hbm(block) for block in blocks]]
    in_specs = [SMEM, SMEM, SMEM, VMEM, HBM] + [HBM] * count
    aliases = {}
    if base is not None:
        aliases = {len(operands): 0}
        operands.append(in_hbm(base))
        in_specs.append(HBM)
    return pl.pallas_call(
        functools.partial(update_kernel, tuple(numbers), width // TILE, base is None),
        out_shape=jax.ShapeDtypeStruct(front.shape, jnp.bfloat16),
        in_specs=in_specs,
        out_specs=HBM,
        scratch_shapes=[
            pltpu.VMEM((room, TILE, 2 * TILE), jnp.bfloat16),
            pltpu.VMEM((room, TILE, width), jnp.bfloat16),
            pltpu.VMEM((room + 1, TILE, width), jnp.bfloat16),
            pltpu.SMEM((room + 1,), jnp.int32),
            pltpu.SemaphoreType.DMA((room,)),
            pltpu.SemaphoreType.DMA((room + 1,)),
            pltpu.SemaphoreType.DMA((room + 1,)),
        ],
        input_output_aliases=aliases,
        compiler_params=pltpu.CompilerParams(vmem_limit_bytes=UPDATE_LIMIT),
        cost_estimate=pl.CostEstimate(
            flops=2 * count * TILE * width * 2 * TILE, bytes_accessed=4 * count * TILE * width, transcendentals=0
        ),
        name="update",
    )(*operands)


def after(values, *others):
    return lax.optimization_barrier((tuple(values), others))[0]


def one_of(g, members):
    result = g == members[0]
    for member in members[1:]:
        result = result | (g == member)
    return result


def shards(front_in, panel_inverse, tile_mask, tile_map):
    front = front_in[0]
    width = front.shape[1]
    tiles = front.shape[0] // TILE
    cols_dev = width // TILE
    inverse = panel_inverse[0]
    mask = tile_mask[0]
    targets = tile_map[0, 0]
    contrib = targets.shape[0]
    rows_out = contrib // cols_dev
    n_grp = lax.axis_size("grp")
    n_dev = n_grp * lax.axis_size("front")
    slots_dev = n_grp // 2
    g = lax.axis_index("grp")
    me = jnp.reshape(g, (1,)).astype(jnp.int32)
    root = g == 0

    perms, rules = routes(n_grp)
    lists = stream_plan(perms, rules, n_grp, tiles, cols_dev, rows_out)
    got = travel(perms, rules, lists, n_grp, tiles)
    events = len(got)
    longest = max(len(lists[0]), len(lists[1]))

    order = [(e, lists[s][e]) for e in range(longest) for s in (0, 1) if e < len(lists[s])] + [(longest, 0)]
    cuts = [0, 4, 8] + list(range(16, len(order) - 2, 8)) + [len(order)]
    made, parts, where_made = [], None, {}

    def make(e, turn):
        nonlocal parts
        while len(made) < len(cuts) - 1:
            begin, end = cuts[len(made)], cuts[len(made) + 1]
            if order[begin][0] > max(0, e + 1 if begin < 8 else e + 2):
                break
            names = [tile for _, tile in order[begin:end]]
            for n, tile in enumerate(names):
                where_made[tile] = (len(made), n)
            if parts is None:
                *made_now, parts, one = factor(front, mask, names, inverse=inverse)
                parts = (parts, one)
            else:
                made_now = factor(front, mask, names, parts=after(parts, *turn))
            made.append(made_now)

    make(-2, ())
    odd = [[n for n in range(n_grp) if rules[s][n] != rules[s][0]] for s in (0, 1)]
    others = [one_of(g, odd[s]) if odd[s] else None for s in (0, 1)]
    scalars = [value for value in (root, *others) if value is not None]
    table = []
    for n in range(n_grp):
        line = []
        for now in got:
            for arrival in now:
                line.append(arrival[n] if arrival[n] not in line else 0)
        table.append(line)
    rows = jnp.asarray(table, jnp.int32)
    used = [[any(line[2 * e + s] for line in table) for s in (0, 1)] for e in range(events)]
    for e in reversed(range(events - CHAINS)):
        for s in (0, 1):
            used[e][s] = used[e][s] or any(used[e + CHAINS])

    needed = [
        [n * cols_dev + c for c in range(cols_dev)] + [tiles - rows_out + r for r in range(rows_out)]
        for n in range(n_grp)
    ]
    ready = max(table[n].index(tile) // 2 for n in range(1, n_grp) for tile in needed[n])

    def own_part():
        blocks, names = [], {}

        def choice(tile, n):
            if n == 0:
                name = (-1, tile)
                which, place = where_made[tile]
                block = made[which][place]
            else:
                name = divmod(table[n].index(tile), 2)
                block = held[name[0]][name[1]]
            if name not in names:
                names[name] = len(blocks)
                blocks.append(block)
            return names[name]

        choices = [[choice(needed[n][part], n) for n in range(n_grp)] for part in range(cols_dev + rows_out)]
        return own_panels(mask, targets, me, front, blocks, choices, rows_out)

    piece = TILE // n_dev

    def exchange(blocks):
        return lax.all_to_all(blocks, ("front", "grp"), split_axis=0, concat_axis=0, tiled=True)

    def sums_of(arrived):
        digits = arrived[:, 0, 0, width : width + 2 * contrib].astype(jnp.int32).reshape(n_dev * contrib, 2)
        labels = digits[:, 0] * 32 + digits[:, 1]
        blocks = arrived[..., :width].reshape(n_dev, rows_out, piece, cols_dev, TILE)
        blocks = jnp.transpose(blocks, (0, 3, 1, 2, 4)).reshape(n_dev * contrib, piece * TILE)
        picker = labels[None, :] == jnp.arange(n_dev * slots_dev, dtype=jnp.int32)[:, None]
        sums = dot(picker.astype(jnp.bfloat16), blocks).astype(jnp.bfloat16)
        return sums.reshape(n_dev, slots_dev, piece, TILE)

    held, turn, result, done = [], (), None, 0

    def step(limit, at_hand, *waits):
        nonlocal result, done
        numbers = list(range(done, min(done + limit, at_hand)))
        done += len(numbers)
        here = after((me,), *waits)[0]
        blocks = [held[n // 2][n % 2] for n in numbers]
        if numbers:
            result = update(rows, mask, here, own, front, numbers, blocks, base=result)

    for e in range(events):
        values = []
        for s in (0, 1):
            value = None
            if e >= CHAINS:
                value = held[e - CHAINS][rules[s][0]]
                if others[s] is not None:
                    value = jnp.where(others[s], held[e - CHAINS][1 - rules[s][0]], value)
            if e < len(lists[s]):
                which, n = where_made[lists[s][e]]
                value = made[which][n] if value is None else jnp.where(root, made[which][n], value)
            values.append(value)
        turn = after(values, *turn, *(scalars if e == 0 else ()))
        held.append([lax.ppermute(turn[s], "grp", perms[s]) if used[e][s] else turn[s] for s in (0, 1)])
        make(e, turn)
        if CHAINS <= e + 1 < events:
            held[e + 1 - CHAINS] = list(after(held[e + 1 - CHAINS], *turn))
        late = e - ready - CHAINS
        if late == 0:
            own, bottom = own_part()
            pieces = jnp.transpose(bottom.reshape(rows_out, n_dev, piece, width + 128), (1, 0, 2, 3))
            arrived = exchange(pieces)
        if late == SUM_AFTER:
            sums = sums_of(after((arrived,), *turn)[0])
            parent_pieces = exchange(sums)
            turn = (*turn, sums)
        if late >= 2 and late % 2 == 0:
            step(12, 2 * (e - CHAINS + 1), *turn)
            turn = (*turn, result)
    parent_tiles = jnp.transpose(parent_pieces, (1, 0, 2, 3)).reshape(slots_dev, TILE, TILE).astype(jnp.float32)
    if done < 2 * (events - CHAINS):
        step(12, 2 * (events - CHAINS), *turn)
    while done < 2 * events:
        step(12, 2 * events, parent_tiles)
    return (result[None], parent_tiles)


def solution(mesh):
    in_specs = (
        P("front", None, "grp"),
        P("front", None, None, None),
        P("front", None, "grp"),
        P("front", "grp", None),
    )
    out_specs = (P("front", None, "grp"), P(("front", "grp"), None, None))
    return jax.shard_map(shards, mesh=mesh, in_specs=in_specs, out_specs=out_specs, check_vma=False)
```

```python
import functools
import itertools

import jax
import jax.numpy as jnp
from jax import lax
from jax.experimental import pallas as pl
from jax.experimental.pallas import tpu as pltpu
from jax.sharding import PartitionSpec as P

TILE = 256
CHAINS = 2
SUM_AFTER = 4
VMEM_LIMIT = 16 * 1024 * 1024
UPDATE_LIMIT = 32 * 1024 * 1024
HBM = pl.BlockSpec(memory_space=pltpu.HBM)
VMEM = pl.BlockSpec(memory_space=pltpu.VMEM)
SMEM = pl.BlockSpec(memory_space=pltpu.SMEM)


def ring_order(n_grp):
    depth = 4 if n_grp % 4 == 0 and n_grp >= 8 else 1
    width = n_grp // depth
    if depth == 1:
        return list(range(n_grp))
    order = [z * width for z in range(depth)]
    for number, z in enumerate(reversed(range(depth))):
        ys = range(1, width) if number % 2 == 0 else range(width - 1, 0, -1)
        order += [z * width + y for y in ys]
    return order


def routes(n_grp):
    if n_grp == 8:
        climb = [(g, (g + 2) % n_grp) for g in range(n_grp)]
        cross = [(g, g ^ 1) for g in range(n_grp)]
        rules = [[0] * n_grp, [0] * n_grp]
        rules[0][1] = rules[0][n_grp - 1] = rules[1][1] = 1
        return [climb, cross], rules
    cycle = ring_order(n_grp)
    ring = [(g, cycle[(d + 1) % n_grp]) for d, g in enumerate(cycle)]
    return [ring, [(b, a) for a, b in ring]], [[0] * n_grp, [1] * n_grp]


def travel(perms, rules, lists, n_grp, tiles):
    got = []
    missing = {(g, tile) for g in range(1, n_grp) for tile in range(1, tiles)}
    while missing:
        e = len(got)
        now = []
        for s in (0, 1):
            arrival = [0] * n_grp
            for g, target in perms[s]:
                if g == 0 and e < len(lists[s]):
                    arrival[target] = lists[s][e]
                elif e >= CHAINS:
                    arrival[target] = got[e - CHAINS][rules[s][g]][g]
            now.append(arrival)
            missing -= set(enumerate(arrival))
        got.append(now)
    return got


def delays(perms, rules, n_grp):
    result = [[None] * n_grp, [None] * n_grp]
    for s in (0, 1):
        lists = [[], []]
        lists[s] = [1]
        for e, now in enumerate(travel(perms, rules, lists, n_grp, 2)):
            for arrival in now:
                for g in range(n_grp):
                    if arrival[g] and result[s][g] is None:
                        result[s][g] = e
    return result


def stream_plan(perms, rules, n_grp, tiles, cols_dev, rows_out):
    hops = delays(perms, rules, n_grp)
    picks = [[], []]
    bottom = [tiles - 1 - r for r in range(rows_out)]
    heads = [bottom[0::2], bottom[1::2]]

    def shorter():
        return 0 if len(heads[0] + picks[0]) <= len(heads[1] + picks[1]) else 1

    rest = [(n // cols_dev, n) for n in range(1, tiles) if n not in bottom]
    for g, tile in rest:
        if g and hops[0][g] != hops[1][g]:
            picks[0 if hops[0][g] < hops[1][g] else 1].append((g, tile))
    for g, tile in rest:
        if g and hops[0][g] == hops[1][g]:
            picks[shorter()].append((g, tile))
    for s in (0, 1):
        picks[s].sort(key=lambda item: (-hops[s][item[0]], item[1]))
    for g, tile in rest:
        if g == 0:
            picks[shorter()].append((g, tile))
    return [heads[s] + [tile for _, tile in picks[s]] for s in (0, 1)]


def live_pairs(perms, rules, lists, got, table, n_grp):
    width = max(n_grp // 4, 1)
    live = [[set(), set()] for _ in got]
    result = [[[], []] for _ in got]
    for e in reversed(range(len(got))):
        for s in (0, 1):
            for g, target in perms[s]:
                needed = target and table[target][2 * e + s]
                later = e + CHAINS
                if target and later < len(got):
                    needed = needed or any(rules[t][target] == s and target in live[later][t] for t in (0, 1))
                if needed:
                    live[e][s].add(g)
            if not live[e][s]:
                continue
            pairs = [(g, target) for g, target in perms[s] if g in live[e][s]]
            sources = set(range(n_grp)) - {g for g, _ in pairs}
            targets = set(range(n_grp)) - {target for _, target in pairs}
            pairs += [(g, g) for g in sorted(sources & targets)]
            sources, targets = sorted(sources - targets, reverse=True), sorted(targets - sources)
            best = list(zip(sources, targets))
            if len(sources) <= 4:
                best = min(
                    (list(zip(sources, order)) for order in itertools.permutations(targets)),
                    key=lambda some: sum(max(0, v // width - u // width) for u, v in some),
                )
            result[e][s] = pairs + best
    return result


def in_hbm(x):
    return pltpu.with_memory_space_constraint(x, pltpu.HBM)


def split2(x):
    hi = x.astype(jnp.bfloat16)
    return hi, (x - hi.astype(jnp.float32)).astype(jnp.bfloat16)


def dot(a, b):
    return jnp.dot(a, b, preferred_element_type=jnp.float32)


def factor_kernel(tiles, head, mask, front, *refs):
    count = len(tiles)
    if head:
        source, outs, rest = refs[0], refs[1 : count + 1], refs[count + 1 :]
        parts, one, blocks, sems, top, top_sem, inverse, inverse_sem = rest
        inverse_copy = pltpu.make_async_copy(source, inverse, inverse_sem)
        inverse_copy.start()
    else:
        parts, one, outs, (blocks, sems) = refs[0], refs[1], refs[2 : count + 2], refs[count + 2 :]
    copies = [
        pltpu.make_async_copy(
            front.at[pl.ds(tile * TILE, TILE), pl.ds(0, 2 * TILE)], blocks.at[n], sems.at[n]
        )
        for n, tile in enumerate(tiles)
    ]
    if head:
        top_copy = pltpu.make_async_copy(front.at[pl.ds(TILE, TILE), pl.ds(0, TILE)], top, top_sem)
        top_copy.start()
    for copy in copies:
        copy.start()

    def first_of(x):
        return (dot(x, parts[1]) + dot(x, parts[0])).astype(jnp.bfloat16)

    if head:
        inverse_copy.wait()
        for which in range(2):
            hi, low = split2(inverse[which].T)
            parts[2 * which] = hi
            parts[2 * which + 1] = low
        top_copy.wait()
        one[...] = first_of(top[...]).astype(jnp.float32).T.astype(jnp.bfloat16)
    for begin in range(0, len(tiles), 2):
        group = list(range(begin, min(begin + 2, len(tiles))))
        for n in group:
            copies[n].wait()
        firsts = first_of(jnp.concatenate([blocks[n, :, :TILE] for n in group], axis=0))
        updates = dot(firsts, one[...])
        works = []
        for place, n in enumerate(group):
            keep = mask[tiles[n] : tiles[n] + 1, 1:2] > 0
            update = updates[place * TILE : (place + 1) * TILE]
            works.append(blocks[n, :, TILE:].astype(jnp.float32) - jnp.where(keep, update, 0.0))
        high, low = split2(jnp.concatenate(works, axis=0))
        seconds = (dot(low, parts[2]) + dot(high, parts[3]) + dot(high, parts[2])).astype(jnp.bfloat16)
        for place, n in enumerate(group):
            span = slice(place * TILE, (place + 1) * TILE)
            empty = jnp.zeros((TILE, TILE), jnp.bfloat16)
            outs[n][:, :TILE] = firsts[span] if tiles[n] > 0 else empty
            outs[n][:, TILE:] = seconds[span] if tiles[n] > 1 else empty


def factor(front, mask, tiles, inverse=None, parts=None):
    head = parts is None
    count = len(tiles)
    out_shape = [jax.ShapeDtypeStruct((TILE, 2 * TILE), jnp.bfloat16)] * count
    scratch = [pltpu.VMEM((count, TILE, 2 * TILE), jnp.bfloat16), pltpu.SemaphoreType.DMA((count,))]
    if head:
        out_shape += [
            jax.ShapeDtypeStruct((4, TILE, TILE), jnp.bfloat16),
            jax.ShapeDtypeStruct((TILE, TILE), jnp.bfloat16),
        ]
        scratch += [pltpu.VMEM((TILE, TILE), jnp.bfloat16), pltpu.SemaphoreType.DMA(())]
        scratch += [pltpu.VMEM((2, TILE, TILE), jnp.float32), pltpu.SemaphoreType.DMA(())]
    operands = (in_hbm(inverse),) if head else parts
    return pl.pallas_call(
        functools.partial(factor_kernel, tuple(tiles), head),
        out_shape=out_shape,
        in_specs=[VMEM, HBM] + [HBM if head else VMEM] * len(operands),
        out_specs=[VMEM] * len(out_shape),
        scratch_shapes=scratch,
        compiler_params=pltpu.CompilerParams(vmem_limit_bytes=VMEM_LIMIT),
        cost_estimate=pl.CostEstimate(
            flops=12 * count * TILE**3, bytes_accessed=4 * count * TILE * 2 * TILE, transcendentals=0
        ),
        name="factor",
    )(mask, in_hbm(front), *operands)


def own_kernel(choices, sources, cols_dev, rows_out, mask, targets, me, front, *refs):
    blocks, (own, bottom, panels, old, sems, old_sem) = refs[:sources], refs[sources:]
    tiles = front.shape[0] // TILE
    width = front.shape[1]

    def copy(part, source):
        return pltpu.make_async_copy(blocks[source], panels.at[part], sems.at[part])

    old_copy = pltpu.make_async_copy(front.at[pl.ds((tiles - rows_out) * TILE, rows_out * TILE)], old, old_sem)
    old_copy.start()
    for part, options in enumerate(choices):
        for g, source in enumerate(options):
            pl.when(me[0] == g)(lambda part=part, source=source: copy(part, source).start())
    lane = lax.broadcasted_iota(jnp.int32, (rows_out * TILE, 128), 1)
    digits = jnp.zeros((rows_out * TILE, 128), jnp.int32)
    for number in range(cols_dev * rows_out):
        target = targets[number]
        digits = jnp.where(lane == 2 * number, target >> 5, digits)
        digits = jnp.where(lane == 2 * number + 1, target & 31, digits)
    bottom[:, width:] = digits.astype(jnp.float32).astype(jnp.bfloat16)
    for part, options in enumerate(choices):
        copy(part, options[0]).wait()
    for c in range(cols_dev):
        own[:, c * TILE : (c + 1) * TILE] = panels[c].astype(jnp.float32).T.astype(jnp.bfloat16)
    old_copy.wait()
    for r in range(rows_out):
        row, rows, panel = tiles - rows_out + r, slice(r * TILE, (r + 1) * TILE), panels.at[cols_dev + r]
        for c in range(cols_dev):
            span = slice(c * TILE, (c + 1) * TILE)
            change = jnp.where(mask[row, c] > 0, dot(panel[...], own[:, span]), 0.0)
            bottom[rows, span] = (old[rows, span].astype(jnp.float32) - change).astype(jnp.bfloat16)

        @pl.when(me[0] == 0)
        def _():
            bottom[rows, : 2 * TILE] = panel[...]


def own_panels(mask, targets, me, front, blocks, choices, rows_out):
    width = front.shape[1]
    parts = len(choices)
    return pl.pallas_call(
        functools.partial(own_kernel, choices, len(blocks), width // TILE, rows_out),
        out_shape=[
            jax.ShapeDtypeStruct((2 * TILE, width), jnp.bfloat16),
            jax.ShapeDtypeStruct((rows_out * TILE, width + 128), jnp.bfloat16),
        ],
        in_specs=[SMEM, SMEM, SMEM, HBM] + [HBM] * len(blocks),
        out_specs=[VMEM, VMEM],
        scratch_shapes=[
            pltpu.VMEM((parts, TILE, 2 * TILE), jnp.bfloat16),
            pltpu.VMEM((rows_out * TILE, width), jnp.bfloat16),
            pltpu.SemaphoreType.DMA((parts,)),
            pltpu.SemaphoreType.DMA(()),
        ],
        compiler_params=pltpu.CompilerParams(vmem_limit_bytes=VMEM_LIMIT),
        cost_estimate=pl.CostEstimate(
            flops=2 * rows_out * TILE * width * 2 * TILE,
            bytes_accessed=4 * parts * TILE * 2 * TILE,
            transcendentals=0,
        ),
        name="own_panels",
    )(mask, targets, me, in_hbm(front), *[in_hbm(block) for block in blocks])


def update_kernel(numbers, room, cols_dev, start, table, mask, me, own, front, *refs):
    count = len(numbers)
    blocks = refs[:count]
    out, panels, old, new, listed, panel_sems, in_sems, out_sems = refs[-8:]

    def place(row):
        return pl.ds(pl.multiple_of(row * TILE, TILE), TILE)

    def fetch(n, spot):
        return pltpu.make_async_copy(blocks[n], panels.at[spot], panel_sems.at[spot])

    def load(row, spot):
        return pltpu.make_async_copy(front.at[place(row)], old.at[spot], in_sems.at[spot])

    def store(row, spot):
        return pltpu.make_async_copy(new.at[spot], out.at[place(row)], out_sems.at[spot])

    spot = jnp.int32(0)
    for n, number in enumerate(numbers):
        row = table[me[0], number]

        def begin(n=n, row=row, spot=spot):
            listed[spot] = row
            fetch(n, spot).start()
            pl.when(spot < 4)(lambda: load(row, spot).start())

        pl.when(row > 0)(begin)
        spot = spot + (row > 0).astype(jnp.int32)
    total = spot
    listed[total] = 0
    if start:
        here = pl.ds(0, TILE)
        top_in = pltpu.make_async_copy(front.at[here], new.at[room], in_sems.at[room])
        top_out = pltpu.make_async_copy(new.at[room], out.at[here], out_sems.at[room])
        top_in.start()
        top_in.wait()
        top_out.start()

    @pl.loop(0, (total + 1) // 2)
    def _(pair):
        first = 2 * pair
        both = first + 1 < total

        def ready(spot):
            fetch(0, spot).wait()
            load(0, spot).wait()

        for ahead in (first + 4, first + 5):
            pl.when(ahead < total)(lambda ahead=ahead: load(listed[ahead], ahead).start())
        ready(first)
        pl.when(both)(lambda: ready(first + 1))
        panel = panels[pl.ds(first, 2)].reshape(2 * TILE, 2 * TILE)
        for c in range(cols_dev):
            span = slice(c * TILE, (c + 1) * TILE)
            change = dot(panel, own[:, span])
            for h in (0, 1):
                keep = mask[listed[first + h], c] > 0
                part = jnp.where(keep, change[h * TILE : (h + 1) * TILE], 0.0)
                before = old[first + h, :, span].astype(jnp.float32)
                new[first + h, :, span] = (before - part).astype(jnp.bfloat16)

        @pl.when(me[0] == 0)
        def _():
            for h in (0, 1):
                new[first + h, :, :TILE] = panels[first + h, :, :TILE]

                @pl.when(listed[first + h] > 1)
                def _():
                    new[first + h, :, TILE : 2 * TILE] = panels[first + h, :, TILE:]

        store(listed[first], first).start()
        pl.when(both)(lambda: store(listed[first + 1], first + 1).start())

    @pl.loop(0, total)
    def _(spot):
        store(0, spot).wait()

    if start:
        top_out.wait()


def update(table, mask, me, own, front, numbers, blocks, room, base=None):
    width = front.shape[1]
    count = len(numbers)
    operands = [table, mask, me, own, in_hbm(front), *[in_hbm(block) for block in blocks]]
    in_specs = [SMEM, SMEM, SMEM, VMEM, HBM] + [HBM] * count
    aliases = {}
    if base is not None:
        aliases = {len(operands): 0}
        operands.append(in_hbm(base))
        in_specs.append(HBM)
    return pl.pallas_call(
        functools.partial(update_kernel, tuple(numbers), room, width // TILE, base is None),
        out_shape=jax.ShapeDtypeStruct(front.shape, jnp.bfloat16),
        in_specs=in_specs,
        out_specs=HBM,
        scratch_shapes=[
            pltpu.VMEM((room, TILE, 2 * TILE), jnp.bfloat16),
            pltpu.VMEM((room, TILE, width), jnp.bfloat16),
            pltpu.VMEM((room + 1, TILE, width), jnp.bfloat16),
            pltpu.SMEM((room + 1,), jnp.int32),
            pltpu.SemaphoreType.DMA((room,)),
            pltpu.SemaphoreType.DMA((room + 1,)),
            pltpu.SemaphoreType.DMA((room + 1,)),
        ],
        input_output_aliases=aliases,
        compiler_params=pltpu.CompilerParams(vmem_limit_bytes=UPDATE_LIMIT),
        cost_estimate=pl.CostEstimate(
            flops=2 * room * TILE * width * 2 * TILE, bytes_accessed=4 * room * TILE * width, transcendentals=0
        ),
        name="update",
    )(*operands)


def after(values, *others):
    return lax.optimization_barrier((tuple(values), others))[0]


def one_of(g, members):
    result = g == members[0]
    for member in members[1:]:
        result = result | (g == member)
    return result


def shards(front_in, panel_inverse, tile_mask, tile_map):
    front = front_in[0]
    width = front.shape[1]
    tiles = front.shape[0] // TILE
    cols_dev = width // TILE
    inverse = panel_inverse[0]
    mask = tile_mask[0]
    targets = tile_map[0, 0]
    contrib = targets.shape[0]
    rows_out = contrib // cols_dev
    n_grp = lax.axis_size("grp")
    n_dev = n_grp * lax.axis_size("front")
    slots_dev = n_grp // 2
    g = lax.axis_index("grp")
    me = jnp.reshape(g, (1,)).astype(jnp.int32)
    root = g == 0

    perms, rules = routes(n_grp)
    lists = stream_plan(perms, rules, n_grp, tiles, cols_dev, rows_out)
    got = travel(perms, rules, lists, n_grp, tiles)
    events = len(got)
    longest = max(len(lists[0]), len(lists[1]))

    order = [(e, lists[s][e]) for e in range(longest) for s in (0, 1) if e < len(lists[s])] + [(longest, 0)]
    cuts = [0, 4, 8] + list(range(16, len(order) - 2, 8)) + [len(order)]
    made, parts, where_made = [], None, {}

    def make(e, turn):
        nonlocal parts
        while len(made) < len(cuts) - 1:
            begin, end = cuts[len(made)], cuts[len(made) + 1]
            if order[begin][0] > max(0, e + 1 if begin < 8 else e + 2):
                break
            names = [tile for _, tile in order[begin:end]]
            for n, tile in enumerate(names):
                where_made[tile] = (len(made), n)
            if parts is None:
                *made_now, parts, one = factor(front, mask, names, inverse=inverse)
                parts = (parts, one)
            else:
                made_now = factor(front, mask, names, parts=after(parts, *turn))
            made.append(made_now)

    make(-2, ())
    odd = [[n for n in range(n_grp) if rules[s][n] != rules[s][0]] for s in (0, 1)]
    others = [one_of(g, odd[s]) if odd[s] else None for s in (0, 1)]
    scalars = [value for value in (root, *others) if value is not None]
    table = []
    for n in range(n_grp):
        line = []
        for now in got:
            for arrival in now:
                line.append(arrival[n] if n and arrival[n] not in line else 0)
        table.append(line)
    pairs = live_pairs(perms, rules, lists, got, table, n_grp)
    numbers_at = [[2 * e, 2 * e + 1] for e in range(events)]
    made_at = {}
    for e, tile in order[:-1]:
        made_at[len(table[0])] = tile
        numbers_at[e].append(len(table[0]))
        for n in range(n_grp):
            table[n].append(0 if n else tile)
    rows = jnp.asarray(table, jnp.int32)

    needed = [
        [n * cols_dev + c for c in range(cols_dev)] + [tiles - rows_out + r for r in range(rows_out)]
        for n in range(n_grp)
    ]
    ready = max(table[n].index(tile) // 2 for n in range(1, n_grp) for tile in needed[n])

    def own_part():
        blocks, names = [], {}

        def choice(tile, n):
            if n == 0:
                name = (-1, tile)
                which, place = where_made[tile]
                block = made[which][place]
            else:
                name = divmod(table[n].index(tile), 2)
                block = held[name[0]][name[1]]
            if name not in names:
                names[name] = len(blocks)
                blocks.append(block)
            return names[name]

        choices = [[choice(needed[n][part], n) for n in range(n_grp)] for part in range(cols_dev + rows_out)]
        return own_panels(mask, targets, me, front, blocks, choices, rows_out)

    piece = TILE // n_dev

    def exchange(blocks):
        return lax.all_to_all(blocks, ("front", "grp"), split_axis=0, concat_axis=0, tiled=True)

    def sums_of(arrived):
        digits = arrived[:, 0, 0, width : width + 2 * contrib].astype(jnp.int32).reshape(n_dev * contrib, 2)
        labels = digits[:, 0] * 32 + digits[:, 1]
        blocks = arrived[..., :width].reshape(n_dev, rows_out, piece, cols_dev, TILE)
        blocks = jnp.transpose(blocks, (0, 3, 1, 2, 4)).reshape(n_dev * contrib, piece * TILE)
        picker = labels[None, :] == jnp.arange(n_dev * slots_dev, dtype=jnp.int32)[:, None]
        sums = dot(picker.astype(jnp.bfloat16), blocks).astype(jnp.bfloat16)
        return sums.reshape(n_dev, slots_dev, piece, TILE)

    held, turn, result, done = [], (), None, 0

    def block_of(number):
        if number in made_at:
            which, place = where_made[made_at[number]]
            return made[which][place]
        return held[number // 2][number % 2]

    def step(count, *waits):
        nonlocal result, done
        numbers = [number for e in range(done, done + count) for number in numbers_at[e]]
        numbers = [number for number in numbers if any(line[number] for line in table)]
        done += count
        here = after((me,), *waits)[0]
        blocks = [block_of(number) for number in numbers]
        result = update(rows, mask, here, own, front, numbers, blocks, 2 * count, base=result)

    for e in range(events):
        values = []
        for s in (0, 1):
            value = None
            if e >= CHAINS:
                value = held[e - CHAINS][rules[s][0]]
                if others[s] is not None:
                    value = jnp.where(others[s], held[e - CHAINS][1 - rules[s][0]], value)
            if e < len(lists[s]):
                which, n = where_made[lists[s][e]]
                value = made[which][n] if value is None else jnp.where(root, made[which][n], value)
            values.append(value)
        turn = after(values, *turn, *(scalars if e == 0 else ()))
        held.append([lax.ppermute(turn[s], "grp", pairs[e][s]) if pairs[e][s] else turn[s] for s in (0, 1)])
        make(e, turn)
        if CHAINS <= e + 1 < events:
            held[e + 1 - CHAINS] = list(after(held[e + 1 - CHAINS], *turn))
        late = e - ready - CHAINS
        if late == 0:
            own, bottom = own_part()
            pieces = jnp.transpose(bottom.reshape(rows_out, n_dev, piece, width + 128), (1, 0, 2, 3))
        if late == 1:
            arrived = exchange(after((pieces,), *turn)[0])
        if late == SUM_AFTER:
            sums = sums_of(after((arrived,), *turn)[0])
            parent_pieces = exchange(sums)
            turn = (*turn, sums)
        elif late >= 2 and e < events - 2:
            step(min(4, e - CHAINS + 1 - done), *turn)
            turn = (*turn, result)
    parent_tiles = jnp.transpose(parent_pieces, (1, 0, 2, 3)).reshape(slots_dev, TILE, TILE).astype(jnp.float32)
    while done < events - CHAINS:
        step(min(6, events - CHAINS - done), *turn)
    step(CHAINS, parent_tiles)
    return (result[None], parent_tiles)


def solution(mesh):
    in_specs = (
        P("front", None, "grp"),
        P("front", None, None, None),
        P("front", None, "grp"),
        P("front", "grp", None),
    )
    out_specs = (P("front", None, "grp"), P(("front", "grp"), None, None))
    return jax.shard_map(shards, mesh=mesh, in_specs=in_specs, out_specs=out_specs, check_vma=False)
```

```python
import functools

import jax
import jax.numpy as jnp
from jax import lax
from jax.experimental import pallas as pl
from jax.experimental.pallas import tpu as pltpu
from jax.sharding import PartitionSpec as P

TILE = 256
CHAINS = 2
RELAY_AFTER = 3
LABEL_ROWS = 16
VMEM_LIMIT = 16 * 1024 * 1024
UPDATE_LIMIT = 32 * 1024 * 1024
HBM = pl.BlockSpec(memory_space=pltpu.HBM)
VMEM = pl.BlockSpec(memory_space=pltpu.VMEM)
SMEM = pl.BlockSpec(memory_space=pltpu.SMEM)


def ring_order(n_grp):
    depth = 4 if n_grp % 4 == 0 and n_grp >= 8 else 1
    width = n_grp // depth
    if depth == 1:
        return list(range(n_grp))
    order = [z * width for z in range(depth)]
    for number, z in enumerate(reversed(range(depth))):
        ys = range(1, width) if number % 2 == 0 else range(width - 1, 0, -1)
        order += [z * width + y for y in ys]
    return order


def routes(n_grp):
    if n_grp == 8:
        climb = [(g, (g + 2) % n_grp) for g in range(n_grp)]
        cross = [(g, g ^ 1) for g in range(n_grp)]
        rules = [[0] * n_grp, [0] * n_grp]
        rules[0][1] = rules[0][n_grp - 1] = rules[1][1] = 1
        return [climb, cross], rules
    cycle = ring_order(n_grp)
    ring = [(g, cycle[(d + 1) % n_grp]) for d, g in enumerate(cycle)]
    return [ring, [(b, a) for a, b in ring]], [[0] * n_grp, [1] * n_grp]


def travel(perms, rules, lists, n_grp, tiles):
    got = []
    missing = {(g, tile) for g in range(n_grp) for tile in range(1, tiles)}
    while missing:
        e = len(got)
        now = []
        for s in (0, 1):
            arrival = [0] * n_grp
            for g, target in perms[s]:
                if g == 0 and e < len(lists[s]):
                    arrival[target] = lists[s][e]
                elif e >= CHAINS:
                    arrival[target] = got[e - CHAINS][rules[s][g]][g]
            now.append(arrival)
            missing -= set(enumerate(arrival))
        got.append(now)
    return got


def delays(perms, rules, n_grp):
    result = [[None] * n_grp, [None] * n_grp]
    for s in (0, 1):
        lists = [[], []]
        lists[s] = [1]
        for e, now in enumerate(travel(perms, rules, lists, n_grp, 2)):
            for arrival in now:
                for g in range(n_grp):
                    if arrival[g] and result[s][g] is None:
                        result[s][g] = e
    return result


def stream_plan(perms, rules, n_grp, tiles, cols_dev, rows_out):
    hops = delays(perms, rules, n_grp)
    picks = [[], []]
    bottom = [tiles - 1 - r for r in range(rows_out)]
    heads = [bottom[0::2], bottom[1::2]]

    def shorter():
        return 0 if len(heads[0] + picks[0]) <= len(heads[1] + picks[1]) else 1

    rest = [(n // cols_dev, n) for n in range(1, tiles) if n not in bottom]
    for g, tile in rest:
        if g and hops[0][g] != hops[1][g]:
            picks[0 if hops[0][g] < hops[1][g] else 1].append((g, tile))
    for g, tile in rest:
        if g and hops[0][g] == hops[1][g]:
            picks[shorter()].append((g, tile))
    for s in (0, 1):
        picks[s].sort(key=lambda item: (-hops[s][item[0]], item[1]))
    for g, tile in rest:
        if g == 0:
            picks[shorter()].append((g, tile))
    return [heads[s] + [tile for _, tile in picks[s]] for s in (0, 1)]


def in_hbm(x):
    return pltpu.with_memory_space_constraint(x, pltpu.HBM)


def split2(x):
    hi = x.astype(jnp.bfloat16)
    return hi, (x - hi.astype(jnp.float32)).astype(jnp.bfloat16)


def dot(a, b):
    return jnp.dot(a, b, preferred_element_type=jnp.float32)


def factor_kernel(tiles, head, mask, front, *refs):
    count = len(tiles)
    if head:
        source, outs, rest = refs[0], refs[1 : count + 1], refs[count + 1 :]
        parts, one, blocks, sems, top, top_sem, inverse, inverse_sem = rest
        inverse_copy = pltpu.make_async_copy(source, inverse, inverse_sem)
        inverse_copy.start()
    else:
        parts, one, outs, (blocks, sems) = refs[0], refs[1], refs[2 : count + 2], refs[count + 2 :]
    copies = [
        pltpu.make_async_copy(
            front.at[pl.ds(tile * TILE, TILE), pl.ds(0, 2 * TILE)], blocks.at[n], sems.at[n]
        )
        for n, tile in enumerate(tiles)
    ]
    if head:
        top_copy = pltpu.make_async_copy(front.at[pl.ds(TILE, TILE), pl.ds(0, TILE)], top, top_sem)
        top_copy.start()
    for copy in copies:
        copy.start()

    def first_of(x):
        return (dot(x, parts[1]) + dot(x, parts[0])).astype(jnp.bfloat16)

    if head:
        inverse_copy.wait()
        for which in range(2):
            hi, low = split2(inverse[which].T)
            parts[2 * which] = hi
            parts[2 * which + 1] = low
        top_copy.wait()
        one[...] = first_of(top[...]).astype(jnp.float32).T.astype(jnp.bfloat16)
    for begin in range(0, len(tiles), 2):
        group = list(range(begin, min(begin + 2, len(tiles))))
        for n in group:
            copies[n].wait()
        firsts = first_of(jnp.concatenate([blocks[n, :, :TILE] for n in group], axis=0))
        updates = dot(firsts, one[...])
        works = []
        for place, n in enumerate(group):
            keep = mask[tiles[n] : tiles[n] + 1, 1:2] > 0
            update = updates[place * TILE : (place + 1) * TILE]
            works.append(blocks[n, :, TILE:].astype(jnp.float32) - jnp.where(keep, update, 0.0))
        high, low = split2(jnp.concatenate(works, axis=0))
        seconds = (dot(low, parts[2]) + dot(high, parts[3]) + dot(high, parts[2])).astype(jnp.bfloat16)
        for place, n in enumerate(group):
            span = slice(place * TILE, (place + 1) * TILE)
            empty = jnp.zeros((TILE, TILE), jnp.bfloat16)
            outs[n][:, :TILE] = firsts[span] if tiles[n] > 0 else empty
            outs[n][:, TILE:] = seconds[span] if tiles[n] > 1 else empty


def factor(front, mask, tiles, inverse=None, parts=None):
    head = parts is None
    count = len(tiles)
    out_shape = [jax.ShapeDtypeStruct((TILE, 2 * TILE), jnp.bfloat16)] * count
    scratch = [pltpu.VMEM((count, TILE, 2 * TILE), jnp.bfloat16), pltpu.SemaphoreType.DMA((count,))]
    if head:
        out_shape += [
            jax.ShapeDtypeStruct((4, TILE, TILE), jnp.bfloat16),
            jax.ShapeDtypeStruct((TILE, TILE), jnp.bfloat16),
        ]
        scratch += [pltpu.VMEM((TILE, TILE), jnp.bfloat16), pltpu.SemaphoreType.DMA(())]
        scratch += [pltpu.VMEM((2, TILE, TILE), jnp.float32), pltpu.SemaphoreType.DMA(())]
    operands = (in_hbm(inverse),) if head else parts
    return pl.pallas_call(
        functools.partial(factor_kernel, tuple(tiles), head),
        out_shape=out_shape,
        in_specs=[VMEM, HBM] + [HBM if head else VMEM] * len(operands),
        out_specs=[VMEM] * len(out_shape),
        scratch_shapes=scratch,
        compiler_params=pltpu.CompilerParams(vmem_limit_bytes=VMEM_LIMIT),
        cost_estimate=pl.CostEstimate(
            flops=12 * count * TILE**3, bytes_accessed=4 * count * TILE * 2 * TILE, transcendentals=0
        ),
        name="factor",
    )(mask, in_hbm(front), *operands)


def own_kernel(choices, sources, cols_dev, rows_out, span_front, mask, targets, me, front, *refs):
    blocks, (own, sends, panels, old, sems, old_sem) = refs[:sources], refs[sources:]
    tiles = front.shape[0] // TILE

    def copy(part, source):
        return pltpu.make_async_copy(blocks[source], panels.at[part], sems.at[part])

    old_copy = pltpu.make_async_copy(front.at[pl.ds((tiles - rows_out) * TILE, rows_out * TILE)], old, old_sem)
    old_copy.start()
    for part, options in enumerate(choices):
        for g, source in enumerate(options):
            pl.when(me[0] == g)(lambda part=part, source=source: copy(part, source).start())
    sends[...] = jnp.zeros_like(sends)
    lane = lax.broadcasted_iota(jnp.int32, (LABEL_ROWS, TILE), 1)
    count = cols_dev * rows_out
    labels = [targets[number] + 1 for number in range(count)]
    parents = [targets[number] // span_front for number in range(count)]
    ranks = [sum([(parents[m] == parents[n]).astype(jnp.int32) for m in range(n)], jnp.int32(0)) for n in range(count)]
    for parent in range(sends.shape[0]):
        digits = jnp.zeros((LABEL_ROWS, TILE), jnp.int32)
        for n in range(count):
            spot = jnp.where(parents[n] == parent, 2 * ranks[n], -2)
            digits = jnp.where(lane == spot, labels[n] // 32, digits)
            digits = jnp.where(lane == spot + 1, labels[n] % 32, digits)
        sends[parent, 2 * TILE :, :] = digits.astype(jnp.float32).astype(jnp.bfloat16)
    for part, options in enumerate(choices):
        copy(part, options[0]).wait()
    for c in range(cols_dev):
        own[:, c * TILE : (c + 1) * TILE] = panels[c].astype(jnp.float32).T.astype(jnp.bfloat16)
    old_copy.wait()
    for c in range(cols_dev):
        for r in range(rows_out):
            row, rows, panel = tiles - rows_out + r, slice(r * TILE, (r + 1) * TILE), panels.at[cols_dev + r]
            span = slice(c * TILE, (c + 1) * TILE)
            change = jnp.where(mask[row, c] > 0, dot(panel[...], own[:, span]), 0.0)
            tile = (old[rows, span].astype(jnp.float32) - change).astype(jnp.bfloat16)
            if c < 2:
                tile = jnp.where(me[0] == 0, panel[:, span], tile)
            number = c * rows_out + r
            place = pl.ds(pl.multiple_of(ranks[number] * TILE, TILE), TILE)
            sends[parents[number], place, :] = tile


def own_panels(mask, targets, me, front, blocks, choices, rows_out, n_front, span_front):
    width = front.shape[1]
    parts = len(choices)
    return pl.pallas_call(
        functools.partial(own_kernel, choices, len(blocks), width // TILE, rows_out, span_front),
        out_shape=[
            jax.ShapeDtypeStruct((2 * TILE, width), jnp.bfloat16),
            jax.ShapeDtypeStruct((n_front, 2 * TILE + LABEL_ROWS, TILE), jnp.bfloat16),
        ],
        in_specs=[SMEM, SMEM, SMEM, HBM] + [HBM] * len(blocks),
        out_specs=[VMEM, VMEM],
        scratch_shapes=[
            pltpu.VMEM((parts, TILE, 2 * TILE), jnp.bfloat16),
            pltpu.VMEM((rows_out * TILE, width), jnp.bfloat16),
            pltpu.SemaphoreType.DMA((parts,)),
            pltpu.SemaphoreType.DMA(()),
        ],
        compiler_params=pltpu.CompilerParams(vmem_limit_bytes=VMEM_LIMIT),
        cost_estimate=pl.CostEstimate(
            flops=2 * rows_out * TILE * width * 2 * TILE,
            bytes_accessed=4 * parts * TILE * 2 * TILE,
            transcendentals=0,
        ),
        name="own_panels",
    )(mask, targets, me, in_hbm(front), *[in_hbm(block) for block in blocks])


def relay_kernel(slots, labels, arrived, sends):
    n_grp = sends.shape[0]
    sends[...] = jnp.zeros_like(sends)
    for source in range(arrived.shape[0]):
        for rank in range(2):
            label = labels[source, rank]

            @pl.when(label > 0)
            def _():
                owner = (label - 1) // slots % n_grp
                slot = ((label - 1) % slots + 1).astype(jnp.float32)
                sends[owner, :TILE, :] = arrived[source, rank * TILE : (rank + 1) * TILE, :]
                sends[owner, TILE:, :] = jnp.full((LABEL_ROWS, TILE), slot, jnp.float32).astype(jnp.bfloat16)


def relay(labels, arrived, slots, n_grp):
    return pl.pallas_call(
        functools.partial(relay_kernel, slots),
        out_shape=jax.ShapeDtypeStruct((n_grp, TILE + LABEL_ROWS, TILE), jnp.bfloat16),
        in_specs=[SMEM, VMEM],
        out_specs=VMEM,
        compiler_params=pltpu.CompilerParams(vmem_limit_bytes=VMEM_LIMIT),
        cost_estimate=pl.CostEstimate(flops=0, bytes_accessed=4 * n_grp * TILE * TILE, transcendentals=0),
        name="relay",
    )(labels, arrived)


def sum_kernel(labels, arrived, out):
    out[...] = jnp.zeros_like(out)
    for source in range(arrived.shape[0]):
        label = labels[source]

        @pl.when(label > 0)
        def _():
            slot = label - 1
            out[slot] = out[slot] + arrived[source, :TILE, :].astype(jnp.float32)


def sum_parents(labels, arrived, slots):
    return pl.pallas_call(
        sum_kernel,
        out_shape=jax.ShapeDtypeStruct((slots, TILE, TILE), jnp.float32),
        in_specs=[SMEM, VMEM],
        out_specs=VMEM,
        compiler_params=pltpu.CompilerParams(vmem_limit_bytes=VMEM_LIMIT),
        cost_estimate=pl.CostEstimate(flops=0, bytes_accessed=8 * slots * TILE * TILE, transcendentals=0),
        name="sum_parents",
    )(labels, arrived)


def update_kernel(numbers, room, cols_dev, start, table, mask, me, own, front, *refs):
    count = len(numbers)
    blocks = refs[:count]
    out, panels, old, new, listed, panel_sems, in_sems, out_sems = refs[-8:]

    def place(row):
        return pl.ds(pl.multiple_of(row * TILE, TILE), TILE)

    def fetch(n, spot):
        return pltpu.make_async_copy(blocks[n], panels.at[spot], panel_sems.at[spot])

    def load(row, spot):
        return pltpu.make_async_copy(front.at[place(row)], old.at[spot], in_sems.at[spot])

    def store(row, spot):
        return pltpu.make_async_copy(new.at[spot], out.at[place(row)], out_sems.at[spot])

    spot = jnp.int32(0)
    for n, number in enumerate(numbers):
        row = table[me[0], number]

        def begin(n=n, row=row, spot=spot):
            listed[spot] = row
            fetch(n, spot).start()
            pl.when(spot < 4)(lambda: load(row, spot).start())

        pl.when(row > 0)(begin)
        spot = spot + (row > 0).astype(jnp.int32)
    total = spot
    listed[total] = 0
    if start:
        here = pl.ds(0, TILE)
        top_in = pltpu.make_async_copy(front.at[here], new.at[room], in_sems.at[room])
        top_out = pltpu.make_async_copy(new.at[room], out.at[here], out_sems.at[room])
        top_in.start()
        top_in.wait()
        top_out.start()

    @pl.loop(0, (total + 1) // 2)
    def _(pair):
        first = 2 * pair
        both = first + 1 < total

        def ready(spot):
            fetch(0, spot).wait()
            load(0, spot).wait()

        for ahead in (first + 4, first + 5):
            pl.when(ahead < total)(lambda ahead=ahead: load(listed[ahead], ahead).start())
        ready(first)
        pl.when(both)(lambda: ready(first + 1))
        panel = panels[pl.ds(first, 2)].reshape(2 * TILE, 2 * TILE)
        for c in range(cols_dev):
            span = slice(c * TILE, (c + 1) * TILE)
            change = dot(panel, own[:, span])
            for h in (0, 1):
                keep = mask[listed[first + h], c] > 0
                part = jnp.where(keep, change[h * TILE : (h + 1) * TILE], 0.0)
                before = old[first + h, :, span].astype(jnp.float32)
                new[first + h, :, span] = (before - part).astype(jnp.bfloat16)

        @pl.when(me[0] == 0)
        def _():
            for h in (0, 1):
                new[first + h, :, :TILE] = panels[first + h, :, :TILE]

                @pl.when(listed[first + h] > 1)
                def _():
                    new[first + h, :, TILE : 2 * TILE] = panels[first + h, :, TILE:]

        store(listed[first], first).start()
        pl.when(both)(lambda: store(listed[first + 1], first + 1).start())

    @pl.loop(0, total)
    def _(spot):
        store(0, spot).wait()

    if start:
        top_out.wait()


def update(table, mask, me, own, front, numbers, blocks, room, base=None):
    width = front.shape[1]
    count = len(numbers)
    operands = [table, mask, me, own, in_hbm(front), *[in_hbm(block) for block in blocks]]
    in_specs = [SMEM, SMEM, SMEM, VMEM, HBM] + [HBM] * count
    aliases = {}
    if base is not None:
        aliases = {len(operands): 0}
        operands.append(in_hbm(base))
        in_specs.append(HBM)
    return pl.pallas_call(
        functools.partial(update_kernel, tuple(numbers), room, width // TILE, base is None),
        out_shape=jax.ShapeDtypeStruct(front.shape, jnp.bfloat16),
        in_specs=in_specs,
        out_specs=HBM,
        scratch_shapes=[
            pltpu.VMEM((room, TILE, 2 * TILE), jnp.bfloat16),
            pltpu.VMEM((room, TILE, width), jnp.bfloat16),
            pltpu.VMEM((room + 1, TILE, width), jnp.bfloat16),
            pltpu.SMEM((room + 1,), jnp.int32),
            pltpu.SemaphoreType.DMA((room,)),
            pltpu.SemaphoreType.DMA((room + 1,)),
            pltpu.SemaphoreType.DMA((room + 1,)),
        ],
        input_output_aliases=aliases,
        compiler_params=pltpu.CompilerParams(vmem_limit_bytes=UPDATE_LIMIT),
        cost_estimate=pl.CostEstimate(
            flops=2 * room * TILE * width * 2 * TILE, bytes_accessed=4 * room * TILE * width, transcendentals=0
        ),
        name="update",
    )(*operands)


def after(values, *others):
    return lax.optimization_barrier((tuple(values), others))[0]


def one_of(g, members):
    result = g == members[0]
    for member in members[1:]:
        result = result | (g == member)
    return result


def shards(front_in, panel_inverse, tile_mask, tile_map):
    front = front_in[0]
    width = front.shape[1]
    tiles = front.shape[0] // TILE
    cols_dev = width // TILE
    inverse = panel_inverse[0]
    mask = tile_mask[0]
    targets = tile_map[0, 0]
    contrib = targets.shape[0]
    rows_out = contrib // cols_dev
    n_grp = lax.axis_size("grp")
    n_front = lax.axis_size("front")
    slots_dev = n_grp // 2
    g = lax.axis_index("grp")
    me = jnp.reshape(g, (1,)).astype(jnp.int32)
    root = g == 0

    perms, rules = routes(n_grp)
    lists = stream_plan(perms, rules, n_grp, tiles, cols_dev, rows_out)
    if n_grp == 8:
        lists[1] += lists[0][-2 * CHAINS :]
    got = travel(perms, rules, lists, n_grp, tiles)
    events = len(got)
    longest = max(len(lists[0]), len(lists[1]))

    order = [(e, lists[s][e]) for e in range(longest) for s in (0, 1) if e < len(lists[s])]
    order = [(e, tile) for n, (e, tile) in enumerate(order) if tile not in [other for _, other in order[:n]]]
    order.append((longest, 0))
    cuts = [0, 4, 8] + list(range(16, len(order) - 2, 8)) + [len(order)]
    made, parts, where_made = [], None, {}

    def make(e, turn):
        nonlocal parts
        while len(made) < len(cuts) - 1:
            begin, end = cuts[len(made)], cuts[len(made) + 1]
            if order[begin][0] > max(0, e + 1 if begin < 8 else e + 2):
                break
            names = [tile for _, tile in order[begin:end]]
            for n, tile in enumerate(names):
                where_made[tile] = (len(made), n)
            if parts is None:
                *made_now, parts, one = factor(front, mask, names, inverse=inverse)
                parts = (parts, one)
            else:
                made_now = factor(front, mask, names, parts=after(parts, *turn))
            made.append(made_now)

    make(-2, ())
    odd = [[n for n in range(n_grp) if rules[s][n] != rules[s][0]] for s in (0, 1)]
    others = [one_of(g, odd[s]) if odd[s] else None for s in (0, 1)]
    scalars = [value for value in (root, *others) if value is not None]
    table = []
    for n in range(n_grp):
        line = []
        for now in got:
            for arrival in now:
                line.append(arrival[n] if arrival[n] not in line else 0)
        table.append(line)
    rows = jnp.asarray(table, jnp.int32)
    used = [[any(line[2 * e + s] for line in table) for s in (0, 1)] for e in range(events)]
    for e in reversed(range(events - CHAINS)):
        for s in (0, 1):
            used[e][s] = used[e][s] or any(used[e + CHAINS])

    needed = [
        [n * cols_dev + c for c in range(cols_dev)] + [tiles - rows_out + r for r in range(rows_out)]
        for n in range(n_grp)
    ]
    ready = max(table[n].index(tile) // 2 for n in range(1, n_grp) for tile in needed[n])

    def own_part():
        blocks, names = [], {}

        def choice(tile, n):
            if n == 0:
                name = (-1, tile)
                which, place = where_made[tile]
                block = made[which][place]
            else:
                name = divmod(table[n].index(tile), 2)
                block = held[name[0]][name[1]]
            if name not in names:
                names[name] = len(blocks)
                blocks.append(block)
            return names[name]

        choices = [[choice(needed[n][part], n) for n in range(n_grp)] for part in range(cols_dev + rows_out)]
        return own_panels(mask, targets, me, front, blocks, choices, rows_out, n_front, n_grp * slots_dev)

    def exchange(blocks, axis):
        return lax.all_to_all(blocks, axis, split_axis=0, concat_axis=0, tiled=True)

    def relayed(arrived):
        digits = arrived[:, 2 * TILE, :4].astype(jnp.int32).reshape(n_front, 2, 2)
        return exchange(relay(digits[..., 0] * 32 + digits[..., 1], arrived, slots_dev, n_grp), "grp")

    held, turn, result, done = [], (), None, 0

    def step(count, *waits):
        nonlocal result, done
        numbers = [n for n in range(2 * done, 2 * (done + count)) if any(line[n] for line in table)]
        done += count
        here = after((me,), *waits)[0]
        blocks = [held[n // 2][n % 2] for n in numbers]
        result = update(rows, mask, here, own, front, numbers, blocks, 2 * count, base=result)

    for e in range(events):
        values = []
        for s in (0, 1):
            value = None
            if e >= CHAINS:
                value = held[e - CHAINS][rules[s][0]]
                if others[s] is not None:
                    value = jnp.where(others[s], held[e - CHAINS][1 - rules[s][0]], value)
            if e < len(lists[s]):
                which, n = where_made[lists[s][e]]
                value = made[which][n] if value is None else jnp.where(root, made[which][n], value)
            values.append(value)
        turn = after(values, *turn, *(scalars if e == 0 else ()))
        held.append([lax.ppermute(turn[s], "grp", perms[s]) if used[e][s] else turn[s] for s in (0, 1)])
        make(e, turn)
        if CHAINS <= e + 1 < events:
            held[e + 1 - CHAINS] = list(after(held[e + 1 - CHAINS], *turn))
        late = e - ready - CHAINS
        if late == 0:
            own, sends = own_part()
        if late == 1:
            arrived = exchange(after((sends,), *turn)[0], "front")
        if late == RELAY_AFTER:
            arrived = relayed(after((arrived,), *turn)[0])
        if late >= 2 and late != RELAY_AFTER and e < events - 1:
            step(min(4, e - CHAINS + 1 - done), *turn)
            turn = (*turn, result)
    while done < events - CHAINS:
        step(min(6, events - CHAINS - done), *turn)
    slots_here = after((arrived,), result)[0]
    parent_tiles = sum_parents(slots_here[:, TILE, 0].astype(jnp.int32), slots_here, slots_dev)
    step(CHAINS, parent_tiles)
    return (result[None], parent_tiles)


def solution(mesh):
    in_specs = (
        P("front", None, "grp"),
        P("front", None, None, None),
        P("front", None, "grp"),
        P("front", "grp", None),
    )
    out_specs = (P("front", None, "grp"), P(("front", "grp"), None, None))
    return jax.shard_map(shards, mesh=mesh, in_specs=in_specs, out_specs=out_specs, check_vma=False)
```

```python
import functools

import jax
import jax.numpy as jnp
from jax import lax
from jax.experimental import pallas as pl
from jax.experimental.pallas import tpu as pltpu
from jax.sharding import PartitionSpec as P

TILE = 256
CHAINS = 2
RELAY_AFTER = 6
LABEL_ROWS = 16
VMEM_LIMIT = 16 * 1024 * 1024
UPDATE_LIMIT = 32 * 1024 * 1024
HBM = pl.BlockSpec(memory_space=pltpu.HBM)
VMEM = pl.BlockSpec(memory_space=pltpu.VMEM)
SMEM = pl.BlockSpec(memory_space=pltpu.SMEM)


def ring_order(n_grp):
    depth = 4 if n_grp % 4 == 0 and n_grp >= 8 else 1
    width = n_grp // depth
    if depth == 1:
        return list(range(n_grp))
    order = [z * width for z in range(depth)]
    for number, z in enumerate(reversed(range(depth))):
        ys = range(1, width) if number % 2 == 0 else range(width - 1, 0, -1)
        order += [z * width + y for y in ys]
    return order


def routes(n_grp):
    if n_grp == 8:
        climb = [(g, (g + 2) % n_grp) for g in range(n_grp)]
        cross = [(g, g ^ 1) for g in range(n_grp)]
        rules = [[0] * n_grp, [0] * n_grp]
        rules[0][1] = rules[0][n_grp - 1] = rules[1][1] = 1
        return [climb, cross], rules
    cycle = ring_order(n_grp)
    ring = [(g, cycle[(d + 1) % n_grp]) for d, g in enumerate(cycle)]
    return [ring, [(b, a) for a, b in ring]], [[0] * n_grp, [1] * n_grp]


def travel(perms, rules, lists, n_grp, tiles):
    got = []
    missing = {(g, tile) for g in range(n_grp) for tile in range(1, tiles)}
    while missing:
        e = len(got)
        now = []
        for s in (0, 1):
            arrival = [0] * n_grp
            for g, target in perms[s]:
                if g == 0 and e < len(lists[s]):
                    arrival[target] = lists[s][e]
                elif e >= CHAINS:
                    arrival[target] = got[e - CHAINS][rules[s][g]][g]
            now.append(arrival)
            missing -= set(enumerate(arrival))
        got.append(now)
    return got


def delays(perms, rules, n_grp):
    result = [[None] * n_grp, [None] * n_grp]
    for s in (0, 1):
        lists = [[], []]
        lists[s] = [1]
        for e, now in enumerate(travel(perms, rules, lists, n_grp, 2)):
            for arrival in now:
                for g in range(n_grp):
                    if arrival[g] and result[s][g] is None:
                        result[s][g] = e
    return result


def stream_plan(perms, rules, n_grp, tiles, cols_dev, rows_out):
    hops = delays(perms, rules, n_grp)
    picks = [[], []]
    bottom = [tiles - 1 - r for r in range(rows_out)]
    heads = [bottom[0::2], bottom[1::2]]

    def shorter():
        return 0 if len(heads[0] + picks[0]) <= len(heads[1] + picks[1]) else 1

    rest = [(n // cols_dev, n) for n in range(1, tiles) if n not in bottom]
    for g, tile in rest:
        if g and hops[0][g] != hops[1][g]:
            picks[0 if hops[0][g] < hops[1][g] else 1].append((g, tile))
    for g, tile in rest:
        if g and hops[0][g] == hops[1][g]:
            picks[shorter()].append((g, tile))
    for s in (0, 1):
        picks[s].sort(key=lambda item: (-hops[s][item[0]], item[1]))
    for g, tile in rest:
        if g == 0:
            picks[shorter()].append((g, tile))
    return [heads[s] + [tile for _, tile in picks[s]] for s in (0, 1)]


def in_hbm(x):
    return pltpu.with_memory_space_constraint(x, pltpu.HBM)


def split2(x):
    hi = x.astype(jnp.bfloat16)
    return hi, (x - hi.astype(jnp.float32)).astype(jnp.bfloat16)


def dot(a, b):
    return jnp.dot(a, b, preferred_element_type=jnp.float32)


def factor_kernel(tiles, head, mask, front, *refs):
    count = len(tiles)
    if head:
        source, outs, rest = refs[0], refs[1 : count + 1], refs[count + 1 :]
        parts, one, blocks, sems, top, top_sem, inverse, inverse_sem = rest
        inverse_copy = pltpu.make_async_copy(source, inverse, inverse_sem)
        inverse_copy.start()
    else:
        parts, one, outs, (blocks, sems) = refs[0], refs[1], refs[2 : count + 2], refs[count + 2 :]
    copies = [
        pltpu.make_async_copy(
            front.at[pl.ds(tile * TILE, TILE), pl.ds(0, 2 * TILE)], blocks.at[n], sems.at[n]
        )
        for n, tile in enumerate(tiles)
    ]
    if head:
        top_copy = pltpu.make_async_copy(front.at[pl.ds(TILE, TILE), pl.ds(0, TILE)], top, top_sem)
        top_copy.start()
    for copy in copies:
        copy.start()

    def first_of(x):
        return (dot(x, parts[1]) + dot(x, parts[0])).astype(jnp.bfloat16)

    if head:
        inverse_copy.wait()
        for which in range(2):
            hi, low = split2(inverse[which].T)
            parts[2 * which] = hi
            parts[2 * which + 1] = low
        top_copy.wait()
        one[...] = first_of(top[...]).astype(jnp.float32).T.astype(jnp.bfloat16)
    for begin in range(0, len(tiles), 2):
        group = list(range(begin, min(begin + 2, len(tiles))))
        for n in group:
            copies[n].wait()
        firsts = first_of(jnp.concatenate([blocks[n, :, :TILE] for n in group], axis=0))
        updates = dot(firsts, one[...])
        works = []
        for place, n in enumerate(group):
            keep = mask[tiles[n] : tiles[n] + 1, 1:2] > 0
            update = updates[place * TILE : (place + 1) * TILE]
            works.append(blocks[n, :, TILE:].astype(jnp.float32) - jnp.where(keep, update, 0.0))
        high, low = split2(jnp.concatenate(works, axis=0))
        seconds = (dot(low, parts[2]) + dot(high, parts[3]) + dot(high, parts[2])).astype(jnp.bfloat16)
        for place, n in enumerate(group):
            span = slice(place * TILE, (place + 1) * TILE)
            empty = jnp.zeros((TILE, TILE), jnp.bfloat16)
            outs[n][:, :TILE] = firsts[span] if tiles[n] > 0 else empty
            outs[n][:, TILE:] = seconds[span] if tiles[n] > 1 else empty


def factor(front, mask, tiles, inverse=None, parts=None):
    head = parts is None
    count = len(tiles)
    out_shape = [jax.ShapeDtypeStruct((TILE, 2 * TILE), jnp.bfloat16)] * count
    scratch = [pltpu.VMEM((count, TILE, 2 * TILE), jnp.bfloat16), pltpu.SemaphoreType.DMA((count,))]
    if head:
        out_shape += [
            jax.ShapeDtypeStruct((4, TILE, TILE), jnp.bfloat16),
            jax.ShapeDtypeStruct((TILE, TILE), jnp.bfloat16),
        ]
        scratch += [pltpu.VMEM((TILE, TILE), jnp.bfloat16), pltpu.SemaphoreType.DMA(())]
        scratch += [pltpu.VMEM((2, TILE, TILE), jnp.float32), pltpu.SemaphoreType.DMA(())]
    operands = (in_hbm(inverse),) if head else parts
    return pl.pallas_call(
        functools.partial(factor_kernel, tuple(tiles), head),
        out_shape=out_shape,
        in_specs=[VMEM, HBM] + [HBM if head else VMEM] * len(operands),
        out_specs=[VMEM] * len(out_shape),
        scratch_shapes=scratch,
        compiler_params=pltpu.CompilerParams(vmem_limit_bytes=VMEM_LIMIT),
        cost_estimate=pl.CostEstimate(
            flops=12 * count * TILE**3, bytes_accessed=4 * count * TILE * 2 * TILE, transcendentals=0
        ),
        name="factor",
    )(mask, in_hbm(front), *operands)


def own_kernel(choices, sources, cols_dev, rows_out, span_front, mask, targets, me, front, *refs):
    blocks, (own, sends, panels, old, sems, old_sem) = refs[:sources], refs[sources:]
    tiles = front.shape[0] // TILE

    def copy(part, source):
        return pltpu.make_async_copy(blocks[source], panels.at[part], sems.at[part])

    old_copy = pltpu.make_async_copy(front.at[pl.ds((tiles - rows_out) * TILE, rows_out * TILE)], old, old_sem)
    old_copy.start()
    for part, options in enumerate(choices):
        for g, source in enumerate(options):
            pl.when(me[0] == g)(lambda part=part, source=source: copy(part, source).start())
    sends[...] = jnp.zeros_like(sends)
    lane = lax.broadcasted_iota(jnp.int32, (LABEL_ROWS, TILE), 1)
    count = cols_dev * rows_out
    labels = [targets[number] + 1 for number in range(count)]
    parents = [targets[number] // span_front for number in range(count)]
    ranks = [sum([(parents[m] == parents[n]).astype(jnp.int32) for m in range(n)], jnp.int32(0)) for n in range(count)]
    for parent in range(sends.shape[0]):
        digits = jnp.zeros((LABEL_ROWS, TILE), jnp.int32)
        for n in range(count):
            spot = jnp.where(parents[n] == parent, 2 * ranks[n], -2)
            digits = jnp.where(lane == spot, labels[n] // 32, digits)
            digits = jnp.where(lane == spot + 1, labels[n] % 32, digits)
        sends[parent, 2 * TILE :, :] = digits.astype(jnp.float32).astype(jnp.bfloat16)
    for part, options in enumerate(choices):
        copy(part, options[0]).wait()
    for c in range(cols_dev):
        own[:, c * TILE : (c + 1) * TILE] = panels[c].astype(jnp.float32).T.astype(jnp.bfloat16)
    old_copy.wait()
    for c in range(cols_dev):
        for r in range(rows_out):
            row, rows, panel = tiles - rows_out + r, slice(r * TILE, (r + 1) * TILE), panels.at[cols_dev + r]
            span = slice(c * TILE, (c + 1) * TILE)
            change = jnp.where(mask[row, c] > 0, dot(panel[...], own[:, span]), 0.0)
            tile = (old[rows, span].astype(jnp.float32) - change).astype(jnp.bfloat16)
            if c < 2:
                tile = jnp.where(me[0] == 0, panel[:, span], tile)
            number = c * rows_out + r
            place = pl.ds(pl.multiple_of(ranks[number] * TILE, TILE), TILE)
            sends[parents[number], place, :] = tile


def own_panels(mask, targets, me, front, blocks, choices, rows_out, n_front, span_front):
    width = front.shape[1]
    parts = len(choices)
    return pl.pallas_call(
        functools.partial(own_kernel, choices, len(blocks), width // TILE, rows_out, span_front),
        out_shape=[
            jax.ShapeDtypeStruct((2 * TILE, width), jnp.bfloat16),
            jax.ShapeDtypeStruct((n_front, 2 * TILE + LABEL_ROWS, TILE), jnp.bfloat16),
        ],
        in_specs=[SMEM, SMEM, SMEM, HBM] + [HBM] * len(blocks),
        out_specs=[VMEM, VMEM],
        scratch_shapes=[
            pltpu.VMEM((parts, TILE, 2 * TILE), jnp.bfloat16),
            pltpu.VMEM((rows_out * TILE, width), jnp.bfloat16),
            pltpu.SemaphoreType.DMA((parts,)),
            pltpu.SemaphoreType.DMA(()),
        ],
        compiler_params=pltpu.CompilerParams(vmem_limit_bytes=VMEM_LIMIT),
        cost_estimate=pl.CostEstimate(
            flops=2 * rows_out * TILE * width * 2 * TILE,
            bytes_accessed=4 * parts * TILE * 2 * TILE,
            transcendentals=0,
        ),
        name="own_panels",
    )(mask, targets, me, in_hbm(front), *[in_hbm(block) for block in blocks])


def relay_kernel(slots, labels, arrived, sends):
    n_grp = sends.shape[0]
    sends[...] = jnp.zeros_like(sends)
    for source in range(arrived.shape[0]):
        for rank in range(2):
            label = labels[source, rank]

            @pl.when(label > 0)
            def _():
                owner = (label - 1) // slots % n_grp
                slot = ((label - 1) % slots + 1).astype(jnp.float32)
                sends[owner, :TILE, :] = arrived[source, rank * TILE : (rank + 1) * TILE, :]
                sends[owner, TILE:, :] = jnp.full((LABEL_ROWS, TILE), slot, jnp.float32).astype(jnp.bfloat16)


def relay(labels, arrived, slots, n_grp):
    return pl.pallas_call(
        functools.partial(relay_kernel, slots),
        out_shape=jax.ShapeDtypeStruct((n_grp, TILE + LABEL_ROWS, TILE), jnp.bfloat16),
        in_specs=[SMEM, VMEM],
        out_specs=VMEM,
        compiler_params=pltpu.CompilerParams(vmem_limit_bytes=VMEM_LIMIT),
        cost_estimate=pl.CostEstimate(flops=0, bytes_accessed=4 * n_grp * TILE * TILE, transcendentals=0),
        name="relay",
    )(labels, arrived)


def sum_kernel(labels, arrived, out):
    out[...] = jnp.zeros_like(out)
    for source in range(arrived.shape[0]):
        label = labels[source]

        @pl.when(label > 0)
        def _():
            slot = label - 1
            out[slot] = out[slot] + arrived[source, :TILE, :].astype(jnp.float32)


def sum_parents(labels, arrived, slots):
    return pl.pallas_call(
        sum_kernel,
        out_shape=jax.ShapeDtypeStruct((slots, TILE, TILE), jnp.float32),
        in_specs=[SMEM, VMEM],
        out_specs=VMEM,
        compiler_params=pltpu.CompilerParams(vmem_limit_bytes=VMEM_LIMIT),
        cost_estimate=pl.CostEstimate(flops=0, bytes_accessed=8 * slots * TILE * TILE, transcendentals=0),
        name="sum_parents",
    )(labels, arrived)


def update_kernel(numbers, room, cols_dev, start, table, mask, me, own, front, *refs):
    count = len(numbers)
    blocks = refs[:count]
    out, panels, old, new, listed, panel_sems, in_sems, out_sems = refs[-8:]

    def place(row):
        return pl.ds(pl.multiple_of(row * TILE, TILE), TILE)

    def fetch(n, spot):
        return pltpu.make_async_copy(blocks[n], panels.at[spot], panel_sems.at[spot])

    def load(row, spot):
        return pltpu.make_async_copy(front.at[place(row)], old.at[spot], in_sems.at[spot])

    def store(row, spot):
        return pltpu.make_async_copy(new.at[spot], out.at[place(row)], out_sems.at[spot])

    spot = jnp.int32(0)
    for n, number in enumerate(numbers):
        row = table[me[0], number]

        def begin(n=n, row=row, spot=spot):
            listed[spot] = row
            fetch(n, spot).start()
            pl.when(spot < 4)(lambda: load(row, spot).start())

        pl.when(row > 0)(begin)
        spot = spot + (row > 0).astype(jnp.int32)
    total = spot
    listed[total] = 0
    if start:
        here = pl.ds(0, TILE)
        top_in = pltpu.make_async_copy(front.at[here], new.at[room], in_sems.at[room])
        top_out = pltpu.make_async_copy(new.at[room], out.at[here], out_sems.at[room])
        top_in.start()
        top_in.wait()
        top_out.start()

    @pl.loop(0, (total + 1) // 2)
    def _(pair):
        first = 2 * pair
        both = first + 1 < total

        def ready(spot):
            fetch(0, spot).wait()
            load(0, spot).wait()

        for ahead in (first + 4, first + 5):
            pl.when(ahead < total)(lambda ahead=ahead: load(listed[ahead], ahead).start())
        ready(first)
        pl.when(both)(lambda: ready(first + 1))
        panel = panels[pl.ds(first, 2)].reshape(2 * TILE, 2 * TILE)
        for c in range(cols_dev):
            span = slice(c * TILE, (c + 1) * TILE)
            change = dot(panel, own[:, span])
            for h in (0, 1):
                keep = mask[listed[first + h], c] > 0
                part = jnp.where(keep, change[h * TILE : (h + 1) * TILE], 0.0)
                before = old[first + h, :, span].astype(jnp.float32)
                new[first + h, :, span] = (before - part).astype(jnp.bfloat16)

        @pl.when(me[0] == 0)
        def _():
            for h in (0, 1):
                new[first + h, :, :TILE] = panels[first + h, :, :TILE]

                @pl.when(listed[first + h] > 1)
                def _():
                    new[first + h, :, TILE : 2 * TILE] = panels[first + h, :, TILE:]

        store(listed[first], first).start()
        pl.when(both)(lambda: store(listed[first + 1], first + 1).start())

    @pl.loop(0, total)
    def _(spot):
        store(0, spot).wait()

    if start:
        top_out.wait()


def update(table, mask, me, own, front, numbers, blocks, room, base=None):
    width = front.shape[1]
    count = len(numbers)
    operands = [table, mask, me, own, in_hbm(front), *[in_hbm(block) for block in blocks]]
    in_specs = [SMEM, SMEM, SMEM, VMEM, HBM] + [HBM] * count
    aliases = {}
    if base is not None:
        aliases = {len(operands): 0}
        operands.append(in_hbm(base))
        in_specs.append(HBM)
    return pl.pallas_call(
        functools.partial(update_kernel, tuple(numbers), room, width // TILE, base is None),
        out_shape=jax.ShapeDtypeStruct(front.shape, jnp.bfloat16),
        in_specs=in_specs,
        out_specs=HBM,
        scratch_shapes=[
            pltpu.VMEM((room, TILE, 2 * TILE), jnp.bfloat16),
            pltpu.VMEM((room, TILE, width), jnp.bfloat16),
            pltpu.VMEM((room + 1, TILE, width), jnp.bfloat16),
            pltpu.SMEM((room + 1,), jnp.int32),
            pltpu.SemaphoreType.DMA((room,)),
            pltpu.SemaphoreType.DMA((room + 1,)),
            pltpu.SemaphoreType.DMA((room + 1,)),
        ],
        input_output_aliases=aliases,
        compiler_params=pltpu.CompilerParams(vmem_limit_bytes=UPDATE_LIMIT),
        cost_estimate=pl.CostEstimate(
            flops=2 * room * TILE * width * 2 * TILE, bytes_accessed=4 * room * TILE * width, transcendentals=0
        ),
        name="update",
    )(*operands)


def after(values, *others):
    return lax.optimization_barrier((tuple(values), others))[0]


def one_of(g, members):
    result = g == members[0]
    for member in members[1:]:
        result = result | (g == member)
    return result


def shards(front_in, panel_inverse, tile_mask, tile_map):
    front = front_in[0]
    width = front.shape[1]
    tiles = front.shape[0] // TILE
    cols_dev = width // TILE
    inverse = panel_inverse[0]
    mask = tile_mask[0]
    targets = tile_map[0, 0]
    contrib = targets.shape[0]
    rows_out = contrib // cols_dev
    n_grp = lax.axis_size("grp")
    n_front = lax.axis_size("front")
    slots_dev = n_grp // 2
    g = lax.axis_index("grp")
    me = jnp.reshape(g, (1,)).astype(jnp.int32)
    root = g == 0

    perms, rules = routes(n_grp)
    lists = stream_plan(perms, rules, n_grp, tiles, cols_dev, rows_out)
    if n_grp == 8:
        lists[1] += lists[0][-2 * CHAINS :]
    got = travel(perms, rules, lists, n_grp, tiles)
    events = len(got)
    longest = max(len(lists[0]), len(lists[1]))

    order = [(e, lists[s][e]) for e in range(longest) for s in (0, 1) if e < len(lists[s])]
    order = [(e, tile) for n, (e, tile) in enumerate(order) if tile not in [other for _, other in order[:n]]]
    order.append((longest, 0))
    cuts = list(range(0, len(order) - 2, 4)) + [len(order)]
    made, parts, where_made = [], None, {}

    def make(e, turn):
        nonlocal parts
        while len(made) < len(cuts) - 1:
            begin, end = cuts[len(made)], cuts[len(made) + 1]
            if order[begin][0] > max(0, e + 1 if begin < 8 else e + 2):
                break
            names = [tile for _, tile in order[begin:end]]
            for n, tile in enumerate(names):
                where_made[tile] = (len(made), n)
            if parts is None:
                *made_now, parts, one = factor(front, mask, names, inverse=inverse)
                parts = (parts, one)
            else:
                made_now = factor(front, mask, names, parts=after(parts, *turn))
            made.append(made_now)

    make(-2, ())
    odd = [[n for n in range(n_grp) if rules[s][n] != rules[s][0]] for s in (0, 1)]
    others = [one_of(g, odd[s]) if odd[s] else None for s in (0, 1)]
    scalars = [value for value in (root, *others) if value is not None]
    table = []
    for n in range(n_grp):
        line = []
        for now in got:
            for arrival in now:
                line.append(arrival[n] if arrival[n] not in line else 0)
        table.append(line)
    rows = jnp.asarray(table, jnp.int32)
    used = [[any(line[2 * e + s] for line in table) for s in (0, 1)] for e in range(events)]
    for e in reversed(range(events - CHAINS)):
        for s in (0, 1):
            used[e][s] = used[e][s] or any(used[e + CHAINS])

    needed = [
        [n * cols_dev + c for c in range(cols_dev)] + [tiles - rows_out + r for r in range(rows_out)]
        for n in range(n_grp)
    ]
    ready = max(table[n].index(tile) // 2 for n in range(1, n_grp) for tile in needed[n])

    def own_part():
        blocks, names = [], {}

        def choice(tile, n):
            if n == 0:
                name = (-1, tile)
                which, place = where_made[tile]
                block = made[which][place]
            else:
                name = divmod(table[n].index(tile), 2)
                block = held[name[0]][name[1]]
            if name not in names:
                names[name] = len(blocks)
                blocks.append(block)
            return names[name]

        choices = [[choice(needed[n][part], n) for n in range(n_grp)] for part in range(cols_dev + rows_out)]
        return own_panels(mask, targets, me, front, blocks, choices, rows_out, n_front, n_grp * slots_dev)

    def exchange(blocks, axis):
        return lax.all_to_all(blocks, axis, split_axis=0, concat_axis=0, tiled=True)

    def relayed(arrived):
        digits = arrived[:, 2 * TILE, :4].astype(jnp.int32).reshape(n_front, 2, 2)
        return exchange(relay(digits[..., 0] * 32 + digits[..., 1], arrived, slots_dev, n_grp), "grp")

    held, turn, result, done = [], (), None, 0

    def step(count, *waits):
        nonlocal result, done
        numbers = [n for n in range(2 * done, 2 * (done + count)) if any(line[n] for line in table)]
        done += count
        here = after((me,), *waits)[0] if waits else me
        blocks = [held[n // 2][n % 2] for n in numbers]
        result = update(rows, mask, here, own, front, numbers, blocks, 2 * count, base=result)

    relay_after = min(RELAY_AFTER, events - 1 - ready - CHAINS)
    for e in range(events):
        values = []
        for s in (0, 1):
            value = None
            if e >= CHAINS:
                value = held[e - CHAINS][rules[s][0]]
                if others[s] is not None:
                    value = jnp.where(others[s], held[e - CHAINS][1 - rules[s][0]], value)
            if e < len(lists[s]):
                which, n = where_made[lists[s][e]]
                value = made[which][n] if value is None else jnp.where(root, made[which][n], value)
            values.append(value)
        turn = after(values, *turn, *(scalars if e == 0 else ()))
        held.append([lax.ppermute(turn[s], "grp", perms[s]) if used[e][s] else turn[s] for s in (0, 1)])
        make(e, turn)
        if CHAINS <= e + 1 < events:
            held[e + 1 - CHAINS] = list(after(held[e + 1 - CHAINS], *turn))
        late = e - ready - CHAINS
        if late == 0:
            own, sends = own_part()
        if late == 1:
            arrived = exchange(after((sends,), *turn)[0], "front")
        if late == relay_after:
            arrived = relayed(after((arrived,), *turn)[0])
        elif late >= 2 and late % 2 == 0 and e < events - 1:
            step(min(8, e - CHAINS + 1 - done), *turn)
            turn = (*turn, result)
    while done < events - CHAINS:
        step(min(8, events - CHAINS - done), *turn)
    step(CHAINS)
    slots_here = after((arrived,), result)[0]
    parent_tiles = sum_parents(slots_here[:, TILE, 0].astype(jnp.int32), slots_here, slots_dev)
    return (result[None], parent_tiles)


def solution(mesh):
    in_specs = (
        P("front", None, "grp"),
        P("front", None, None, None),
        P("front", None, "grp"),
        P("front", "grp", None),
    )
    out_specs = (P("front", None, "grp"), P(("front", "grp"), None, None))
    return jax.shard_map(shards, mesh=mesh, in_specs=in_specs, out_specs=out_specs, check_vma=False)
```

```python
import functools

import jax
import jax.numpy as jnp
from jax import lax
from jax.experimental import pallas as pl
from jax.experimental.pallas import tpu as pltpu
from jax.sharding import PartitionSpec as P

TILE = 256
CHAINS = 2
RELAY_AFTER = 7
LABEL_ROWS = 16
VMEM_LIMIT = 16 * 1024 * 1024
UPDATE_LIMIT = 32 * 1024 * 1024
HBM = pl.BlockSpec(memory_space=pltpu.HBM)
VMEM = pl.BlockSpec(memory_space=pltpu.VMEM)
SMEM = pl.BlockSpec(memory_space=pltpu.SMEM)


def ring_order(n_grp):
    depth = 4 if n_grp % 4 == 0 and n_grp >= 8 else 1
    width = n_grp // depth
    if depth == 1:
        return list(range(n_grp))
    order = [z * width for z in range(depth)]
    for number, z in enumerate(reversed(range(depth))):
        ys = range(1, width) if number % 2 == 0 else range(width - 1, 0, -1)
        order += [z * width + y for y in ys]
    return order


def routes(n_grp):
    if n_grp == 8:
        climb = [(g, (g + 2) % n_grp) for g in range(n_grp)]
        cross = [(g, g ^ 1) for g in range(n_grp)]
        rules = [[0] * n_grp, [0] * n_grp]
        rules[0][1] = rules[0][n_grp - 1] = rules[1][1] = 1
        return [climb, cross], rules
    cycle = ring_order(n_grp)
    ring = [(g, cycle[(d + 1) % n_grp]) for d, g in enumerate(cycle)]
    return [ring, [(b, a) for a, b in ring]], [[0] * n_grp, [1] * n_grp]


def travel(perms, rules, lists, n_grp, tiles):
    got = []
    missing = {(g, tile) for g in range(n_grp) for tile in range(1, tiles)}
    while missing:
        e = len(got)
        now = []
        for s in (0, 1):
            arrival = [0] * n_grp
            for g, target in perms[s]:
                if g == 0 and e < len(lists[s]):
                    arrival[target] = lists[s][e]
                elif e >= CHAINS:
                    arrival[target] = got[e - CHAINS][rules[s][g]][g]
            now.append(arrival)
            missing -= set(enumerate(arrival))
        got.append(now)
    return got


def delays(perms, rules, n_grp):
    result = [[None] * n_grp, [None] * n_grp]
    for s in (0, 1):
        lists = [[], []]
        lists[s] = [1]
        for e, now in enumerate(travel(perms, rules, lists, n_grp, 2)):
            for arrival in now:
                for g in range(n_grp):
                    if arrival[g] and result[s][g] is None:
                        result[s][g] = e
    return result


def stream_plan(perms, rules, n_grp, tiles, cols_dev, rows_out):
    hops = delays(perms, rules, n_grp)
    picks = [[], []]
    bottom = [tiles - 1 - r for r in range(rows_out)]
    heads = [bottom[0::2], bottom[1::2]]

    def shorter():
        return 0 if len(heads[0] + picks[0]) <= len(heads[1] + picks[1]) else 1

    rest = [(n // cols_dev, n) for n in range(1, tiles) if n not in bottom]
    for g, tile in rest:
        if g and hops[0][g] != hops[1][g]:
            picks[0 if hops[0][g] < hops[1][g] else 1].append((g, tile))
    for g, tile in rest:
        if g and hops[0][g] == hops[1][g]:
            picks[shorter()].append((g, tile))
    for s in (0, 1):
        picks[s].sort(key=lambda item: (-hops[s][item[0]], item[1]))
    for g, tile in rest:
        if g == 0:
            picks[shorter()].append((g, tile))
    return [heads[s] + [tile for _, tile in picks[s]] for s in (0, 1)]


def in_hbm(x):
    return pltpu.with_memory_space_constraint(x, pltpu.HBM)


def split2(x):
    hi = x.astype(jnp.bfloat16)
    return hi, (x - hi.astype(jnp.float32)).astype(jnp.bfloat16)


def dot(a, b):
    return jnp.dot(a, b, preferred_element_type=jnp.float32)


def factor_kernel(tiles, head, mask, front, *refs):
    count = len(tiles)
    if head:
        source, outs, rest = refs[0], refs[1 : count + 1], refs[count + 1 :]
        parts, one, blocks, sems, top, top_sem, inverse, inverse_sem = rest
        inverse_copy = pltpu.make_async_copy(source, inverse, inverse_sem)
        inverse_copy.start()
    else:
        parts, one, outs, (blocks, sems) = refs[0], refs[1], refs[2 : count + 2], refs[count + 2 :]
    copies = [
        pltpu.make_async_copy(
            front.at[pl.ds(tile * TILE, TILE), pl.ds(0, 2 * TILE)], blocks.at[n], sems.at[n]
        )
        for n, tile in enumerate(tiles)
    ]
    if head:
        top_copy = pltpu.make_async_copy(front.at[pl.ds(TILE, TILE), pl.ds(0, TILE)], top, top_sem)
        top_copy.start()
    for copy in copies:
        copy.start()

    def first_of(x):
        return (dot(x, parts[1]) + dot(x, parts[0])).astype(jnp.bfloat16)

    if head:
        inverse_copy.wait()
        for which in range(2):
            hi, low = split2(inverse[which].T)
            parts[2 * which] = hi
            parts[2 * which + 1] = low
        top_copy.wait()
        one[...] = first_of(top[...]).astype(jnp.float32).T.astype(jnp.bfloat16)
    for begin in range(0, len(tiles), 2):
        group = list(range(begin, min(begin + 2, len(tiles))))
        for n in group:
            copies[n].wait()
        firsts = first_of(jnp.concatenate([blocks[n, :, :TILE] for n in group], axis=0))
        updates = dot(firsts, one[...])
        works = []
        for place, n in enumerate(group):
            keep = mask[tiles[n] : tiles[n] + 1, 1:2] > 0
            update = updates[place * TILE : (place + 1) * TILE]
            works.append(blocks[n, :, TILE:].astype(jnp.float32) - jnp.where(keep, update, 0.0))
        high, low = split2(jnp.concatenate(works, axis=0))
        seconds = (dot(low, parts[2]) + dot(high, parts[3]) + dot(high, parts[2])).astype(jnp.bfloat16)
        for place, n in enumerate(group):
            span = slice(place * TILE, (place + 1) * TILE)
            empty = jnp.zeros((TILE, TILE), jnp.bfloat16)
            outs[n][:, :TILE] = firsts[span] if tiles[n] > 0 else empty
            outs[n][:, TILE:] = seconds[span] if tiles[n] > 1 else empty


def factor(front, mask, tiles, inverse=None, parts=None):
    head = parts is None
    count = len(tiles)
    out_shape = [jax.ShapeDtypeStruct((TILE, 2 * TILE), jnp.bfloat16)] * count
    scratch = [pltpu.VMEM((count, TILE, 2 * TILE), jnp.bfloat16), pltpu.SemaphoreType.DMA((count,))]
    if head:
        out_shape += [
            jax.ShapeDtypeStruct((4, TILE, TILE), jnp.bfloat16),
            jax.ShapeDtypeStruct((TILE, TILE), jnp.bfloat16),
        ]
        scratch += [pltpu.VMEM((TILE, TILE), jnp.bfloat16), pltpu.SemaphoreType.DMA(())]
        scratch += [pltpu.VMEM((2, TILE, TILE), jnp.float32), pltpu.SemaphoreType.DMA(())]
    operands = (in_hbm(inverse),) if head else parts
    return pl.pallas_call(
        functools.partial(factor_kernel, tuple(tiles), head),
        out_shape=out_shape,
        in_specs=[VMEM, HBM] + [HBM if head else VMEM] * len(operands),
        out_specs=[VMEM] * len(out_shape),
        scratch_shapes=scratch,
        compiler_params=pltpu.CompilerParams(vmem_limit_bytes=VMEM_LIMIT),
        cost_estimate=pl.CostEstimate(
            flops=12 * count * TILE**3, bytes_accessed=4 * count * TILE * 2 * TILE, transcendentals=0
        ),
        name="factor",
    )(mask, in_hbm(front), *operands)


def own_kernel(choices, sources, cols_dev, rows_out, span_front, mask, targets, me, front, *refs):
    blocks, (own, sends, panels, old, sems, old_sem) = refs[:sources], refs[sources:]
    tiles = front.shape[0] // TILE

    def copy(part, source):
        return pltpu.make_async_copy(blocks[source], panels.at[part], sems.at[part])

    old_copy = pltpu.make_async_copy(front.at[pl.ds((tiles - rows_out) * TILE, rows_out * TILE)], old, old_sem)
    old_copy.start()
    for part, options in enumerate(choices):
        for g, source in enumerate(options):
            pl.when(me[0] == g)(lambda part=part, source=source: copy(part, source).start())
    sends[...] = jnp.zeros_like(sends)
    lane = lax.broadcasted_iota(jnp.int32, (LABEL_ROWS, TILE), 1)
    count = cols_dev * rows_out
    labels = [targets[number] + 1 for number in range(count)]
    parents = [targets[number] // span_front for number in range(count)]
    ranks = [sum([(parents[m] == parents[n]).astype(jnp.int32) for m in range(n)], jnp.int32(0)) for n in range(count)]
    for parent in range(sends.shape[0]):
        digits = jnp.zeros((LABEL_ROWS, TILE), jnp.int32)
        for n in range(count):
            spot = jnp.where(parents[n] == parent, 2 * ranks[n], -2)
            digits = jnp.where(lane == spot, labels[n] // 32, digits)
            digits = jnp.where(lane == spot + 1, labels[n] % 32, digits)
        sends[parent, 2 * TILE :, :] = digits.astype(jnp.float32).astype(jnp.bfloat16)
    for part, options in enumerate(choices):
        copy(part, options[0]).wait()
    for c in range(cols_dev):
        own[:, c * TILE : (c + 1) * TILE] = panels[c].astype(jnp.float32).T.astype(jnp.bfloat16)
    old_copy.wait()
    for c in range(cols_dev):
        for r in range(rows_out):
            row, rows, panel = tiles - rows_out + r, slice(r * TILE, (r + 1) * TILE), panels.at[cols_dev + r]
            span = slice(c * TILE, (c + 1) * TILE)
            change = jnp.where(mask[row, c] > 0, dot(panel[...], own[:, span]), 0.0)
            tile = (old[rows, span].astype(jnp.float32) - change).astype(jnp.bfloat16)
            if c < 2:
                tile = jnp.where(me[0] == 0, panel[:, span], tile)
            number = c * rows_out + r
            place = pl.ds(pl.multiple_of(ranks[number] * TILE, TILE), TILE)
            sends[parents[number], place, :] = tile


def own_panels(mask, targets, me, front, blocks, choices, rows_out, n_front, span_front):
    width = front.shape[1]
    parts = len(choices)
    return pl.pallas_call(
        functools.partial(own_kernel, choices, len(blocks), width // TILE, rows_out, span_front),
        out_shape=[
            jax.ShapeDtypeStruct((2 * TILE, width), jnp.bfloat16),
            jax.ShapeDtypeStruct((n_front, 2 * TILE + LABEL_ROWS, TILE), jnp.bfloat16),
        ],
        in_specs=[SMEM, SMEM, SMEM, HBM] + [HBM] * len(blocks),
        out_specs=[VMEM, VMEM],
        scratch_shapes=[
            pltpu.VMEM((parts, TILE, 2 * TILE), jnp.bfloat16),
            pltpu.VMEM((rows_out * TILE, width), jnp.bfloat16),
            pltpu.SemaphoreType.DMA((parts,)),
            pltpu.SemaphoreType.DMA(()),
        ],
        compiler_params=pltpu.CompilerParams(vmem_limit_bytes=VMEM_LIMIT),
        cost_estimate=pl.CostEstimate(
            flops=2 * rows_out * TILE * width * 2 * TILE,
            bytes_accessed=4 * parts * TILE * 2 * TILE,
            transcendentals=0,
        ),
        name="own_panels",
    )(mask, targets, me, in_hbm(front), *[in_hbm(block) for block in blocks])


def relay_kernel(slots, labels, arrived, sends):
    n_grp = sends.shape[0]
    sends[...] = jnp.zeros_like(sends)
    for source in range(arrived.shape[0]):
        for rank in range(2):
            label = labels[source, rank]

            @pl.when(label > 0)
            def _():
                owner = (label - 1) // slots % n_grp
                slot = ((label - 1) % slots + 1).astype(jnp.float32)
                sends[owner, :TILE, :] = arrived[source, rank * TILE : (rank + 1) * TILE, :]
                sends[owner, TILE:, :] = jnp.full((LABEL_ROWS, TILE), slot, jnp.float32).astype(jnp.bfloat16)


def relay(labels, arrived, slots, n_grp):
    return pl.pallas_call(
        functools.partial(relay_kernel, slots),
        out_shape=jax.ShapeDtypeStruct((n_grp, TILE + LABEL_ROWS, TILE), jnp.bfloat16),
        in_specs=[SMEM, VMEM],
        out_specs=VMEM,
        compiler_params=pltpu.CompilerParams(vmem_limit_bytes=VMEM_LIMIT),
        cost_estimate=pl.CostEstimate(flops=0, bytes_accessed=4 * n_grp * TILE * TILE, transcendentals=0),
        name="relay",
    )(labels, arrived)


def sum_kernel(labels, arrived, out):
    out[...] = jnp.zeros_like(out)
    for source in range(arrived.shape[0]):
        label = labels[source]

        @pl.when(label > 0)
        def _():
            slot = label - 1
            out[slot] = out[slot] + arrived[source, :TILE, :].astype(jnp.float32)


def sum_parents(labels, arrived, slots):
    return pl.pallas_call(
        sum_kernel,
        out_shape=jax.ShapeDtypeStruct((slots, TILE, TILE), jnp.float32),
        in_specs=[SMEM, VMEM],
        out_specs=VMEM,
        compiler_params=pltpu.CompilerParams(vmem_limit_bytes=VMEM_LIMIT),
        cost_estimate=pl.CostEstimate(flops=0, bytes_accessed=8 * slots * TILE * TILE, transcendentals=0),
        name="sum_parents",
    )(labels, arrived)


def update_kernel(numbers, room, cols_dev, start, table, mask, me, own, front, *refs):
    count = len(numbers)
    blocks = refs[:count]
    out, panels, old, new, listed, panel_sems, in_sems, out_sems = refs[-8:]

    def place(row):
        return pl.ds(pl.multiple_of(row * TILE, TILE), TILE)

    def fetch(n, spot):
        return pltpu.make_async_copy(blocks[n], panels.at[spot], panel_sems.at[spot])

    def load(row, spot):
        return pltpu.make_async_copy(front.at[place(row)], old.at[spot], in_sems.at[spot])

    def store(row, spot):
        return pltpu.make_async_copy(new.at[spot], out.at[place(row)], out_sems.at[spot])

    spot = jnp.int32(0)
    for n, number in enumerate(numbers):
        row = table[me[0], number]

        def begin(n=n, row=row, spot=spot):
            listed[spot] = row
            fetch(n, spot).start()
            pl.when(spot < 4)(lambda: load(row, spot).start())

        pl.when(row > 0)(begin)
        spot = spot + (row > 0).astype(jnp.int32)
    total = spot
    listed[total] = 0
    if start:
        here = pl.ds(0, TILE)
        top_in = pltpu.make_async_copy(front.at[here], new.at[room], in_sems.at[room])
        top_out = pltpu.make_async_copy(new.at[room], out.at[here], out_sems.at[room])
        top_in.start()
        top_in.wait()
        top_out.start()

    @pl.loop(0, (total + 1) // 2)
    def _(pair):
        first = 2 * pair
        both = first + 1 < total

        def ready(spot):
            fetch(0, spot).wait()
            load(0, spot).wait()

        for ahead in (first + 4, first + 5):
            pl.when(ahead < total)(lambda ahead=ahead: load(listed[ahead], ahead).start())
        ready(first)
        pl.when(both)(lambda: ready(first + 1))
        panel = panels[pl.ds(first, 2)].reshape(2 * TILE, 2 * TILE)
        for c in range(cols_dev):
            span = slice(c * TILE, (c + 1) * TILE)
            change = dot(panel, own[:, span])
            for h in (0, 1):
                keep = mask[listed[first + h], c] > 0
                part = jnp.where(keep, change[h * TILE : (h + 1) * TILE], 0.0)
                before = old[first + h, :, span].astype(jnp.float32)
                new[first + h, :, span] = (before - part).astype(jnp.bfloat16)

        @pl.when(me[0] == 0)
        def _():
            for h in (0, 1):
                new[first + h, :, :TILE] = panels[first + h, :, :TILE]

                @pl.when(listed[first + h] > 1)
                def _():
                    new[first + h, :, TILE : 2 * TILE] = panels[first + h, :, TILE:]

        store(listed[first], first).start()
        pl.when(both)(lambda: store(listed[first + 1], first + 1).start())

    @pl.loop(0, total)
    def _(spot):
        store(0, spot).wait()

    if start:
        top_out.wait()


def update(table, mask, me, own, front, numbers, blocks, room, base=None):
    width = front.shape[1]
    count = len(numbers)
    operands = [table, mask, me, own, in_hbm(front), *[in_hbm(block) for block in blocks]]
    in_specs = [SMEM, SMEM, SMEM, VMEM, HBM] + [HBM] * count
    aliases = {}
    if base is not None:
        aliases = {len(operands): 0}
        operands.append(in_hbm(base))
        in_specs.append(HBM)
    return pl.pallas_call(
        functools.partial(update_kernel, tuple(numbers), room, width // TILE, base is None),
        out_shape=jax.ShapeDtypeStruct(front.shape, jnp.bfloat16),
        in_specs=in_specs,
        out_specs=HBM,
        scratch_shapes=[
            pltpu.VMEM((room, TILE, 2 * TILE), jnp.bfloat16),
            pltpu.VMEM((room, TILE, width), jnp.bfloat16),
            pltpu.VMEM((room + 1, TILE, width), jnp.bfloat16),
            pltpu.SMEM((room + 1,), jnp.int32),
            pltpu.SemaphoreType.DMA((room,)),
            pltpu.SemaphoreType.DMA((room + 1,)),
            pltpu.SemaphoreType.DMA((room + 1,)),
        ],
        input_output_aliases=aliases,
        compiler_params=pltpu.CompilerParams(vmem_limit_bytes=UPDATE_LIMIT),
        cost_estimate=pl.CostEstimate(
            flops=2 * room * TILE * width * 2 * TILE, bytes_accessed=4 * room * TILE * width, transcendentals=0
        ),
        name="update",
    )(*operands)


def after(values, *others):
    return lax.optimization_barrier((tuple(values), others))[0]


def one_of(g, members):
    result = g == members[0]
    for member in members[1:]:
        result = result | (g == member)
    return result


def shards(front_in, panel_inverse, tile_mask, tile_map):
    front = front_in[0]
    width = front.shape[1]
    tiles = front.shape[0] // TILE
    cols_dev = width // TILE
    inverse = panel_inverse[0]
    mask = tile_mask[0]
    targets = tile_map[0, 0]
    contrib = targets.shape[0]
    rows_out = contrib // cols_dev
    n_grp = lax.axis_size("grp")
    n_front = lax.axis_size("front")
    slots_dev = n_grp // 2
    g = lax.axis_index("grp")
    me = jnp.reshape(g, (1,)).astype(jnp.int32)
    root = g == 0

    perms, rules = routes(n_grp)
    lists = stream_plan(perms, rules, n_grp, tiles, cols_dev, rows_out)
    if n_grp == 8:
        lists[1] += lists[0][-2 * CHAINS :]
    got = travel(perms, rules, lists, n_grp, tiles)
    events = len(got)
    longest = max(len(lists[0]), len(lists[1]))

    order = [(e, lists[s][e]) for e in range(longest) for s in (0, 1) if e < len(lists[s])]
    order = [(e, tile) for n, (e, tile) in enumerate(order) if tile not in [other for _, other in order[:n]]]
    order.append((longest, 0))
    cuts = list(range(0, len(order) - 2, 4)) + [len(order)]
    made, parts, where_made = [], None, {}

    def make(e, turn):
        nonlocal parts
        while len(made) < len(cuts) - 1:
            begin, end = cuts[len(made)], cuts[len(made) + 1]
            if order[begin][0] > max(0, e + 1 if begin < 8 else e + 2):
                break
            names = [tile for _, tile in order[begin:end]]
            for n, tile in enumerate(names):
                where_made[tile] = (len(made), n)
            if parts is None:
                *made_now, parts, one = factor(front, mask, names, inverse=inverse)
                parts = (parts, one)
            else:
                made_now = factor(front, mask, names, parts=after(parts, *turn))
            made.append(made_now)

    make(-2, ())
    odd = [[n for n in range(n_grp) if rules[s][n] != rules[s][0]] for s in (0, 1)]
    others = [one_of(g, odd[s]) if odd[s] else None for s in (0, 1)]
    scalars = [value for value in (root, *others) if value is not None]
    table = []
    for n in range(n_grp):
        line = []
        for now in got:
            for arrival in now:
                line.append(arrival[n] if arrival[n] not in line else 0)
        table.append(line)
    rows = jnp.asarray(table, jnp.int32)
    used = [[any(line[2 * e + s] for line in table) for s in (0, 1)] for e in range(events)]
    for e in reversed(range(events - CHAINS)):
        for s in (0, 1):
            used[e][s] = used[e][s] or any(used[e + CHAINS])

    needed = [
        [n * cols_dev + c for c in range(cols_dev)] + [tiles - rows_out + r for r in range(rows_out)]
        for n in range(n_grp)
    ]
    ready = max(table[n].index(tile) // 2 for n in range(1, n_grp) for tile in needed[n])

    def own_part():
        blocks, names = [], {}

        def choice(tile, n):
            if n == 0:
                name = (-1, tile)
                which, place = where_made[tile]
                block = made[which][place]
            else:
                name = divmod(table[n].index(tile), 2)
                block = held[name[0]][name[1]]
            if name not in names:
                names[name] = len(blocks)
                blocks.append(block)
            return names[name]

        choices = [[choice(needed[n][part], n) for n in range(n_grp)] for part in range(cols_dev + rows_out)]
        return own_panels(mask, targets, me, front, blocks, choices, rows_out, n_front, n_grp * slots_dev)

    def exchange(blocks, axis):
        return lax.all_to_all(blocks, axis, split_axis=0, concat_axis=0, tiled=True)

    def relayed(arrived):
        digits = arrived[:, 2 * TILE, :4].astype(jnp.int32).reshape(n_front, 2, 2)
        return exchange(relay(digits[..., 0] * 32 + digits[..., 1], arrived, slots_dev, n_grp), "grp")

    held, turn, result, done = [], (), None, 0

    def step(count, *waits):
        nonlocal result, done
        numbers = [n for n in range(2 * done, 2 * (done + count)) if any(line[n] for line in table)]
        done += count
        here = after((me,), *waits)[0] if waits else me
        blocks = [held[n // 2][n % 2] for n in numbers]
        result = update(rows, mask, here, own, front, numbers, blocks, 2 * count, base=result)

    relay_after = min(RELAY_AFTER, events - 1 - ready - CHAINS)
    for e in range(events):
        values = []
        for s in (0, 1):
            value = None
            if e >= CHAINS:
                value = held[e - CHAINS][rules[s][0]]
                if others[s] is not None:
                    value = jnp.where(others[s], held[e - CHAINS][1 - rules[s][0]], value)
            if e < len(lists[s]):
                which, n = where_made[lists[s][e]]
                value = made[which][n] if value is None else jnp.where(root, made[which][n], value)
            values.append(value)
        turn = after(values, *turn, *(scalars if e == 0 else ()))
        held.append([lax.ppermute(turn[s], "grp", perms[s]) if used[e][s] else turn[s] for s in (0, 1)])
        make(e, turn)
        if CHAINS <= e + 1 < events:
            held[e + 1 - CHAINS] = list(after(held[e + 1 - CHAINS], *turn))
        late = e - ready - CHAINS
        if late == 0:
            own, sends = own_part()
        if late == 1:
            arrived = exchange(after((sends,), *turn)[0], "front")
        if late == relay_after:
            arrived = relayed(after((arrived,), *turn)[0])
        elif late == 2 or late > RELAY_AFTER and e % 4 == 0:
            step(min(8, e - CHAINS + 1 - done), *turn)
            turn = (*turn, result)
    while done < events:
        step(min(8, events - done), *turn)
    slots_here = after((arrived,), result)[0]
    parent_tiles = sum_parents(slots_here[:, TILE, 0].astype(jnp.int32), slots_here, slots_dev)
    return (result[None], parent_tiles)


def solution(mesh):
    in_specs = (
        P("front", None, "grp"),
        P("front", None, None, None),
        P("front", None, "grp"),
        P("front", "grp", None),
    )
    out_specs = (P("front", None, "grp"), P(("front", "grp"), None, None))
    return jax.shard_map(shards, mesh=mesh, in_specs=in_specs, out_specs=out_specs, check_vma=False)
```

```python
import functools

import jax
import jax.numpy as jnp
from jax import lax
from jax.experimental import pallas as pl
from jax.experimental.pallas import tpu as pltpu
from jax.sharding import PartitionSpec as P

TILE = 256
CHAINS = 2
LABEL_ROWS = 16
VMEM_LIMIT = 16 * 1024 * 1024
UPDATE_LIMIT = 32 * 1024 * 1024
HBM = pl.BlockSpec(memory_space=pltpu.HBM)
VMEM = pl.BlockSpec(memory_space=pltpu.VMEM)
SMEM = pl.BlockSpec(memory_space=pltpu.SMEM)


def ring_order(n_grp):
    depth = 4 if n_grp % 4 == 0 and n_grp >= 8 else 1
    width = n_grp // depth
    if depth == 1:
        return list(range(n_grp))
    order = [z * width for z in range(depth)]
    for number, z in enumerate(reversed(range(depth))):
        ys = range(1, width) if number % 2 == 0 else range(width - 1, 0, -1)
        order += [z * width + y for y in ys]
    return order


def routes(n_grp):
    if n_grp == 8:
        climb = [(g, (g + 2) % n_grp) for g in range(n_grp)]
        cross = [(g, g ^ 1) for g in range(n_grp)]
        rules = [[0] * n_grp, [0] * n_grp]
        rules[0][1] = rules[0][n_grp - 1] = rules[1][1] = 1
        return [climb, cross], rules
    cycle = ring_order(n_grp)
    ring = [(g, cycle[(d + 1) % n_grp]) for d, g in enumerate(cycle)]
    return [ring, [(b, a) for a, b in ring]], [[0] * n_grp, [1] * n_grp]


def travel(perms, rules, lists, n_grp, tiles):
    got = []
    missing = {(g, tile) for g in range(n_grp) for tile in range(1, tiles)}
    while missing:
        e = len(got)
        now = []
        for s in (0, 1):
            arrival = [0] * n_grp
            for g, target in perms[s]:
                if g == 0 and e < len(lists[s]):
                    arrival[target] = lists[s][e]
                elif e >= CHAINS:
                    arrival[target] = got[e - CHAINS][rules[s][g]][g]
            now.append(arrival)
            missing -= set(enumerate(arrival))
        got.append(now)
    return got


def delays(perms, rules, n_grp):
    result = [[None] * n_grp, [None] * n_grp]
    for s in (0, 1):
        lists = [[], []]
        lists[s] = [1]
        for e, now in enumerate(travel(perms, rules, lists, n_grp, 2)):
            for arrival in now:
                for g in range(n_grp):
                    if arrival[g] and result[s][g] is None:
                        result[s][g] = e
    return result


def stream_plan(perms, rules, n_grp, tiles, cols_dev, rows_out):
    hops = delays(perms, rules, n_grp)
    picks = [[], []]
    bottom = [tiles - 1 - r for r in range(rows_out)]
    heads = [bottom[0::2], bottom[1::2]]

    def shorter():
        return 0 if len(heads[0] + picks[0]) <= len(heads[1] + picks[1]) else 1

    rest = [(n // cols_dev, n) for n in range(1, tiles) if n not in bottom]
    for g, tile in rest:
        if g and hops[0][g] != hops[1][g]:
            picks[0 if hops[0][g] < hops[1][g] else 1].append((g, tile))
    for g, tile in rest:
        if g and hops[0][g] == hops[1][g]:
            picks[shorter()].append((g, tile))
    for s in (0, 1):
        picks[s].sort(key=lambda item: (-hops[s][item[0]], item[1]))
    for g, tile in rest:
        if g == 0:
            picks[shorter()].append((g, tile))
    return [heads[s] + [tile for _, tile in picks[s]] for s in (0, 1)]


def in_hbm(x):
    return pltpu.with_memory_space_constraint(x, pltpu.HBM)


def split2(x):
    hi = x.astype(jnp.bfloat16)
    return hi, (x - hi.astype(jnp.float32)).astype(jnp.bfloat16)


def dot(a, b):
    return jnp.dot(a, b, preferred_element_type=jnp.float32)


def factor_kernel(tiles, head, mask, front, *refs):
    count = len(tiles)
    if head:
        source, outs, rest = refs[0], refs[1 : count + 1], refs[count + 1 :]
        parts, one, blocks, sems, top, top_sem, inverse, inverse_sem = rest
        inverse_copy = pltpu.make_async_copy(source, inverse, inverse_sem)
        inverse_copy.start()
    else:
        parts, one, outs, (blocks, sems) = refs[0], refs[1], refs[2 : count + 2], refs[count + 2 :]
    copies = [
        pltpu.make_async_copy(
            front.at[pl.ds(tile * TILE, TILE), pl.ds(0, 2 * TILE)], blocks.at[n], sems.at[n]
        )
        for n, tile in enumerate(tiles)
    ]
    if head:
        top_copy = pltpu.make_async_copy(front.at[pl.ds(TILE, TILE), pl.ds(0, TILE)], top, top_sem)
        top_copy.start()
    for copy in copies:
        copy.start()

    def first_of(x):
        return (dot(x, parts[1]) + dot(x, parts[0])).astype(jnp.bfloat16)

    if head:
        inverse_copy.wait()
        for which in range(2):
            hi, low = split2(inverse[which].T)
            parts[2 * which] = hi
            parts[2 * which + 1] = low
        top_copy.wait()
        one[...] = first_of(top[...]).astype(jnp.float32).T.astype(jnp.bfloat16)
    for begin in range(0, len(tiles), 2):
        group = list(range(begin, min(begin + 2, len(tiles))))
        for n in group:
            copies[n].wait()
        firsts = first_of(jnp.concatenate([blocks[n, :, :TILE] for n in group], axis=0))
        updates = dot(firsts, one[...])
        works = []
        for place, n in enumerate(group):
            keep = mask[tiles[n] : tiles[n] + 1, 1:2] > 0
            update = updates[place * TILE : (place + 1) * TILE]
            works.append(blocks[n, :, TILE:].astype(jnp.float32) - jnp.where(keep, update, 0.0))
        high, low = split2(jnp.concatenate(works, axis=0))
        seconds = (dot(low, parts[2]) + dot(high, parts[3]) + dot(high, parts[2])).astype(jnp.bfloat16)
        for place, n in enumerate(group):
            span = slice(place * TILE, (place + 1) * TILE)
            empty = jnp.zeros((TILE, TILE), jnp.bfloat16)
            outs[n][:, :TILE] = firsts[span] if tiles[n] > 0 else empty
            outs[n][:, TILE:] = seconds[span] if tiles[n] > 1 else empty


def factor(front, mask, tiles, inverse=None, parts=None):
    head = parts is None
    count = len(tiles)
    out_shape = [jax.ShapeDtypeStruct((TILE, 2 * TILE), jnp.bfloat16)] * count
    scratch = [pltpu.VMEM((count, TILE, 2 * TILE), jnp.bfloat16), pltpu.SemaphoreType.DMA((count,))]
    if head:
        out_shape += [
            jax.ShapeDtypeStruct((4, TILE, TILE), jnp.bfloat16),
            jax.ShapeDtypeStruct((TILE, TILE), jnp.bfloat16),
        ]
        scratch += [pltpu.VMEM((TILE, TILE), jnp.bfloat16), pltpu.SemaphoreType.DMA(())]
        scratch += [pltpu.VMEM((2, TILE, TILE), jnp.float32), pltpu.SemaphoreType.DMA(())]
    operands = (in_hbm(inverse),) if head else parts
    return pl.pallas_call(
        functools.partial(factor_kernel, tuple(tiles), head),
        out_shape=out_shape,
        in_specs=[VMEM, HBM] + [HBM if head else VMEM] * len(operands),
        out_specs=[VMEM] * len(out_shape),
        scratch_shapes=scratch,
        compiler_params=pltpu.CompilerParams(vmem_limit_bytes=VMEM_LIMIT),
        cost_estimate=pl.CostEstimate(
            flops=12 * count * TILE**3, bytes_accessed=4 * count * TILE * 2 * TILE, transcendentals=0
        ),
        name="factor",
    )(mask, in_hbm(front), *operands)


def own_kernel(choices, sources, cols_dev, rows_out, span_front, mask, targets, me, front, *refs):
    blocks, (own, sends, panels, old, sems, old_sem) = refs[:sources], refs[sources:]
    tiles = front.shape[0] // TILE

    def copy(part, source):
        return pltpu.make_async_copy(blocks[source], panels.at[part], sems.at[part])

    old_copy = pltpu.make_async_copy(front.at[pl.ds((tiles - rows_out) * TILE, rows_out * TILE)], old, old_sem)
    old_copy.start()
    for part, options in enumerate(choices):
        for g, source in enumerate(options):
            pl.when(me[0] == g)(lambda part=part, source=source: copy(part, source).start())
    sends[...] = jnp.zeros_like(sends)
    lane = lax.broadcasted_iota(jnp.int32, (LABEL_ROWS, TILE), 1)
    count = cols_dev * rows_out
    labels = [targets[number] + 1 for number in range(count)]
    parents = [targets[number] // span_front for number in range(count)]
    ranks = [sum([(parents[m] == parents[n]).astype(jnp.int32) for m in range(n)], jnp.int32(0)) for n in range(count)]
    for parent in range(sends.shape[0]):
        digits = jnp.zeros((LABEL_ROWS, TILE), jnp.int32)
        for n in range(count):
            spot = jnp.where(parents[n] == parent, 2 * ranks[n], -2)
            digits = jnp.where(lane == spot, labels[n] // 32, digits)
            digits = jnp.where(lane == spot + 1, labels[n] % 32, digits)
        sends[parent, 2 * TILE :, :] = digits.astype(jnp.float32).astype(jnp.bfloat16)
    for part, options in enumerate(choices):
        copy(part, options[0]).wait()
    for c in range(cols_dev):
        own[:, c * TILE : (c + 1) * TILE] = panels[c].astype(jnp.float32).T.astype(jnp.bfloat16)
    old_copy.wait()
    for c in range(cols_dev):
        for r in range(rows_out):
            row, rows, panel = tiles - rows_out + r, slice(r * TILE, (r + 1) * TILE), panels.at[cols_dev + r]
            span = slice(c * TILE, (c + 1) * TILE)
            change = jnp.where(mask[row, c] > 0, dot(panel[...], own[:, span]), 0.0)
            tile = (old[rows, span].astype(jnp.float32) - change).astype(jnp.bfloat16)
            if c < 2:
                tile = jnp.where(me[0] == 0, panel[:, span], tile)
            number = c * rows_out + r
            place = pl.ds(pl.multiple_of(ranks[number] * TILE, TILE), TILE)
            sends[parents[number], place, :] = tile


def own_panels(mask, targets, me, front, blocks, choices, rows_out, n_front, span_front):
    width = front.shape[1]
    parts = len(choices)
    return pl.pallas_call(
        functools.partial(own_kernel, choices, len(blocks), width // TILE, rows_out, span_front),
        out_shape=[
            jax.ShapeDtypeStruct((2 * TILE, width), jnp.bfloat16),
            jax.ShapeDtypeStruct((n_front, 2 * TILE + LABEL_ROWS, TILE), jnp.bfloat16),
        ],
        in_specs=[SMEM, SMEM, SMEM, HBM] + [HBM] * len(blocks),
        out_specs=[VMEM, VMEM],
        scratch_shapes=[
            pltpu.VMEM((parts, TILE, 2 * TILE), jnp.bfloat16),
            pltpu.VMEM((rows_out * TILE, width), jnp.bfloat16),
            pltpu.SemaphoreType.DMA((parts,)),
            pltpu.SemaphoreType.DMA(()),
        ],
        compiler_params=pltpu.CompilerParams(vmem_limit_bytes=VMEM_LIMIT),
        cost_estimate=pl.CostEstimate(
            flops=2 * rows_out * TILE * width * 2 * TILE,
            bytes_accessed=4 * parts * TILE * 2 * TILE,
            transcendentals=0,
        ),
        name="own_panels",
    )(mask, targets, me, in_hbm(front), *[in_hbm(block) for block in blocks])


def relay_kernel(slots, labels, arrived, sends):
    n_grp = sends.shape[0]
    sends[...] = jnp.zeros_like(sends)
    for source in range(arrived.shape[0]):
        for rank in range(2):
            label = labels[source, rank]

            @pl.when(label > 0)
            def _():
                owner = (label - 1) // slots % n_grp
                slot = ((label - 1) % slots + 1).astype(jnp.float32)
                sends[owner, :TILE, :] = arrived[source, rank * TILE : (rank + 1) * TILE, :]
                sends[owner, TILE:, :] = jnp.full((LABEL_ROWS, TILE), slot, jnp.float32).astype(jnp.bfloat16)


def relay(labels, arrived, slots, n_grp):
    return pl.pallas_call(
        functools.partial(relay_kernel, slots),
        out_shape=jax.ShapeDtypeStruct((n_grp, TILE + LABEL_ROWS, TILE), jnp.bfloat16),
        in_specs=[SMEM, VMEM],
        out_specs=VMEM,
        compiler_params=pltpu.CompilerParams(vmem_limit_bytes=VMEM_LIMIT),
        cost_estimate=pl.CostEstimate(flops=0, bytes_accessed=4 * n_grp * TILE * TILE, transcendentals=0),
        name="relay",
    )(labels, arrived)


def sum_kernel(labels, arrived, out):
    out[...] = jnp.zeros_like(out)
    for source in range(arrived.shape[0]):
        label = labels[source]

        @pl.when(label > 0)
        def _():
            slot = label - 1
            out[slot] = out[slot] + arrived[source, :TILE, :].astype(jnp.float32)


def sum_parents(labels, arrived, slots):
    return pl.pallas_call(
        sum_kernel,
        out_shape=jax.ShapeDtypeStruct((slots, TILE, TILE), jnp.float32),
        in_specs=[SMEM, VMEM],
        out_specs=VMEM,
        compiler_params=pltpu.CompilerParams(vmem_limit_bytes=VMEM_LIMIT),
        cost_estimate=pl.CostEstimate(flops=0, bytes_accessed=8 * slots * TILE * TILE, transcendentals=0),
        name="sum_parents",
    )(labels, arrived)


def update_kernel(numbers, room, cols_dev, start, table, mask, me, own, front, *refs):
    count = len(numbers)
    blocks = refs[:count]
    out, panels, old, new, listed, panel_sems, in_sems, out_sems = refs[-8:]

    def place(row):
        return pl.ds(pl.multiple_of(row * TILE, TILE), TILE)

    def fetch(n, spot):
        return pltpu.make_async_copy(blocks[n], panels.at[spot], panel_sems.at[spot])

    def load(row, spot):
        return pltpu.make_async_copy(front.at[place(row)], old.at[spot], in_sems.at[spot])

    def store(row, spot):
        return pltpu.make_async_copy(new.at[spot], out.at[place(row)], out_sems.at[spot])

    spot = jnp.int32(0)
    for n, number in enumerate(numbers):
        row = table[me[0], number]

        def begin(n=n, row=row, spot=spot):
            listed[spot] = row
            fetch(n, spot).start()
            pl.when(spot < 4)(lambda: load(row, spot).start())

        pl.when(row > 0)(begin)
        spot = spot + (row > 0).astype(jnp.int32)
    total = spot
    listed[total] = 0
    if start:
        here = pl.ds(0, TILE)
        top_in = pltpu.make_async_copy(front.at[here], new.at[room], in_sems.at[room])
        top_out = pltpu.make_async_copy(new.at[room], out.at[here], out_sems.at[room])
        top_in.start()
        top_in.wait()
        top_out.start()

    @pl.loop(0, (total + 1) // 2)
    def _(pair):
        first = 2 * pair
        both = first + 1 < total

        def ready(spot):
            fetch(0, spot).wait()
            load(0, spot).wait()

        for ahead in (first + 4, first + 5):
            pl.when(ahead < total)(lambda ahead=ahead: load(listed[ahead], ahead).start())
        ready(first)
        pl.when(both)(lambda: ready(first + 1))
        panel = panels[pl.ds(first, 2)].reshape(2 * TILE, 2 * TILE)
        for c in range(cols_dev):
            span = slice(c * TILE, (c + 1) * TILE)
            change = dot(panel, own[:, span])
            for h in (0, 1):
                keep = mask[listed[first + h], c] > 0
                part = jnp.where(keep, change[h * TILE : (h + 1) * TILE], 0.0)
                before = old[first + h, :, span].astype(jnp.float32)
                new[first + h, :, span] = (before - part).astype(jnp.bfloat16)

        @pl.when(me[0] == 0)
        def _():
            for h in (0, 1):
                new[first + h, :, :TILE] = panels[first + h, :, :TILE]

                @pl.when(listed[first + h] > 1)
                def _():
                    new[first + h, :, TILE : 2 * TILE] = panels[first + h, :, TILE:]

        store(listed[first], first).start()
        pl.when(both)(lambda: store(listed[first + 1], first + 1).start())

    @pl.loop(0, total)
    def _(spot):
        store(0, spot).wait()

    if start:
        top_out.wait()


def update(table, mask, me, own, front, numbers, blocks, room, base=None):
    width = front.shape[1]
    count = len(numbers)
    operands = [table, mask, me, own, in_hbm(front), *[in_hbm(block) for block in blocks]]
    in_specs = [SMEM, SMEM, SMEM, VMEM, HBM] + [HBM] * count
    aliases = {}
    if base is not None:
        aliases = {len(operands): 0}
        operands.append(in_hbm(base))
        in_specs.append(HBM)
    return pl.pallas_call(
        functools.partial(update_kernel, tuple(numbers), room, width // TILE, base is None),
        out_shape=jax.ShapeDtypeStruct(front.shape, jnp.bfloat16),
        in_specs=in_specs,
        out_specs=HBM,
        scratch_shapes=[
            pltpu.VMEM((room, TILE, 2 * TILE), jnp.bfloat16),
            pltpu.VMEM((room, TILE, width), jnp.bfloat16),
            pltpu.VMEM((room + 1, TILE, width), jnp.bfloat16),
            pltpu.SMEM((room + 1,), jnp.int32),
            pltpu.SemaphoreType.DMA((room,)),
            pltpu.SemaphoreType.DMA((room + 1,)),
            pltpu.SemaphoreType.DMA((room + 1,)),
        ],
        input_output_aliases=aliases,
        compiler_params=pltpu.CompilerParams(vmem_limit_bytes=UPDATE_LIMIT),
        cost_estimate=pl.CostEstimate(
            flops=2 * room * TILE * width * 2 * TILE, bytes_accessed=4 * room * TILE * width, transcendentals=0
        ),
        name="update",
    )(*operands)


def after(values, *others):
    return lax.optimization_barrier((tuple(values), others))[0]


def one_of(g, members):
    result = g == members[0]
    for member in members[1:]:
        result = result | (g == member)
    return result


def shards(front_in, panel_inverse, tile_mask, tile_map):
    front = front_in[0]
    width = front.shape[1]
    tiles = front.shape[0] // TILE
    cols_dev = width // TILE
    inverse = panel_inverse[0]
    mask = tile_mask[0]
    targets = tile_map[0, 0]
    contrib = targets.shape[0]
    rows_out = contrib // cols_dev
    n_grp = lax.axis_size("grp")
    n_front = lax.axis_size("front")
    slots_dev = n_grp // 2
    g = lax.axis_index("grp")
    me = jnp.reshape(g, (1,)).astype(jnp.int32)
    root = g == 0

    perms, rules = routes(n_grp)
    lists = stream_plan(perms, rules, n_grp, tiles, cols_dev, rows_out)
    if n_grp == 8:
        lists = [lists[0] + lists[1][-1:], lists[1] + lists[0][-2 * CHAINS :]]
    got = travel(perms, rules, lists, n_grp, tiles)
    events = len(got)
    longest = max(len(lists[0]), len(lists[1]))

    order = [(e, lists[s][e]) for e in range(longest) for s in (0, 1) if e < len(lists[s])]
    order = [(e, tile) for n, (e, tile) in enumerate(order) if tile not in [other for _, other in order[:n]]]
    order.append((longest, 0))
    cuts = list(range(0, len(order) - 2, 4)) + [len(order)]
    made, parts, where_made = [], None, {}

    def make(e, turn):
        nonlocal parts
        while len(made) < len(cuts) - 1:
            begin, end = cuts[len(made)], cuts[len(made) + 1]
            if order[begin][0] > max(0, e + 1 if begin < 8 else e + 2):
                break
            names = [tile for _, tile in order[begin:end]]
            for n, tile in enumerate(names):
                where_made[tile] = (len(made), n)
            if parts is None:
                *made_now, parts, one = factor(front, mask, names, inverse=inverse)
                parts = (parts, one)
            else:
                made_now = factor(front, mask, names, parts=after(parts, *turn))
            made.append(made_now)

    make(-2, ())
    odd = [[n for n in range(n_grp) if rules[s][n] != rules[s][0]] for s in (0, 1)]
    others = [one_of(g, odd[s]) if odd[s] else None for s in (0, 1)]
    scalars = [value for value in (root, *others) if value is not None]
    table = []
    for n in range(n_grp):
        line = []
        for now in got:
            for arrival in now:
                line.append(arrival[n] if arrival[n] not in line else 0)
        table.append(line)
    rows = jnp.asarray(table, jnp.int32)
    used = [[any(line[2 * e + s] for line in table) for s in (0, 1)] for e in range(events)]
    for e in reversed(range(events - CHAINS)):
        for s in (0, 1):
            used[e][s] = used[e][s] or any(used[e + CHAINS])

    needed = [
        [n * cols_dev + c for c in range(cols_dev)] + [tiles - rows_out + r for r in range(rows_out)]
        for n in range(n_grp)
    ]
    ready = max(table[n].index(tile) // 2 for n in range(1, n_grp) for tile in needed[n])

    def own_part():
        blocks, names = [], {}

        def choice(tile, n):
            if n == 0:
                name = (-1, tile)
                which, place = where_made[tile]
                block = made[which][place]
            else:
                name = divmod(table[n].index(tile), 2)
                block = held[name[0]][name[1]]
            if name not in names:
                names[name] = len(blocks)
                blocks.append(block)
            return names[name]

        choices = [[choice(needed[n][part], n) for n in range(n_grp)] for part in range(cols_dev + rows_out)]
        return own_panels(mask, targets, me, front, blocks, choices, rows_out, n_front, n_grp * slots_dev)

    def exchange(blocks, axis):
        return lax.all_to_all(blocks, axis, split_axis=0, concat_axis=0, tiled=True)

    def relayed(arrived):
        digits = arrived[:, 2 * TILE, :4].astype(jnp.int32).reshape(n_front, 2, 2)
        return relay(digits[..., 0] * 32 + digits[..., 1], arrived, slots_dev, n_grp)

    held, turn, result, done = [], (), None, 0

    def step(count, *waits):
        nonlocal result, done
        numbers = [n for n in range(2 * done, 2 * (done + count)) if any(line[n] for line in table)]
        done += count
        here = after((me,), *waits)[0] if waits else me
        blocks = [held[n // 2][n % 2] for n in numbers]
        result = update(rows, mask, here, own, front, numbers, blocks, 2 * count, base=result)

    for e in range(events):
        values = []
        for s in (0, 1):
            value = None
            if e >= CHAINS:
                value = held[e - CHAINS][rules[s][0]]
                if others[s] is not None:
                    value = jnp.where(others[s], held[e - CHAINS][1 - rules[s][0]], value)
            if e < len(lists[s]):
                which, n = where_made[lists[s][e]]
                value = made[which][n] if value is None else jnp.where(root, made[which][n], value)
            values.append(value)
        turn = after(values, *turn, *(scalars if e == 0 else ()))
        held.append([lax.ppermute(turn[s], "grp", perms[s]) if used[e][s] else turn[s] for s in (0, 1)])
        make(e, turn)
        if CHAINS <= e + 1 < events:
            held[e + 1 - CHAINS] = list(after(held[e + 1 - CHAINS], *turn))
        late = e - ready - CHAINS
        if late == 0:
            own, sends = own_part()
        if late == 1:
            arrived = exchange(after((sends,), *turn)[0], "front")
        if late >= 2 and late % 2 == 0 and e < events - 1:
            step(min(4, e - CHAINS + 1 - done), *turn)
            turn = (*turn, result)
    passed = relayed(after((arrived,), *held[-1], *held[-2])[0])
    arrived = exchange(passed, "grp")
    while done < events:
        step(min(8, events - done), passed)
    slots_here = after((arrived,), result)[0]
    parent_tiles = sum_parents(slots_here[:, TILE, 0].astype(jnp.int32), slots_here, slots_dev)
    return (result[None], parent_tiles)


def solution(mesh):
    in_specs = (
        P("front", None, "grp"),
        P("front", None, None, None),
        P("front", None, "grp"),
        P("front", "grp", None),
    )
    out_specs = (P("front", None, "grp"), P(("front", "grp"), None, None))
    return jax.shard_map(shards, mesh=mesh, in_specs=in_specs, out_specs=out_specs, check_vma=False)
```

```python
import functools

import jax
import jax.numpy as jnp
from jax import lax
from jax.experimental import pallas as pl
from jax.experimental.pallas import tpu as pltpu
from jax.sharding import PartitionSpec as P

TILE = 256
CHAINS = 2
LABEL_ROWS = 16
VMEM_LIMIT = 16 * 1024 * 1024
UPDATE_LIMIT = 32 * 1024 * 1024
HBM = pl.BlockSpec(memory_space=pltpu.HBM)
VMEM = pl.BlockSpec(memory_space=pltpu.VMEM)
SMEM = pl.BlockSpec(memory_space=pltpu.SMEM)


def ring_order(n_grp):
    depth = 4 if n_grp % 4 == 0 and n_grp >= 8 else 1
    width = n_grp // depth
    if depth == 1:
        return list(range(n_grp))
    order = [z * width for z in range(depth)]
    for number, z in enumerate(reversed(range(depth))):
        ys = range(1, width) if number % 2 == 0 else range(width - 1, 0, -1)
        order += [z * width + y for y in ys]
    return order


def routes(n_grp):
    if n_grp == 8:
        climb = [(g, (g + 2) % n_grp) for g in range(n_grp)]
        cross = [(g, g ^ 1) for g in range(n_grp)]
        rules = [[0] * n_grp, [0] * n_grp]
        rules[0][1] = rules[0][n_grp - 1] = rules[1][1] = 1
        return [climb, cross], rules
    cycle = ring_order(n_grp)
    ring = [(g, cycle[(d + 1) % n_grp]) for d, g in enumerate(cycle)]
    return [ring, [(b, a) for a, b in ring]], [[0] * n_grp, [1] * n_grp]


def travel(perms, rules, lists, n_grp, tiles):
    got = []
    missing = {(g, tile) for g in range(n_grp) for tile in range(1, tiles)}
    while missing:
        e = len(got)
        now = []
        for s in (0, 1):
            arrival = [0] * n_grp
            for g, target in perms[s]:
                if g == 0 and e < len(lists[s]):
                    arrival[target] = lists[s][e]
                elif e >= CHAINS:
                    arrival[target] = got[e - CHAINS][rules[s][g]][g]
            now.append(arrival)
            missing -= set(enumerate(arrival))
        got.append(now)
    return got


def delays(perms, rules, n_grp):
    result = [[None] * n_grp, [None] * n_grp]
    for s in (0, 1):
        lists = [[], []]
        lists[s] = [1]
        for e, now in enumerate(travel(perms, rules, lists, n_grp, 2)):
            for arrival in now:
                for g in range(n_grp):
                    if arrival[g] and result[s][g] is None:
                        result[s][g] = e
    return result


def stream_plan(perms, rules, n_grp, tiles, cols_dev, rows_out):
    hops = delays(perms, rules, n_grp)
    picks = [[], []]
    bottom = [tiles - 1 - r for r in range(rows_out)]
    heads = [bottom[0::2], bottom[1::2]]

    def shorter():
        return 0 if len(heads[0] + picks[0]) <= len(heads[1] + picks[1]) else 1

    rest = [(n // cols_dev, n) for n in range(1, tiles) if n not in bottom]
    for g, tile in rest:
        if g and hops[0][g] != hops[1][g]:
            picks[0 if hops[0][g] < hops[1][g] else 1].append((g, tile))
    for g, tile in rest:
        if g and hops[0][g] == hops[1][g]:
            picks[shorter()].append((g, tile))
    for s in (0, 1):
        picks[s].sort(key=lambda item: (-hops[s][item[0]], item[1]))
    for g, tile in rest:
        if g == 0:
            picks[shorter()].append((g, tile))
    return [heads[s] + [tile for _, tile in picks[s]] for s in (0, 1)]


def in_hbm(x):
    return pltpu.with_memory_space_constraint(x, pltpu.HBM)


def split2(x):
    hi = x.astype(jnp.bfloat16)
    return hi, (x - hi.astype(jnp.float32)).astype(jnp.bfloat16)


def dot(a, b):
    return jnp.dot(a, b, preferred_element_type=jnp.float32)


def factor_kernel(tiles, head, mask, front, *refs):
    count = len(tiles)
    if head:
        source, outs, rest = refs[0], refs[1 : count + 1], refs[count + 1 :]
        parts, one, blocks, sems, top, top_sem, inverse, inverse_sem = rest
        inverse_copy = pltpu.make_async_copy(source, inverse, inverse_sem)
        inverse_copy.start()
    else:
        parts, one, outs, (blocks, sems) = refs[0], refs[1], refs[2 : count + 2], refs[count + 2 :]
    copies = [
        pltpu.make_async_copy(
            front.at[pl.ds(tile * TILE, TILE), pl.ds(0, 2 * TILE)], blocks.at[n], sems.at[n]
        )
        for n, tile in enumerate(tiles)
    ]
    if head:
        top_copy = pltpu.make_async_copy(front.at[pl.ds(TILE, TILE), pl.ds(0, TILE)], top, top_sem)
        top_copy.start()
    for copy in copies:
        copy.start()

    def first_of(x):
        return (dot(x, parts[1]) + dot(x, parts[0])).astype(jnp.bfloat16)

    if head:
        inverse_copy.wait()
        for which in range(2):
            hi, low = split2(inverse[which].T)
            parts[2 * which] = hi
            parts[2 * which + 1] = low
        top_copy.wait()
        one[...] = first_of(top[...]).astype(jnp.float32).T.astype(jnp.bfloat16)
    for begin in range(0, len(tiles), 2):
        group = list(range(begin, min(begin + 2, len(tiles))))
        for n in group:
            copies[n].wait()
        firsts = first_of(jnp.concatenate([blocks[n, :, :TILE] for n in group], axis=0))
        updates = dot(firsts, one[...])
        works = []
        for place, n in enumerate(group):
            keep = mask[tiles[n] : tiles[n] + 1, 1:2] > 0
            update = updates[place * TILE : (place + 1) * TILE]
            works.append(blocks[n, :, TILE:].astype(jnp.float32) - jnp.where(keep, update, 0.0))
        high, low = split2(jnp.concatenate(works, axis=0))
        seconds = (dot(low, parts[2]) + dot(high, parts[3]) + dot(high, parts[2])).astype(jnp.bfloat16)
        for place, n in enumerate(group):
            span = slice(place * TILE, (place + 1) * TILE)
            empty = jnp.zeros((TILE, TILE), jnp.bfloat16)
            outs[n][:, :TILE] = firsts[span] if tiles[n] > 0 else empty
            outs[n][:, TILE:] = seconds[span] if tiles[n] > 1 else empty


def factor(front, mask, tiles, inverse=None, parts=None):
    head = parts is None
    count = len(tiles)
    out_shape = [jax.ShapeDtypeStruct((TILE, 2 * TILE), jnp.bfloat16)] * count
    scratch = [pltpu.VMEM((count, TILE, 2 * TILE), jnp.bfloat16), pltpu.SemaphoreType.DMA((count,))]
    if head:
        out_shape += [
            jax.ShapeDtypeStruct((4, TILE, TILE), jnp.bfloat16),
            jax.ShapeDtypeStruct((TILE, TILE), jnp.bfloat16),
        ]
        scratch += [pltpu.VMEM((TILE, TILE), jnp.bfloat16), pltpu.SemaphoreType.DMA(())]
        scratch += [pltpu.VMEM((2, TILE, TILE), jnp.float32), pltpu.SemaphoreType.DMA(())]
    operands = (in_hbm(inverse),) if head else parts
    return pl.pallas_call(
        functools.partial(factor_kernel, tuple(tiles), head),
        out_shape=out_shape,
        in_specs=[VMEM, HBM] + [HBM if head else VMEM] * len(operands),
        out_specs=[VMEM] * len(out_shape),
        scratch_shapes=scratch,
        compiler_params=pltpu.CompilerParams(vmem_limit_bytes=VMEM_LIMIT),
        cost_estimate=pl.CostEstimate(
            flops=12 * count * TILE**3, bytes_accessed=4 * count * TILE * 2 * TILE, transcendentals=0
        ),
        name="factor",
    )(mask, in_hbm(front), *operands)


def own_kernel(choices, sources, cols_dev, rows_out, span_front, mask, targets, me, front, *refs):
    blocks, (own, sends, panels, old, sems, old_sem) = refs[:sources], refs[sources:]
    tiles = front.shape[0] // TILE

    def copy(part, source):
        return pltpu.make_async_copy(blocks[source], panels.at[part], sems.at[part])

    old_copy = pltpu.make_async_copy(front.at[pl.ds((tiles - rows_out) * TILE, rows_out * TILE)], old, old_sem)
    old_copy.start()
    for part, options in enumerate(choices):
        for g, source in enumerate(options):
            pl.when(me[0] == g)(lambda part=part, source=source: copy(part, source).start())
    sends[...] = jnp.zeros_like(sends)
    lane = lax.broadcasted_iota(jnp.int32, (LABEL_ROWS, TILE), 1)
    count = cols_dev * rows_out
    labels = [targets[number] + 1 for number in range(count)]
    parents = [targets[number] // span_front for number in range(count)]
    ranks = [sum([(parents[m] == parents[n]).astype(jnp.int32) for m in range(n)], jnp.int32(0)) for n in range(count)]
    for parent in range(sends.shape[0]):
        digits = jnp.zeros((LABEL_ROWS, TILE), jnp.int32)
        for n in range(count):
            spot = jnp.where(parents[n] == parent, 2 * ranks[n], -2)
            digits = jnp.where(lane == spot, labels[n] // 32, digits)
            digits = jnp.where(lane == spot + 1, labels[n] % 32, digits)
        sends[parent, 2 * TILE :, :] = digits.astype(jnp.float32).astype(jnp.bfloat16)
    for part, options in enumerate(choices):
        copy(part, options[0]).wait()
    for c in range(cols_dev):
        own[:, c * TILE : (c + 1) * TILE] = panels[c].astype(jnp.float32).T.astype(jnp.bfloat16)
    old_copy.wait()
    for c in range(cols_dev):
        for r in range(rows_out):
            row, rows, panel = tiles - rows_out + r, slice(r * TILE, (r + 1) * TILE), panels.at[cols_dev + r]
            span = slice(c * TILE, (c + 1) * TILE)
            change = jnp.where(mask[row, c] > 0, dot(panel[...], own[:, span]), 0.0)
            tile = (old[rows, span].astype(jnp.float32) - change).astype(jnp.bfloat16)
            if c < 2:
                tile = jnp.where(me[0] == 0, panel[:, span], tile)
            number = c * rows_out + r
            place = pl.ds(pl.multiple_of(ranks[number] * TILE, TILE), TILE)
            sends[parents[number], place, :] = tile


def own_panels(mask, targets, me, front, blocks, choices, rows_out, n_front, span_front):
    width = front.shape[1]
    parts = len(choices)
    return pl.pallas_call(
        functools.partial(own_kernel, choices, len(blocks), width // TILE, rows_out, span_front),
        out_shape=[
            jax.ShapeDtypeStruct((2 * TILE, width), jnp.bfloat16),
            jax.ShapeDtypeStruct((n_front, 2 * TILE + LABEL_ROWS, TILE), jnp.bfloat16),
        ],
        in_specs=[SMEM, SMEM, SMEM, HBM] + [HBM] * len(blocks),
        out_specs=[VMEM, VMEM],
        scratch_shapes=[
            pltpu.VMEM((parts, TILE, 2 * TILE), jnp.bfloat16),
            pltpu.VMEM((rows_out * TILE, width), jnp.bfloat16),
            pltpu.SemaphoreType.DMA((parts,)),
            pltpu.SemaphoreType.DMA(()),
        ],
        compiler_params=pltpu.CompilerParams(vmem_limit_bytes=VMEM_LIMIT),
        cost_estimate=pl.CostEstimate(
            flops=2 * rows_out * TILE * width * 2 * TILE,
            bytes_accessed=4 * parts * TILE * 2 * TILE,
            transcendentals=0,
        ),
        name="own_panels",
    )(mask, targets, me, in_hbm(front), *[in_hbm(block) for block in blocks])


def relay_kernel(slots, labels, arrived, sends):
    n_grp = sends.shape[0]
    sends[...] = jnp.zeros_like(sends)
    for source in range(arrived.shape[0]):
        for rank in range(2):
            label = labels[source, rank]

            @pl.when(label > 0)
            def _():
                owner = (label - 1) // slots % n_grp
                slot = ((label - 1) % slots + 1).astype(jnp.float32)
                sends[owner, :TILE, :] = arrived[source, rank * TILE : (rank + 1) * TILE, :]
                sends[owner, TILE:, :] = jnp.full((LABEL_ROWS, TILE), slot, jnp.float32).astype(jnp.bfloat16)


def relay(labels, arrived, slots, n_grp):
    return pl.pallas_call(
        functools.partial(relay_kernel, slots),
        out_shape=jax.ShapeDtypeStruct((n_grp, TILE + LABEL_ROWS, TILE), jnp.bfloat16),
        in_specs=[SMEM, VMEM],
        out_specs=VMEM,
        compiler_params=pltpu.CompilerParams(vmem_limit_bytes=VMEM_LIMIT),
        cost_estimate=pl.CostEstimate(flops=0, bytes_accessed=4 * n_grp * TILE * TILE, transcendentals=0),
        name="relay",
    )(labels, arrived)


def sum_kernel(labels, arrived, out):
    out[...] = jnp.zeros_like(out)
    for source in range(arrived.shape[0]):
        label = labels[source]

        @pl.when(label > 0)
        def _():
            slot = label - 1
            out[slot] = out[slot] + arrived[source, :TILE, :].astype(jnp.float32)


def sum_parents(labels, arrived, slots):
    return pl.pallas_call(
        sum_kernel,
        out_shape=jax.ShapeDtypeStruct((slots, TILE, TILE), jnp.float32),
        in_specs=[SMEM, VMEM],
        out_specs=VMEM,
        compiler_params=pltpu.CompilerParams(vmem_limit_bytes=VMEM_LIMIT),
        cost_estimate=pl.CostEstimate(flops=0, bytes_accessed=8 * slots * TILE * TILE, transcendentals=0),
        name="sum_parents",
    )(labels, arrived)


def update_kernel(numbers, room, cols_dev, start, table, mask, me, own, front, *refs):
    count = len(numbers)
    blocks = refs[:count]
    out, panels, old, new, listed, panel_sems, in_sems, out_sems = refs[-8:]

    def place(row):
        return pl.ds(pl.multiple_of(row * TILE, TILE), TILE)

    def fetch(n, spot):
        return pltpu.make_async_copy(blocks[n], panels.at[spot], panel_sems.at[spot])

    def load(row, spot):
        return pltpu.make_async_copy(front.at[place(row)], old.at[spot], in_sems.at[spot])

    def store(row, spot):
        return pltpu.make_async_copy(new.at[spot], out.at[place(row)], out_sems.at[spot])

    spot = jnp.int32(0)
    for n, number in enumerate(numbers):
        row = table[me[0], number]

        def begin(n=n, row=row, spot=spot):
            listed[spot] = row
            fetch(n, spot).start()
            pl.when(spot < 4)(lambda: load(row, spot).start())

        pl.when(row > 0)(begin)
        spot = spot + (row > 0).astype(jnp.int32)
    total = spot
    listed[total] = 0
    if start:
        here = pl.ds(0, TILE)
        top_in = pltpu.make_async_copy(front.at[here], new.at[room], in_sems.at[room])
        top_out = pltpu.make_async_copy(new.at[room], out.at[here], out_sems.at[room])
        top_in.start()
        top_in.wait()
        top_out.start()

    @pl.loop(0, (total + 1) // 2)
    def _(pair):
        first = 2 * pair
        both = first + 1 < total

        def ready(spot):
            fetch(0, spot).wait()
            load(0, spot).wait()

        for ahead in (first + 4, first + 5):
            pl.when(ahead < total)(lambda ahead=ahead: load(listed[ahead], ahead).start())
        ready(first)
        pl.when(both)(lambda: ready(first + 1))
        panel = panels[pl.ds(first, 2)].reshape(2 * TILE, 2 * TILE)
        for c in range(cols_dev):
            span = slice(c * TILE, (c + 1) * TILE)
            change = dot(panel, own[:, span])
            for h in (0, 1):
                keep = mask[listed[first + h], c] > 0
                part = jnp.where(keep, change[h * TILE : (h + 1) * TILE], 0.0)
                before = old[first + h, :, span].astype(jnp.float32)
                new[first + h, :, span] = (before - part).astype(jnp.bfloat16)

        @pl.when(me[0] == 0)
        def _():
            for h in (0, 1):
                new[first + h, :, :TILE] = panels[first + h, :, :TILE]

                @pl.when(listed[first + h] > 1)
                def _():
                    new[first + h, :, TILE : 2 * TILE] = panels[first + h, :, TILE:]

        store(listed[first], first).start()
        pl.when(both)(lambda: store(listed[first + 1], first + 1).start())

    @pl.loop(0, total)
    def _(spot):
        store(0, spot).wait()

    if start:
        top_out.wait()


def update(table, mask, me, own, front, numbers, blocks, room, base=None):
    width = front.shape[1]
    count = len(numbers)
    operands = [table, mask, me, own, in_hbm(front), *[in_hbm(block) for block in blocks]]
    in_specs = [SMEM, SMEM, SMEM, VMEM, HBM] + [HBM] * count
    aliases = {}
    if base is not None:
        aliases = {len(operands): 0}
        operands.append(in_hbm(base))
        in_specs.append(HBM)
    return pl.pallas_call(
        functools.partial(update_kernel, tuple(numbers), room, width // TILE, base is None),
        out_shape=jax.ShapeDtypeStruct(front.shape, jnp.bfloat16),
        in_specs=in_specs,
        out_specs=HBM,
        scratch_shapes=[
            pltpu.VMEM((room, TILE, 2 * TILE), jnp.bfloat16),
            pltpu.VMEM((room, TILE, width), jnp.bfloat16),
            pltpu.VMEM((room + 1, TILE, width), jnp.bfloat16),
            pltpu.SMEM((room + 1,), jnp.int32),
            pltpu.SemaphoreType.DMA((room,)),
            pltpu.SemaphoreType.DMA((room + 1,)),
            pltpu.SemaphoreType.DMA((room + 1,)),
        ],
        input_output_aliases=aliases,
        compiler_params=pltpu.CompilerParams(vmem_limit_bytes=UPDATE_LIMIT),
        cost_estimate=pl.CostEstimate(
            flops=2 * room * TILE * width * 2 * TILE, bytes_accessed=4 * room * TILE * width, transcendentals=0
        ),
        name="update",
    )(*operands)


def after(values, *others):
    return lax.optimization_barrier((tuple(values), others))[0]


def one_of(g, members):
    result = g == members[0]
    for member in members[1:]:
        result = result | (g == member)
    return result


def shards(front_in, panel_inverse, tile_mask, tile_map):
    front = front_in[0]
    width = front.shape[1]
    tiles = front.shape[0] // TILE
    cols_dev = width // TILE
    inverse = panel_inverse[0]
    mask = tile_mask[0]
    targets = tile_map[0, 0]
    contrib = targets.shape[0]
    rows_out = contrib // cols_dev
    n_grp = lax.axis_size("grp")
    n_front = lax.axis_size("front")
    slots_dev = n_grp // 2
    g = lax.axis_index("grp")
    me = jnp.reshape(g, (1,)).astype(jnp.int32)
    root = g == 0

    perms, rules = routes(n_grp)
    lists = stream_plan(perms, rules, n_grp, tiles, cols_dev, rows_out)
    if n_grp == 8:
        lists = [lists[0] + lists[1][-1:], lists[1] + lists[0][-2 * CHAINS :]]
    got = travel(perms, rules, lists, n_grp, tiles)
    events = len(got)
    longest = max(len(lists[0]), len(lists[1]))

    order = [(e, lists[s][e]) for e in range(longest) for s in (0, 1) if e < len(lists[s])]
    order = [(e, tile) for n, (e, tile) in enumerate(order) if tile not in [other for _, other in order[:n]]]
    order.append((longest, 0))
    cuts = list(range(0, len(order) - 2, 4)) + [len(order)]
    made, parts, where_made = [], None, {}

    def make(e, turn):
        nonlocal parts
        while len(made) < len(cuts) - 1:
            begin, end = cuts[len(made)], cuts[len(made) + 1]
            if order[begin][0] > max(0, e + 1 if begin < 8 else e + 2):
                break
            names = [tile for _, tile in order[begin:end]]
            for n, tile in enumerate(names):
                where_made[tile] = (len(made), n)
            if parts is None:
                *made_now, parts, one = factor(front, mask, names, inverse=inverse)
                parts = (parts, one)
            else:
                made_now = factor(front, mask, names, parts=after(parts, *turn))
            made.append(made_now)

    make(-2, ())
    odd = [[n for n in range(n_grp) if rules[s][n] != rules[s][0]] for s in (0, 1)]
    others = [one_of(g, odd[s]) if odd[s] else None for s in (0, 1)]
    scalars = [value for value in (root, *others) if value is not None]
    table = []
    for n in range(n_grp):
        line = []
        for now in got:
            for arrival in now:
                line.append(arrival[n] if arrival[n] not in line else 0)
        table.append(line)
    rows = jnp.asarray(table, jnp.int32)
    used = [[any(line[2 * e + s] for line in table) for s in (0, 1)] for e in range(events)]
    for e in reversed(range(events - CHAINS)):
        for s in (0, 1):
            used[e][s] = used[e][s] or any(used[e + CHAINS])

    needed = [
        [n * cols_dev + c for c in range(cols_dev)] + [tiles - rows_out + r for r in range(rows_out)]
        for n in range(n_grp)
    ]
    ready = max(table[n].index(tile) // 2 for n in range(1, n_grp) for tile in needed[n])

    def own_part():
        blocks, names = [], {}

        def choice(tile, n):
            if n == 0:
                name = (-1, tile)
                which, place = where_made[tile]
                block = made[which][place]
            else:
                name = divmod(table[n].index(tile), 2)
                block = held[name[0]][name[1]]
            if name not in names:
                names[name] = len(blocks)
                blocks.append(block)
            return names[name]

        choices = [[choice(needed[n][part], n) for n in range(n_grp)] for part in range(cols_dev + rows_out)]
        return own_panels(mask, targets, me, front, blocks, choices, rows_out, n_front, n_grp * slots_dev)

    def exchange(blocks, axis):
        return lax.all_to_all(blocks, axis, split_axis=0, concat_axis=0, tiled=True)

    def relayed(arrived):
        digits = arrived[:, 2 * TILE, :4].astype(jnp.int32).reshape(n_front, 2, 2)
        return relay(digits[..., 0] * 32 + digits[..., 1], arrived, slots_dev, n_grp)

    held, turn, result, done = [], (), None, 0

    def step(count, *waits):
        nonlocal result, done
        numbers = [n for n in range(2 * done, 2 * (done + count)) if any(line[n] for line in table)]
        done += count
        here = after((me,), *waits)[0] if waits else me
        blocks = [held[n // 2][n % 2] for n in numbers]
        result = update(rows, mask, here, own, front, numbers, blocks, 2 * count, base=result)

    for e in range(events):
        values = []
        for s in (0, 1):
            value = None
            if e >= CHAINS:
                value = held[e - CHAINS][rules[s][0]]
                if others[s] is not None:
                    value = jnp.where(others[s], held[e - CHAINS][1 - rules[s][0]], value)
            if e < len(lists[s]):
                which, n = where_made[lists[s][e]]
                value = made[which][n] if value is None else jnp.where(root, made[which][n], value)
            values.append(value)
        turn = after(values, *turn, *(scalars if e == 0 else ()))
        held.append([lax.ppermute(turn[s], "grp", perms[s]) if used[e][s] else turn[s] for s in (0, 1)])
        make(e, turn)
        if CHAINS <= e + 1 < events:
            held[e + 1 - CHAINS] = list(after(held[e + 1 - CHAINS], *turn))
        late = e - ready - CHAINS
        if late == 0:
            own, sends = own_part()
        if late == 1:
            arrived = exchange(after((sends,), *turn)[0], "front")
        if late >= 3 and e < events - 1:
            step(2, *turn)
            turn = (*turn, result)
    passed = relayed(after((arrived,), *held[-1], *held[-2])[0])
    arrived = exchange(passed, "grp")
    while done < events:
        step(min(8, events - done), passed)
    slots_here = after((arrived,), result)[0]
    parent_tiles = sum_parents(slots_here[:, TILE, 0].astype(jnp.int32), slots_here, slots_dev)
    return (result[None], parent_tiles)


def solution(mesh):
    in_specs = (
        P("front", None, "grp"),
        P("front", None, None, None),
        P("front", None, "grp"),
        P("front", "grp", None),
    )
    out_specs = (P("front", None, "grp"), P(("front", "grp"), None, None))
    return jax.shard_map(shards, mesh=mesh, in_specs=in_specs, out_specs=out_specs, check_vma=False)
```

```python
import functools

import jax
import jax.numpy as jnp
from jax import lax
from jax.experimental import pallas as pl
from jax.experimental.pallas import tpu as pltpu
from jax.sharding import PartitionSpec as P

TILE = 256
CHAINS = 2
LABEL_ROWS = 16
VMEM_LIMIT = 16 * 1024 * 1024
UPDATE_LIMIT = 32 * 1024 * 1024
HBM = pl.BlockSpec(memory_space=pltpu.HBM)
VMEM = pl.BlockSpec(memory_space=pltpu.VMEM)
SMEM = pl.BlockSpec(memory_space=pltpu.SMEM)


def ring_order(n_grp):
    depth = 4 if n_grp % 4 == 0 and n_grp >= 8 else 1
    width = n_grp // depth
    if depth == 1:
        return list(range(n_grp))
    order = [z * width for z in range(depth)]
    for number, z in enumerate(reversed(range(depth))):
        ys = range(1, width) if number % 2 == 0 else range(width - 1, 0, -1)
        order += [z * width + y for y in ys]
    return order


def routes(n_grp):
    if n_grp == 8:
        climb = [(g, (g + 2) % n_grp) for g in range(n_grp)]
        cross = [(g, g ^ 1) for g in range(n_grp)]
        rules = [[0] * n_grp, [0] * n_grp]
        rules[0][1] = rules[0][n_grp - 1] = rules[1][1] = 1
        return [climb, cross], rules
    cycle = ring_order(n_grp)
    ring = [(g, cycle[(d + 1) % n_grp]) for d, g in enumerate(cycle)]
    return [ring, [(b, a) for a, b in ring]], [[0] * n_grp, [1] * n_grp]


def travel(perms, rules, lists, n_grp, tiles):
    got = []
    missing = {(g, tile) for g in range(n_grp) for tile in range(1, tiles)}
    while missing:
        e = len(got)
        now = []
        for s in (0, 1):
            arrival = [0] * n_grp
            for g, target in perms[s]:
                if g == 0 and e < len(lists[s]):
                    arrival[target] = lists[s][e]
                elif e >= CHAINS:
                    arrival[target] = got[e - CHAINS][rules[s][g]][g]
            now.append(arrival)
            missing -= set(enumerate(arrival))
        got.append(now)
    return got


def delays(perms, rules, n_grp):
    result = [[None] * n_grp, [None] * n_grp]
    for s in (0, 1):
        lists = [[], []]
        lists[s] = [1]
        for e, now in enumerate(travel(perms, rules, lists, n_grp, 2)):
            for arrival in now:
                for g in range(n_grp):
                    if arrival[g] and result[s][g] is None:
                        result[s][g] = e
    return result


def stream_plan(perms, rules, n_grp, tiles, cols_dev, rows_out):
    hops = delays(perms, rules, n_grp)
    picks = [[], []]
    bottom = [tiles - 1 - r for r in range(rows_out)]
    heads = [bottom[0::2], bottom[1::2]]

    def shorter():
        return 0 if len(heads[0] + picks[0]) <= len(heads[1] + picks[1]) else 1

    rest = [(n // cols_dev, n) for n in range(1, tiles) if n not in bottom]
    for g, tile in rest:
        if g and hops[0][g] != hops[1][g]:
            picks[0 if hops[0][g] < hops[1][g] else 1].append((g, tile))
    for g, tile in rest:
        if g and hops[0][g] == hops[1][g]:
            picks[shorter()].append((g, tile))
    for s in (0, 1):
        picks[s].sort(key=lambda item: (-hops[s][item[0]], item[1]))
    for g, tile in rest:
        if g == 0:
            picks[shorter()].append((g, tile))
    return [heads[s] + [tile for _, tile in picks[s]] for s in (0, 1)]


def in_hbm(x):
    return pltpu.with_memory_space_constraint(x, pltpu.HBM)


def split2(x):
    hi = x.astype(jnp.bfloat16)
    return hi, (x - hi.astype(jnp.float32)).astype(jnp.bfloat16)


def dot(a, b):
    return jnp.dot(a, b, preferred_element_type=jnp.float32)


def factor_kernel(tiles, head, mask, front, *refs):
    count = len(tiles)
    if head:
        source, outs, rest = refs[0], refs[1 : count + 1], refs[count + 1 :]
        parts, one, blocks, sems, top, top_sem, inverse, inverse_sem = rest
        inverse_copy = pltpu.make_async_copy(source, inverse, inverse_sem)
        inverse_copy.start()
    else:
        parts, one, outs, (blocks, sems) = refs[0], refs[1], refs[2 : count + 2], refs[count + 2 :]
    copies = [
        pltpu.make_async_copy(
            front.at[pl.ds(tile * TILE, TILE), pl.ds(0, 2 * TILE)], blocks.at[n], sems.at[n]
        )
        for n, tile in enumerate(tiles)
    ]
    if head:
        top_copy = pltpu.make_async_copy(front.at[pl.ds(TILE, TILE), pl.ds(0, TILE)], top, top_sem)
        top_copy.start()
    for copy in copies:
        copy.start()

    def first_of(x):
        return (dot(x, parts[1]) + dot(x, parts[0])).astype(jnp.bfloat16)

    if head:
        inverse_copy.wait()
        for which in range(2):
            hi, low = split2(inverse[which].T)
            parts[2 * which] = hi
            parts[2 * which + 1] = low
        top_copy.wait()
        one[...] = first_of(top[...]).astype(jnp.float32).T.astype(jnp.bfloat16)
    for begin in range(0, len(tiles), 2):
        group = list(range(begin, min(begin + 2, len(tiles))))
        for n in group:
            copies[n].wait()
        firsts = first_of(jnp.concatenate([blocks[n, :, :TILE] for n in group], axis=0))
        updates = dot(firsts, one[...])
        works = []
        for place, n in enumerate(group):
            keep = mask[tiles[n] : tiles[n] + 1, 1:2] > 0
            update = updates[place * TILE : (place + 1) * TILE]
            works.append(blocks[n, :, TILE:].astype(jnp.float32) - jnp.where(keep, update, 0.0))
        high, low = split2(jnp.concatenate(works, axis=0))
        seconds = (dot(low, parts[2]) + dot(high, parts[3]) + dot(high, parts[2])).astype(jnp.bfloat16)
        for place, n in enumerate(group):
            span = slice(place * TILE, (place + 1) * TILE)
            empty = jnp.zeros((TILE, TILE), jnp.bfloat16)
            outs[n][:, :TILE] = firsts[span] if tiles[n] > 0 else empty
            outs[n][:, TILE:] = seconds[span] if tiles[n] > 1 else empty


def factor(front, mask, tiles, inverse=None, parts=None):
    head = parts is None
    count = len(tiles)
    out_shape = [jax.ShapeDtypeStruct((TILE, 2 * TILE), jnp.bfloat16)] * count
    scratch = [pltpu.VMEM((count, TILE, 2 * TILE), jnp.bfloat16), pltpu.SemaphoreType.DMA((count,))]
    if head:
        out_shape += [
            jax.ShapeDtypeStruct((4, TILE, TILE), jnp.bfloat16),
            jax.ShapeDtypeStruct((TILE, TILE), jnp.bfloat16),
        ]
        scratch += [pltpu.VMEM((TILE, TILE), jnp.bfloat16), pltpu.SemaphoreType.DMA(())]
        scratch += [pltpu.VMEM((2, TILE, TILE), jnp.float32), pltpu.SemaphoreType.DMA(())]
    operands = (in_hbm(inverse),) if head else parts
    return pl.pallas_call(
        functools.partial(factor_kernel, tuple(tiles), head),
        out_shape=out_shape,
        in_specs=[VMEM, HBM] + [HBM if head else VMEM] * len(operands),
        out_specs=[VMEM] * len(out_shape),
        scratch_shapes=scratch,
        compiler_params=pltpu.CompilerParams(vmem_limit_bytes=VMEM_LIMIT),
        cost_estimate=pl.CostEstimate(
            flops=12 * count * TILE**3, bytes_accessed=4 * count * TILE * 2 * TILE, transcendentals=0
        ),
        name="factor",
    )(mask, in_hbm(front), *operands)


def own_kernel(choices, sources, cols_dev, rows_out, span_front, mask, targets, me, front, *refs):
    blocks, (own, sends, panels, old, sems, old_sem) = refs[:sources], refs[sources:]
    tiles = front.shape[0] // TILE

    def copy(part, source):
        return pltpu.make_async_copy(blocks[source], panels.at[part], sems.at[part])

    old_copy = pltpu.make_async_copy(front.at[pl.ds((tiles - rows_out) * TILE, rows_out * TILE)], old, old_sem)
    old_copy.start()
    for part, options in enumerate(choices):
        for g, source in enumerate(options):
            pl.when(me[0] == g)(lambda part=part, source=source: copy(part, source).start())
    sends[...] = jnp.zeros_like(sends)
    lane = lax.broadcasted_iota(jnp.int32, (LABEL_ROWS, TILE), 1)
    count = cols_dev * rows_out
    labels = [targets[number] + 1 for number in range(count)]
    parents = [targets[number] // span_front for number in range(count)]
    ranks = [sum([(parents[m] == parents[n]).astype(jnp.int32) for m in range(n)], jnp.int32(0)) for n in range(count)]
    for parent in range(sends.shape[0]):
        digits = jnp.zeros((LABEL_ROWS, TILE), jnp.int32)
        for n in range(count):
            spot = jnp.where(parents[n] == parent, 2 * ranks[n], -2)
            digits = jnp.where(lane == spot, labels[n] // 32, digits)
            digits = jnp.where(lane == spot + 1, labels[n] % 32, digits)
        sends[parent, 2 * TILE :, :] = digits.astype(jnp.float32).astype(jnp.bfloat16)
    for part, options in enumerate(choices):
        copy(part, options[0]).wait()
    for c in range(cols_dev):
        own[:, c * TILE : (c + 1) * TILE] = panels[c].astype(jnp.float32).T.astype(jnp.bfloat16)
    old_copy.wait()
    for c in range(cols_dev):
        for r in range(rows_out):
            row, rows, panel = tiles - rows_out + r, slice(r * TILE, (r + 1) * TILE), panels.at[cols_dev + r]
            span = slice(c * TILE, (c + 1) * TILE)
            change = jnp.where(mask[row, c] > 0, dot(panel[...], own[:, span]), 0.0)
            tile = (old[rows, span].astype(jnp.float32) - change).astype(jnp.bfloat16)
            if c < 2:
                tile = jnp.where(me[0] == 0, panel[:, span], tile)
            number = c * rows_out + r
            place = pl.ds(pl.multiple_of(ranks[number] * TILE, TILE), TILE)
            sends[parents[number], place, :] = tile


def own_panels(mask, targets, me, front, blocks, choices, rows_out, n_front, span_front):
    width = front.shape[1]
    parts = len(choices)
    return pl.pallas_call(
        functools.partial(own_kernel, choices, len(blocks), width // TILE, rows_out, span_front),
        out_shape=[
            jax.ShapeDtypeStruct((2 * TILE, width), jnp.bfloat16),
            jax.ShapeDtypeStruct((n_front, 2 * TILE + LABEL_ROWS, TILE), jnp.bfloat16),
        ],
        in_specs=[SMEM, SMEM, SMEM, HBM] + [HBM] * len(blocks),
        out_specs=[VMEM, VMEM],
        scratch_shapes=[
            pltpu.VMEM((parts, TILE, 2 * TILE), jnp.bfloat16),
            pltpu.VMEM((rows_out * TILE, width), jnp.bfloat16),
            pltpu.SemaphoreType.DMA((parts,)),
            pltpu.SemaphoreType.DMA(()),
        ],
        compiler_params=pltpu.CompilerParams(vmem_limit_bytes=VMEM_LIMIT),
        cost_estimate=pl.CostEstimate(
            flops=2 * rows_out * TILE * width * 2 * TILE,
            bytes_accessed=4 * parts * TILE * 2 * TILE,
            transcendentals=0,
        ),
        name="own_panels",
    )(mask, targets, me, in_hbm(front), *[in_hbm(block) for block in blocks])


def relay_kernel(slots, labels, arrived, sends):
    n_grp = sends.shape[0]
    sends[...] = jnp.zeros_like(sends)
    for source in range(arrived.shape[0]):
        for rank in range(2):
            label = labels[source, rank]

            @pl.when(label > 0)
            def _():
                owner = (label - 1) // slots % n_grp
                slot = ((label - 1) % slots + 1).astype(jnp.float32)
                sends[owner, :TILE, :] = arrived[source, rank * TILE : (rank + 1) * TILE, :]
                sends[owner, TILE:, :] = jnp.full((LABEL_ROWS, TILE), slot, jnp.float32).astype(jnp.bfloat16)


def relay(labels, arrived, slots, n_grp):
    return pl.pallas_call(
        functools.partial(relay_kernel, slots),
        out_shape=jax.ShapeDtypeStruct((n_grp, TILE + LABEL_ROWS, TILE), jnp.bfloat16),
        in_specs=[SMEM, VMEM],
        out_specs=VMEM,
        compiler_params=pltpu.CompilerParams(vmem_limit_bytes=VMEM_LIMIT),
        cost_estimate=pl.CostEstimate(flops=0, bytes_accessed=4 * n_grp * TILE * TILE, transcendentals=0),
        name="relay",
    )(labels, arrived)


def sum_kernel(labels, arrived, out):
    out[...] = jnp.zeros_like(out)
    for source in range(arrived.shape[0]):
        label = labels[source]

        @pl.when(label > 0)
        def _():
            slot = label - 1
            out[slot] = out[slot] + arrived[source, :TILE, :].astype(jnp.float32)


def sum_parents(labels, arrived, slots):
    return pl.pallas_call(
        sum_kernel,
        out_shape=jax.ShapeDtypeStruct((slots, TILE, TILE), jnp.float32),
        in_specs=[SMEM, VMEM],
        out_specs=VMEM,
        compiler_params=pltpu.CompilerParams(vmem_limit_bytes=VMEM_LIMIT),
        cost_estimate=pl.CostEstimate(flops=0, bytes_accessed=8 * slots * TILE * TILE, transcendentals=0),
        name="sum_parents",
    )(labels, arrived)


def update_kernel(numbers, room, cols_dev, start, table, mask, me, own, front, *refs):
    count = len(numbers)
    blocks = refs[:count]
    out, panels, old, new, listed, panel_sems, in_sems, out_sems = refs[-8:]

    def place(row):
        return pl.ds(pl.multiple_of(row * TILE, TILE), TILE)

    def fetch(n, spot):
        return pltpu.make_async_copy(blocks[n], panels.at[spot], panel_sems.at[spot])

    def load(row, spot):
        return pltpu.make_async_copy(front.at[place(row)], old.at[spot], in_sems.at[spot])

    def store(row, spot):
        return pltpu.make_async_copy(new.at[spot], out.at[place(row)], out_sems.at[spot])

    spot = jnp.int32(0)
    for n, number in enumerate(numbers):
        row = table[me[0], number]

        def begin(n=n, row=row, spot=spot):
            listed[spot] = row
            fetch(n, spot).start()
            pl.when(spot < 4)(lambda: load(row, spot).start())

        pl.when(row > 0)(begin)
        spot = spot + (row > 0).astype(jnp.int32)
    total = spot
    listed[total] = 0
    if start:
        here = pl.ds(0, TILE)
        top_in = pltpu.make_async_copy(front.at[here], new.at[room], in_sems.at[room])
        top_out = pltpu.make_async_copy(new.at[room], out.at[here], out_sems.at[room])
        top_in.start()
        top_in.wait()
        top_out.start()

    @pl.loop(0, (total + 1) // 2)
    def _(pair):
        first = 2 * pair
        both = first + 1 < total

        def ready(spot):
            fetch(0, spot).wait()
            load(0, spot).wait()

        for ahead in (first + 4, first + 5):
            pl.when(ahead < total)(lambda ahead=ahead: load(listed[ahead], ahead).start())
        ready(first)
        pl.when(both)(lambda: ready(first + 1))
        panel = panels[pl.ds(first, 2)].reshape(2 * TILE, 2 * TILE)
        for c in range(cols_dev):
            span = slice(c * TILE, (c + 1) * TILE)
            change = dot(panel, own[:, span])
            for h in (0, 1):
                keep = mask[listed[first + h], c] > 0
                part = jnp.where(keep, change[h * TILE : (h + 1) * TILE], 0.0)
                before = old[first + h, :, span].astype(jnp.float32)
                new[first + h, :, span] = (before - part).astype(jnp.bfloat16)

        @pl.when(me[0] == 0)
        def _():
            for h in (0, 1):
                new[first + h, :, :TILE] = panels[first + h, :, :TILE]

                @pl.when(listed[first + h] > 1)
                def _():
                    new[first + h, :, TILE : 2 * TILE] = panels[first + h, :, TILE:]

        store(listed[first], first).start()
        pl.when(both)(lambda: store(listed[first + 1], first + 1).start())

    @pl.loop(0, total)
    def _(spot):
        store(0, spot).wait()

    if start:
        top_out.wait()


def update(table, mask, me, own, front, numbers, blocks, room, base=None):
    width = front.shape[1]
    count = len(numbers)
    operands = [table, mask, me, own, in_hbm(front), *[in_hbm(block) for block in blocks]]
    in_specs = [SMEM, SMEM, SMEM, VMEM, HBM] + [HBM] * count
    aliases = {}
    if base is not None:
        aliases = {len(operands): 0}
        operands.append(in_hbm(base))
        in_specs.append(HBM)
    return pl.pallas_call(
        functools.partial(update_kernel, tuple(numbers), room, width // TILE, base is None),
        out_shape=jax.ShapeDtypeStruct(front.shape, jnp.bfloat16),
        in_specs=in_specs,
        out_specs=HBM,
        scratch_shapes=[
            pltpu.VMEM((room, TILE, 2 * TILE), jnp.bfloat16),
            pltpu.VMEM((room, TILE, width), jnp.bfloat16),
            pltpu.VMEM((room + 1, TILE, width), jnp.bfloat16),
            pltpu.SMEM((room + 1,), jnp.int32),
            pltpu.SemaphoreType.DMA((room,)),
            pltpu.SemaphoreType.DMA((room + 1,)),
            pltpu.SemaphoreType.DMA((room + 1,)),
        ],
        input_output_aliases=aliases,
        compiler_params=pltpu.CompilerParams(vmem_limit_bytes=UPDATE_LIMIT),
        cost_estimate=pl.CostEstimate(
            flops=2 * room * TILE * width * 2 * TILE, bytes_accessed=4 * room * TILE * width, transcendentals=0
        ),
        name="update",
    )(*operands)


def after(values, *others):
    return lax.optimization_barrier((tuple(values), others))[0]


def one_of(g, members):
    result = g == members[0]
    for member in members[1:]:
        result = result | (g == member)
    return result


def shards(front_in, panel_inverse, tile_mask, tile_map):
    front = front_in[0]
    width = front.shape[1]
    tiles = front.shape[0] // TILE
    cols_dev = width // TILE
    inverse = panel_inverse[0]
    mask = tile_mask[0]
    targets = tile_map[0, 0]
    contrib = targets.shape[0]
    rows_out = contrib // cols_dev
    n_grp = lax.axis_size("grp")
    n_front = lax.axis_size("front")
    slots_dev = n_grp // 2
    g = lax.axis_index("grp")
    me = jnp.reshape(g, (1,)).astype(jnp.int32)
    root = g == 0

    perms, rules = routes(n_grp)
    lists = stream_plan(perms, rules, n_grp, tiles, cols_dev, rows_out)
    if n_grp == 8:
        lists = [lists[0] + lists[1][-1:], lists[1] + lists[0][-2 * CHAINS :]]
    got = travel(perms, rules, lists, n_grp, tiles)
    events = len(got)
    longest = max(len(lists[0]), len(lists[1]))

    order = [(e, lists[s][e]) for e in range(longest) for s in (0, 1) if e < len(lists[s])]
    order = [(e, tile) for n, (e, tile) in enumerate(order) if tile not in [other for _, other in order[:n]]]
    order.append((longest, 0))
    cuts = list(range(0, len(order) - 2, 4)) + [len(order)]
    made, parts, where_made = [], None, {}

    def make(e, turn):
        nonlocal parts
        while len(made) < len(cuts) - 1:
            begin, end = cuts[len(made)], cuts[len(made) + 1]
            if order[begin][0] > max(0, e + 1 if begin < 8 else e + 2):
                break
            names = [tile for _, tile in order[begin:end]]
            for n, tile in enumerate(names):
                where_made[tile] = (len(made), n)
            if parts is None:
                *made_now, parts, one = factor(front, mask, names, inverse=inverse)
                parts = (parts, one)
            else:
                made_now = factor(front, mask, names, parts=after(parts, *turn))
            made.append(made_now)

    make(-2, ())
    odd = [[n for n in range(n_grp) if rules[s][n] != rules[s][0]] for s in (0, 1)]
    others = [one_of(g, odd[s]) if odd[s] else None for s in (0, 1)]
    scalars = [value for value in (root, *others) if value is not None]
    table = []
    for n in range(n_grp):
        line = []
        for now in got:
            for arrival in now:
                line.append(arrival[n] if arrival[n] not in line else 0)
        table.append(line)
    rows = jnp.asarray(table, jnp.int32)
    used = [[any(line[2 * e + s] for line in table) for s in (0, 1)] for e in range(events)]
    for e in reversed(range(events - CHAINS)):
        for s in (0, 1):
            used[e][s] = used[e][s] or any(used[e + CHAINS])

    needed = [
        [n * cols_dev + c for c in range(cols_dev)] + [tiles - rows_out + r for r in range(rows_out)]
        for n in range(n_grp)
    ]
    ready = max(table[n].index(tile) // 2 for n in range(1, n_grp) for tile in needed[n])

    def own_part():
        blocks, names = [], {}

        def choice(tile, n):
            if n == 0:
                name = (-1, tile)
                which, place = where_made[tile]
                block = made[which][place]
            else:
                name = divmod(table[n].index(tile), 2)
                block = held[name[0]][name[1]]
            if name not in names:
                names[name] = len(blocks)
                blocks.append(block)
            return names[name]

        choices = [[choice(needed[n][part], n) for n in range(n_grp)] for part in range(cols_dev + rows_out)]
        return own_panels(mask, targets, me, front, blocks, choices, rows_out, n_front, n_grp * slots_dev)

    def exchange(blocks, axis):
        return lax.all_to_all(blocks, axis, split_axis=0, concat_axis=0, tiled=True)

    def relayed(arrived):
        digits = arrived[:, 2 * TILE, :4].astype(jnp.int32).reshape(n_front, 2, 2)
        return relay(digits[..., 0] * 32 + digits[..., 1], arrived, slots_dev, n_grp)

    held, turn, result, done = [], (), None, 0

    def step(count, *waits):
        nonlocal result, done
        numbers = [n for n in range(2 * done, 2 * (done + count)) if any(line[n] for line in table)]
        done += count
        here = after((me,), *waits)[0] if waits else me
        blocks = [held[n // 2][n % 2] for n in numbers]
        result = update(rows, mask, here, own, front, numbers, blocks, 2 * count, base=result)

    for e in range(events):
        values = []
        for s in (0, 1):
            value = None
            if e >= CHAINS:
                value = held[e - CHAINS][rules[s][0]]
                if others[s] is not None:
                    value = jnp.where(others[s], held[e - CHAINS][1 - rules[s][0]], value)
            if e < len(lists[s]):
                which, n = where_made[lists[s][e]]
                value = made[which][n] if value is None else jnp.where(root, made[which][n], value)
            values.append(value)
        turn = after(values, *turn, *(scalars if e == 0 else ()))
        held.append([lax.ppermute(turn[s], "grp", perms[s]) if used[e][s] else turn[s] for s in (0, 1)])
        make(e, turn)
        if CHAINS <= e + 1 < events:
            held[e + 1 - CHAINS] = list(after(held[e + 1 - CHAINS], *turn))
        late = e - ready - CHAINS
        if late == 0:
            own, sends = own_part()
        if late == 1:
            arrived = exchange(after((sends,), *turn)[0], "front")
        if late == 4:
            step(4, *turn)
            turn = (*turn, result)
    passed = relayed(after((arrived,), *held[-1], *held[-2])[0])
    arrived = exchange(passed, "grp")
    while done < events:
        step(min(8, events - done), passed)
    slots_here = after((arrived,), result)[0]
    parent_tiles = sum_parents(slots_here[:, TILE, 0].astype(jnp.int32), slots_here, slots_dev)
    return (result[None], parent_tiles)


def solution(mesh):
    in_specs = (
        P("front", None, "grp"),
        P("front", None, None, None),
        P("front", None, "grp"),
        P("front", "grp", None),
    )
    out_specs = (P("front", None, "grp"), P(("front", "grp"), None, None))
    return jax.shard_map(shards, mesh=mesh, in_specs=in_specs, out_specs=out_specs, check_vma=False)
```

```python
import functools

import jax
import jax.numpy as jnp
from jax import lax
from jax.experimental import pallas as pl
from jax.experimental.pallas import tpu as pltpu
from jax.sharding import PartitionSpec as P

TILE = 256
CHAINS = 2
LABEL_ROWS = 16
VMEM_LIMIT = 16 * 1024 * 1024
UPDATE_LIMIT = 32 * 1024 * 1024
HBM = pl.BlockSpec(memory_space=pltpu.HBM)
VMEM = pl.BlockSpec(memory_space=pltpu.VMEM)
SMEM = pl.BlockSpec(memory_space=pltpu.SMEM)


def ring_order(n_grp):
    depth = 4 if n_grp % 4 == 0 and n_grp >= 8 else 1
    width = n_grp // depth
    if depth == 1:
        return list(range(n_grp))
    order = [z * width for z in range(depth)]
    for number, z in enumerate(reversed(range(depth))):
        ys = range(1, width) if number % 2 == 0 else range(width - 1, 0, -1)
        order += [z * width + y for y in ys]
    return order


def routes(n_grp):
    if n_grp == 8:
        climb = [(g, (g + 2) % n_grp) for g in range(n_grp)]
        cross = [(g, g ^ 1) for g in range(n_grp)]
        rules = [[0] * n_grp, [0] * n_grp]
        rules[0][1] = rules[0][n_grp - 1] = rules[1][1] = 1
        return [climb, cross], rules
    cycle = ring_order(n_grp)
    ring = [(g, cycle[(d + 1) % n_grp]) for d, g in enumerate(cycle)]
    return [ring, [(b, a) for a, b in ring]], [[0] * n_grp, [1] * n_grp]


def travel(perms, rules, lists, n_grp, tiles):
    got = []
    missing = {(g, tile) for g in range(n_grp) for tile in range(1, tiles)}
    while missing:
        e = len(got)
        now = []
        for s in (0, 1):
            arrival = [0] * n_grp
            for g, target in perms[s]:
                if g == 0 and e < len(lists[s]):
                    arrival[target] = lists[s][e]
                elif e >= CHAINS:
                    arrival[target] = got[e - CHAINS][rules[s][g]][g]
            now.append(arrival)
            missing -= set(enumerate(arrival))
        got.append(now)
    return got


def delays(perms, rules, n_grp):
    result = [[None] * n_grp, [None] * n_grp]
    for s in (0, 1):
        lists = [[], []]
        lists[s] = [1]
        for e, now in enumerate(travel(perms, rules, lists, n_grp, 2)):
            for arrival in now:
                for g in range(n_grp):
                    if arrival[g] and result[s][g] is None:
                        result[s][g] = e
    return result


def stream_plan(perms, rules, n_grp, tiles, cols_dev, rows_out):
    hops = delays(perms, rules, n_grp)
    picks = [[], []]
    bottom = [tiles - 1 - r for r in range(rows_out)]
    heads = [bottom[0::2], bottom[1::2]]

    def shorter():
        return 0 if len(heads[0] + picks[0]) <= len(heads[1] + picks[1]) else 1

    rest = [(n // cols_dev, n) for n in range(1, tiles) if n not in bottom]
    for g, tile in rest:
        if g and hops[0][g] != hops[1][g]:
            picks[0 if hops[0][g] < hops[1][g] else 1].append((g, tile))
    for g, tile in rest:
        if g and hops[0][g] == hops[1][g]:
            picks[shorter()].append((g, tile))
    for s in (0, 1):
        picks[s].sort(key=lambda item: (-hops[s][item[0]], item[1]))
    for g, tile in rest:
        if g == 0:
            picks[shorter()].append((g, tile))
    return [heads[s] + [tile for _, tile in picks[s]] for s in (0, 1)]


def in_hbm(x):
    return pltpu.with_memory_space_constraint(x, pltpu.HBM)


def split2(x):
    hi = x.astype(jnp.bfloat16)
    return hi, (x - hi.astype(jnp.float32)).astype(jnp.bfloat16)


def dot(a, b):
    return jnp.dot(a, b, preferred_element_type=jnp.float32)


def factor_kernel(tiles, head, mask, front, *refs):
    count = len(tiles)
    if head:
        source, outs, rest = refs[0], refs[1 : count + 1], refs[count + 1 :]
        parts, one, blocks, sems, top, top_sem, inverse, inverse_sem = rest
        inverse_copy = pltpu.make_async_copy(source, inverse, inverse_sem)
        inverse_copy.start()
    else:
        parts, one, outs, (blocks, sems) = refs[0], refs[1], refs[2 : count + 2], refs[count + 2 :]
    copies = [
        pltpu.make_async_copy(
            front.at[pl.ds(tile * TILE, TILE), pl.ds(0, 2 * TILE)], blocks.at[n], sems.at[n]
        )
        for n, tile in enumerate(tiles)
    ]
    if head:
        top_copy = pltpu.make_async_copy(front.at[pl.ds(TILE, TILE), pl.ds(0, TILE)], top, top_sem)
        top_copy.start()
    for copy in copies:
        copy.start()

    def first_of(x):
        return (dot(x, parts[1]) + dot(x, parts[0])).astype(jnp.bfloat16)

    if head:
        inverse_copy.wait()
        for which in range(2):
            hi, low = split2(inverse[which].T)
            parts[2 * which] = hi
            parts[2 * which + 1] = low
        top_copy.wait()
        one[...] = first_of(top[...]).astype(jnp.float32).T.astype(jnp.bfloat16)
    for begin in range(0, len(tiles), 2):
        group = list(range(begin, min(begin + 2, len(tiles))))
        for n in group:
            copies[n].wait()
        firsts = first_of(jnp.concatenate([blocks[n, :, :TILE] for n in group], axis=0))
        updates = dot(firsts, one[...])
        works = []
        for place, n in enumerate(group):
            keep = mask[tiles[n] : tiles[n] + 1, 1:2] > 0
            update = updates[place * TILE : (place + 1) * TILE]
            works.append(blocks[n, :, TILE:].astype(jnp.float32) - jnp.where(keep, update, 0.0))
        high, low = split2(jnp.concatenate(works, axis=0))
        seconds = (dot(low, parts[2]) + dot(high, parts[3]) + dot(high, parts[2])).astype(jnp.bfloat16)
        for place, n in enumerate(group):
            span = slice(place * TILE, (place + 1) * TILE)
            empty = jnp.zeros((TILE, TILE), jnp.bfloat16)
            outs[n][:, :TILE] = firsts[span] if tiles[n] > 0 else empty
            outs[n][:, TILE:] = seconds[span] if tiles[n] > 1 else empty


def factor(front, mask, tiles, inverse=None, parts=None):
    head = parts is None
    count = len(tiles)
    out_shape = [jax.ShapeDtypeStruct((TILE, 2 * TILE), jnp.bfloat16)] * count
    scratch = [pltpu.VMEM((count, TILE, 2 * TILE), jnp.bfloat16), pltpu.SemaphoreType.DMA((count,))]
    if head:
        out_shape += [
            jax.ShapeDtypeStruct((4, TILE, TILE), jnp.bfloat16),
            jax.ShapeDtypeStruct((TILE, TILE), jnp.bfloat16),
        ]
        scratch += [pltpu.VMEM((TILE, TILE), jnp.bfloat16), pltpu.SemaphoreType.DMA(())]
        scratch += [pltpu.VMEM((2, TILE, TILE), jnp.float32), pltpu.SemaphoreType.DMA(())]
    operands = (in_hbm(inverse),) if head else parts
    return pl.pallas_call(
        functools.partial(factor_kernel, tuple(tiles), head),
        out_shape=out_shape,
        in_specs=[VMEM, HBM] + [HBM if head else VMEM] * len(operands),
        out_specs=[VMEM] * len(out_shape),
        scratch_shapes=scratch,
        compiler_params=pltpu.CompilerParams(vmem_limit_bytes=VMEM_LIMIT),
        cost_estimate=pl.CostEstimate(
            flops=12 * count * TILE**3, bytes_accessed=4 * count * TILE * 2 * TILE, transcendentals=0
        ),
        name="factor",
    )(mask, in_hbm(front), *operands)


def own_kernel(choices, sources, cols_dev, rows_out, span_front, mask, targets, me, front, *refs):
    blocks, (own, sends, panels, old, sems, old_sem) = refs[:sources], refs[sources:]
    tiles = front.shape[0] // TILE

    def copy(part, source):
        return pltpu.make_async_copy(blocks[source], panels.at[part], sems.at[part])

    old_copy = pltpu.make_async_copy(front.at[pl.ds((tiles - rows_out) * TILE, rows_out * TILE)], old, old_sem)
    old_copy.start()
    for part, options in enumerate(choices):
        for g, source in enumerate(options):
            pl.when(me[0] == g)(lambda part=part, source=source: copy(part, source).start())
    sends[...] = jnp.zeros_like(sends)
    lane = lax.broadcasted_iota(jnp.int32, (LABEL_ROWS, TILE), 1)
    count = cols_dev * rows_out
    labels = [targets[number] + 1 for number in range(count)]
    parents = [targets[number] // span_front for number in range(count)]
    ranks = [sum([(parents[m] == parents[n]).astype(jnp.int32) for m in range(n)], jnp.int32(0)) for n in range(count)]
    for parent in range(sends.shape[0]):
        digits = jnp.zeros((LABEL_ROWS, TILE), jnp.int32)
        for n in range(count):
            spot = jnp.where(parents[n] == parent, 2 * ranks[n], -2)
            digits = jnp.where(lane == spot, labels[n] // 32, digits)
            digits = jnp.where(lane == spot + 1, labels[n] % 32, digits)
        sends[parent, 2 * TILE :, :] = digits.astype(jnp.float32).astype(jnp.bfloat16)
    for part, options in enumerate(choices):
        copy(part, options[0]).wait()
    for c in range(cols_dev):
        own[:, c * TILE : (c + 1) * TILE] = panels[c].astype(jnp.float32).T.astype(jnp.bfloat16)
    old_copy.wait()
    for c in range(cols_dev):
        for r in range(rows_out):
            row, rows, panel = tiles - rows_out + r, slice(r * TILE, (r + 1) * TILE), panels.at[cols_dev + r]
            span = slice(c * TILE, (c + 1) * TILE)
            change = jnp.where(mask[row, c] > 0, dot(panel[...], own[:, span]), 0.0)
            tile = (old[rows, span].astype(jnp.float32) - change).astype(jnp.bfloat16)
            if c < 2:
                tile = jnp.where(me[0] == 0, panel[:, span], tile)
            number = c * rows_out + r
            place = pl.ds(pl.multiple_of(ranks[number] * TILE, TILE), TILE)
            sends[parents[number], place, :] = tile


def own_panels(mask, targets, me, front, blocks, choices, rows_out, n_front, span_front):
    width = front.shape[1]
    parts = len(choices)
    return pl.pallas_call(
        functools.partial(own_kernel, choices, len(blocks), width // TILE, rows_out, span_front),
        out_shape=[
            jax.ShapeDtypeStruct((2 * TILE, width), jnp.bfloat16),
            jax.ShapeDtypeStruct((n_front, 2 * TILE + LABEL_ROWS, TILE), jnp.bfloat16),
        ],
        in_specs=[SMEM, SMEM, SMEM, HBM] + [HBM] * len(blocks),
        out_specs=[VMEM, VMEM],
        scratch_shapes=[
            pltpu.VMEM((parts, TILE, 2 * TILE), jnp.bfloat16),
            pltpu.VMEM((rows_out * TILE, width), jnp.bfloat16),
            pltpu.SemaphoreType.DMA((parts,)),
            pltpu.SemaphoreType.DMA(()),
        ],
        compiler_params=pltpu.CompilerParams(vmem_limit_bytes=VMEM_LIMIT),
        cost_estimate=pl.CostEstimate(
            flops=2 * rows_out * TILE * width * 2 * TILE,
            bytes_accessed=4 * parts * TILE * 2 * TILE,
            transcendentals=0,
        ),
        name="own_panels",
    )(mask, targets, me, in_hbm(front), *[in_hbm(block) for block in blocks])


def relay_kernel(slots, labels, arrived, sends):
    n_grp = sends.shape[0]
    sends[...] = jnp.zeros_like(sends)
    for source in range(arrived.shape[0]):
        for rank in range(2):
            label = labels[source, rank]

            @pl.when(label > 0)
            def _():
                owner = (label - 1) // slots % n_grp
                slot = ((label - 1) % slots + 1).astype(jnp.float32)
                sends[owner, :TILE, :] = arrived[source, rank * TILE : (rank + 1) * TILE, :]
                sends[owner, TILE:, :] = jnp.full((LABEL_ROWS, TILE), slot, jnp.float32).astype(jnp.bfloat16)


def relay(labels, arrived, slots, n_grp):
    return pl.pallas_call(
        functools.partial(relay_kernel, slots),
        out_shape=jax.ShapeDtypeStruct((n_grp, TILE + LABEL_ROWS, TILE), jnp.bfloat16),
        in_specs=[SMEM, VMEM],
        out_specs=VMEM,
        compiler_params=pltpu.CompilerParams(vmem_limit_bytes=VMEM_LIMIT),
        cost_estimate=pl.CostEstimate(flops=0, bytes_accessed=4 * n_grp * TILE * TILE, transcendentals=0),
        name="relay",
    )(labels, arrived)


def sum_kernel(labels, arrived, out):
    out[...] = jnp.zeros_like(out)
    for source in range(arrived.shape[0]):
        label = labels[source]

        @pl.when(label > 0)
        def _():
            slot = label - 1
            out[slot] = out[slot] + arrived[source, :TILE, :].astype(jnp.float32)


def sum_parents(labels, arrived, slots):
    return pl.pallas_call(
        sum_kernel,
        out_shape=jax.ShapeDtypeStruct((slots, TILE, TILE), jnp.float32),
        in_specs=[SMEM, VMEM],
        out_specs=VMEM,
        compiler_params=pltpu.CompilerParams(vmem_limit_bytes=VMEM_LIMIT),
        cost_estimate=pl.CostEstimate(flops=0, bytes_accessed=8 * slots * TILE * TILE, transcendentals=0),
        name="sum_parents",
    )(labels, arrived)


def update_kernel(numbers, room, cols_dev, start, table, mask, me, own, front, *refs):
    count = len(numbers)
    blocks = refs[:count]
    out, panels, old, new, listed, panel_sems, in_sems, out_sems = refs[-8:]

    def place(row):
        return pl.ds(pl.multiple_of(row * TILE, TILE), TILE)

    def fetch(n, spot):
        return pltpu.make_async_copy(blocks[n], panels.at[spot], panel_sems.at[spot])

    def load(row, spot):
        return pltpu.make_async_copy(front.at[place(row)], old.at[spot], in_sems.at[spot])

    def store(row, spot):
        return pltpu.make_async_copy(new.at[spot], out.at[place(row)], out_sems.at[spot])

    spot = jnp.int32(0)
    for n, number in enumerate(numbers):
        row = table[me[0], number]

        def begin(n=n, row=row, spot=spot):
            listed[spot] = row
            fetch(n, spot).start()
            pl.when(spot < 4)(lambda: load(row, spot).start())

        pl.when(row > 0)(begin)
        spot = spot + (row > 0).astype(jnp.int32)
    total = spot
    listed[total] = 0
    if start:
        here = pl.ds(0, TILE)
        top_in = pltpu.make_async_copy(front.at[here], new.at[room], in_sems.at[room])
        top_out = pltpu.make_async_copy(new.at[room], out.at[here], out_sems.at[room])
        top_in.start()
        top_in.wait()
        top_out.start()

    @pl.loop(0, (total + 1) // 2)
    def _(pair):
        first = 2 * pair
        both = first + 1 < total

        def ready(spot):
            fetch(0, spot).wait()
            load(0, spot).wait()

        for ahead in (first + 4, first + 5):
            pl.when(ahead < total)(lambda ahead=ahead: load(listed[ahead], ahead).start())
        ready(first)
        pl.when(both)(lambda: ready(first + 1))
        panel = panels[pl.ds(first, 2)].reshape(2 * TILE, 2 * TILE)
        for c in range(cols_dev):
            span = slice(c * TILE, (c + 1) * TILE)
            change = dot(panel, own[:, span])
            for h in (0, 1):
                keep = mask[listed[first + h], c] > 0
                part = jnp.where(keep, change[h * TILE : (h + 1) * TILE], 0.0)
                before = old[first + h, :, span].astype(jnp.float32)
                new[first + h, :, span] = (before - part).astype(jnp.bfloat16)

        @pl.when(me[0] == 0)
        def _():
            for h in (0, 1):
                new[first + h, :, :TILE] = panels[first + h, :, :TILE]

                @pl.when(listed[first + h] > 1)
                def _():
                    new[first + h, :, TILE : 2 * TILE] = panels[first + h, :, TILE:]

        store(listed[first], first).start()
        pl.when(both)(lambda: store(listed[first + 1], first + 1).start())

    @pl.loop(0, total)
    def _(spot):
        store(0, spot).wait()

    if start:
        top_out.wait()


def update(table, mask, me, own, front, numbers, blocks, room, base=None):
    width = front.shape[1]
    count = len(numbers)
    operands = [table, mask, me, own, in_hbm(front), *[in_hbm(block) for block in blocks]]
    in_specs = [SMEM, SMEM, SMEM, VMEM, HBM] + [HBM] * count
    aliases = {}
    if base is not None:
        aliases = {len(operands): 0}
        operands.append(in_hbm(base))
        in_specs.append(HBM)
    return pl.pallas_call(
        functools.partial(update_kernel, tuple(numbers), room, width // TILE, base is None),
        out_shape=jax.ShapeDtypeStruct(front.shape, jnp.bfloat16),
        in_specs=in_specs,
        out_specs=HBM,
        scratch_shapes=[
            pltpu.VMEM((room, TILE, 2 * TILE), jnp.bfloat16),
            pltpu.VMEM((room, TILE, width), jnp.bfloat16),
            pltpu.VMEM((room + 1, TILE, width), jnp.bfloat16),
            pltpu.SMEM((room + 1,), jnp.int32),
            pltpu.SemaphoreType.DMA((room,)),
            pltpu.SemaphoreType.DMA((room + 1,)),
            pltpu.SemaphoreType.DMA((room + 1,)),
        ],
        input_output_aliases=aliases,
        compiler_params=pltpu.CompilerParams(vmem_limit_bytes=UPDATE_LIMIT),
        cost_estimate=pl.CostEstimate(
            flops=2 * room * TILE * width * 2 * TILE, bytes_accessed=4 * room * TILE * width, transcendentals=0
        ),
        name="update",
    )(*operands)


def after(values, *others):
    return lax.optimization_barrier((tuple(values), others))[0]


def one_of(g, members):
    result = g == members[0]
    for member in members[1:]:
        result = result | (g == member)
    return result


def shards(front_in, panel_inverse, tile_mask, tile_map):
    front = front_in[0]
    width = front.shape[1]
    tiles = front.shape[0] // TILE
    cols_dev = width // TILE
    inverse = panel_inverse[0]
    mask = tile_mask[0]
    targets = tile_map[0, 0]
    contrib = targets.shape[0]
    rows_out = contrib // cols_dev
    n_grp = lax.axis_size("grp")
    n_front = lax.axis_size("front")
    slots_dev = n_grp // 2
    g = lax.axis_index("grp")
    me = jnp.reshape(g, (1,)).astype(jnp.int32)
    root = g == 0

    perms, rules = routes(n_grp)
    lists = stream_plan(perms, rules, n_grp, tiles, cols_dev, rows_out)
    if n_grp == 8:
        lists = [lists[0] + lists[1][-1:], lists[1] + lists[0][-2 * CHAINS :]]
    got = travel(perms, rules, lists, n_grp, tiles)
    events = len(got)
    longest = max(len(lists[0]), len(lists[1]))

    order = [(e, lists[s][e]) for e in range(longest) for s in (0, 1) if e < len(lists[s])]
    order = [(e, tile) for n, (e, tile) in enumerate(order) if tile not in [other for _, other in order[:n]]]
    order.append((longest, 0))
    cuts = list(range(0, len(order) - 2, 4)) + [len(order)]
    made, parts, where_made = [], None, {}

    def make(e, turn):
        nonlocal parts
        while len(made) < len(cuts) - 1:
            begin, end = cuts[len(made)], cuts[len(made) + 1]
            if order[begin][0] > max(0, e + 1 if begin < 8 else e + 2):
                break
            names = [tile for _, tile in order[begin:end]]
            for n, tile in enumerate(names):
                where_made[tile] = (len(made), n)
            if parts is None:
                *made_now, parts, one = factor(front, mask, names, inverse=inverse)
                parts = (parts, one)
            else:
                made_now = factor(front, mask, names, parts=after(parts, *turn))
            made.append(made_now)

    make(-2, ())
    odd = [[n for n in range(n_grp) if rules[s][n] != rules[s][0]] for s in (0, 1)]
    others = [one_of(g, odd[s]) if odd[s] else None for s in (0, 1)]
    scalars = [value for value in (root, *others) if value is not None]
    table = []
    for n in range(n_grp):
        line = []
        for now in got:
            for arrival in now:
                line.append(arrival[n] if arrival[n] not in line else 0)
        table.append(line)
    rows = jnp.asarray(table, jnp.int32)
    used = [[any(line[2 * e + s] for line in table) for s in (0, 1)] for e in range(events)]
    for e in reversed(range(events - CHAINS)):
        for s in (0, 1):
            used[e][s] = used[e][s] or any(used[e + CHAINS])

    needed = [
        [n * cols_dev + c for c in range(cols_dev)] + [tiles - rows_out + r for r in range(rows_out)]
        for n in range(n_grp)
    ]
    ready = max(table[n].index(tile) // 2 for n in range(1, n_grp) for tile in needed[n])

    def own_part():
        blocks, names = [], {}

        def choice(tile, n):
            if n == 0:
                name = (-1, tile)
                which, place = where_made[tile]
                block = made[which][place]
            else:
                name = divmod(table[n].index(tile), 2)
                block = held[name[0]][name[1]]
            if name not in names:
                names[name] = len(blocks)
                blocks.append(block)
            return names[name]

        choices = [[choice(needed[n][part], n) for n in range(n_grp)] for part in range(cols_dev + rows_out)]
        return own_panels(mask, targets, me, front, blocks, choices, rows_out, n_front, n_grp * slots_dev)

    def exchange(blocks, axis):
        return lax.all_to_all(blocks, axis, split_axis=0, concat_axis=0, tiled=True)

    def relayed(arrived):
        digits = arrived[:, 2 * TILE, :4].astype(jnp.int32).reshape(n_front, 2, 2)
        return relay(digits[..., 0] * 32 + digits[..., 1], arrived, slots_dev, n_grp)

    held, turn, result, done = [], (), None, 0

    def step(count, *waits):
        nonlocal result, done
        numbers = [n for n in range(2 * done, 2 * (done + count)) if any(line[n] for line in table)]
        done += count
        here = after((me,), *waits)[0] if waits else me
        blocks = [held[n // 2][n % 2] for n in numbers]
        result = update(rows, mask, here, own, front, numbers, blocks, 2 * count, base=result)

    for e in range(events):
        values = []
        for s in (0, 1):
            value = None
            if e >= CHAINS:
                value = held[e - CHAINS][rules[s][0]]
                if others[s] is not None:
                    value = jnp.where(others[s], held[e - CHAINS][1 - rules[s][0]], value)
            if e < len(lists[s]):
                which, n = where_made[lists[s][e]]
                value = made[which][n] if value is None else jnp.where(root, made[which][n], value)
            values.append(value)
        turn = after(values, *turn, *(scalars if e == 0 else ()))
        held.append([lax.ppermute(turn[s], "grp", perms[s]) if used[e][s] else turn[s] for s in (0, 1)])
        make(e, turn)
        if CHAINS <= e + 1 < events:
            held[e + 1 - CHAINS] = list(after(held[e + 1 - CHAINS], *turn))
        late = e - ready - CHAINS
        if late == 0:
            own, sends = own_part()
            turn = (*turn, own)
        if late == 1:
            arrived = exchange(after((sends,), *turn)[0], "front")
        if late == 4:
            step(4, *turn)
            turn = (*turn, result)
    passed = relayed(after((arrived,), *held[-1], *held[-2])[0])
    arrived = exchange(passed, "grp")
    while done < events:
        step(min(8, events - done), passed)
    slots_here = after((arrived,), result)[0]
    parent_tiles = sum_parents(slots_here[:, TILE, 0].astype(jnp.int32), slots_here, slots_dev)
    return (result[None], parent_tiles)


def solution(mesh):
    in_specs = (
        P("front", None, "grp"),
        P("front", None, None, None),
        P("front", None, "grp"),
        P("front", "grp", None),
    )
    out_specs = (P("front", None, "grp"), P(("front", "grp"), None, None))
    return jax.shard_map(shards, mesh=mesh, in_specs=in_specs, out_specs=out_specs, check_vma=False)
```

```python
import functools

import jax
import jax.numpy as jnp
from jax import lax
from jax.experimental import pallas as pl
from jax.experimental.pallas import tpu as pltpu
from jax.sharding import PartitionSpec as P

TILE = 256
CHAINS = 2
LABEL_ROWS = 16
VMEM_LIMIT = 16 * 1024 * 1024
UPDATE_LIMIT = 32 * 1024 * 1024
HBM = pl.BlockSpec(memory_space=pltpu.HBM)
VMEM = pl.BlockSpec(memory_space=pltpu.VMEM)
SMEM = pl.BlockSpec(memory_space=pltpu.SMEM)


def ring_order(n_grp):
    depth = 4 if n_grp % 4 == 0 and n_grp >= 8 else 1
    width = n_grp // depth
    if depth == 1:
        return list(range(n_grp))
    order = [z * width for z in range(depth)]
    for number, z in enumerate(reversed(range(depth))):
        ys = range(1, width) if number % 2 == 0 else range(width - 1, 0, -1)
        order += [z * width + y for y in ys]
    return order


def routes(n_grp):
    if n_grp == 8:
        climb = [(g, (g + 2) % n_grp) for g in range(n_grp)]
        cross = [(g, g ^ 1) for g in range(n_grp)]
        rules = [[0] * n_grp, [0] * n_grp]
        rules[0][1] = rules[0][n_grp - 1] = rules[1][1] = 1
        return [climb, cross], rules
    cycle = ring_order(n_grp)
    ring = [(g, cycle[(d + 1) % n_grp]) for d, g in enumerate(cycle)]
    return [ring, [(b, a) for a, b in ring]], [[0] * n_grp, [1] * n_grp]


def travel(perms, rules, lists, n_grp, tiles):
    got = []
    missing = {(g, tile) for g in range(n_grp) for tile in range(1, tiles)}
    while missing:
        e = len(got)
        now = []
        for s in (0, 1):
            arrival = [0] * n_grp
            for g, target in perms[s]:
                if g == 0 and e < len(lists[s]):
                    arrival[target] = lists[s][e]
                elif e >= CHAINS:
                    arrival[target] = got[e - CHAINS][rules[s][g]][g]
            now.append(arrival)
            missing -= set(enumerate(arrival))
        got.append(now)
    return got


def delays(perms, rules, n_grp):
    result = [[None] * n_grp, [None] * n_grp]
    for s in (0, 1):
        lists = [[], []]
        lists[s] = [1]
        for e, now in enumerate(travel(perms, rules, lists, n_grp, 2)):
            for arrival in now:
                for g in range(n_grp):
                    if arrival[g] and result[s][g] is None:
                        result[s][g] = e
    return result


def stream_plan(perms, rules, n_grp, tiles, cols_dev, rows_out):
    hops = delays(perms, rules, n_grp)
    picks = [[], []]
    bottom = [tiles - 1 - r for r in range(rows_out)]
    heads = [bottom[0::2], bottom[1::2]]

    def shorter():
        return 0 if len(heads[0] + picks[0]) <= len(heads[1] + picks[1]) else 1

    rest = [(n // cols_dev, n) for n in range(1, tiles) if n not in bottom]
    for g, tile in rest:
        if g and hops[0][g] != hops[1][g]:
            picks[0 if hops[0][g] < hops[1][g] else 1].append((g, tile))
    for g, tile in rest:
        if g and hops[0][g] == hops[1][g]:
            picks[shorter()].append((g, tile))
    for s in (0, 1):
        picks[s].sort(key=lambda item: (-hops[s][item[0]], item[1]))
    for g, tile in rest:
        if g == 0:
            picks[shorter()].append((g, tile))
    return [heads[s] + [tile for _, tile in picks[s]] for s in (0, 1)]


def in_hbm(x):
    return pltpu.with_memory_space_constraint(x, pltpu.HBM)


def split2(x):
    hi = x.astype(jnp.bfloat16)
    return hi, (x - hi.astype(jnp.float32)).astype(jnp.bfloat16)


def dot(a, b):
    return jnp.dot(a, b, preferred_element_type=jnp.float32)


def factor_kernel(tiles, head, mask, front, *refs):
    count = len(tiles)
    if head:
        source, outs, rest = refs[0], refs[1 : count + 1], refs[count + 1 :]
        parts, one, blocks, sems, top, top_sem, inverse, inverse_sem = rest
        inverse_copy = pltpu.make_async_copy(source, inverse, inverse_sem)
        inverse_copy.start()
    else:
        parts, one, outs, (blocks, sems) = refs[0], refs[1], refs[2 : count + 2], refs[count + 2 :]
    copies = [
        pltpu.make_async_copy(
            front.at[pl.ds(tile * TILE, TILE), pl.ds(0, 2 * TILE)], blocks.at[n], sems.at[n]
        )
        for n, tile in enumerate(tiles)
    ]
    if head:
        top_copy = pltpu.make_async_copy(front.at[pl.ds(TILE, TILE), pl.ds(0, TILE)], top, top_sem)
        top_copy.start()
    for copy in copies:
        copy.start()

    def first_of(x):
        return (dot(x, parts[1]) + dot(x, parts[0])).astype(jnp.bfloat16)

    if head:
        inverse_copy.wait()
        for which in range(2):
            hi, low = split2(inverse[which].T)
            parts[2 * which] = hi
            parts[2 * which + 1] = low
        top_copy.wait()
        one[...] = first_of(top[...]).astype(jnp.float32).T.astype(jnp.bfloat16)
    for begin in range(0, len(tiles), 2):
        group = list(range(begin, min(begin + 2, len(tiles))))
        for n in group:
            copies[n].wait()
        firsts = first_of(jnp.concatenate([blocks[n, :, :TILE] for n in group], axis=0))
        updates = dot(firsts, one[...])
        works = []
        for place, n in enumerate(group):
            keep = mask[tiles[n] : tiles[n] + 1, 1:2] > 0
            update = updates[place * TILE : (place + 1) * TILE]
            works.append(blocks[n, :, TILE:].astype(jnp.float32) - jnp.where(keep, update, 0.0))
        high, low = split2(jnp.concatenate(works, axis=0))
        seconds = (dot(low, parts[2]) + dot(high, parts[3]) + dot(high, parts[2])).astype(jnp.bfloat16)
        for place, n in enumerate(group):
            span = slice(place * TILE, (place + 1) * TILE)
            empty = jnp.zeros((TILE, TILE), jnp.bfloat16)
            outs[n][:, :TILE] = firsts[span] if tiles[n] > 0 else empty
            outs[n][:, TILE:] = seconds[span] if tiles[n] > 1 else empty


def factor(front, mask, tiles, inverse=None, parts=None):
    head = parts is None
    count = len(tiles)
    out_shape = [jax.ShapeDtypeStruct((TILE, 2 * TILE), jnp.bfloat16)] * count
    scratch = [pltpu.VMEM((count, TILE, 2 * TILE), jnp.bfloat16), pltpu.SemaphoreType.DMA((count,))]
    if head:
        out_shape += [
            jax.ShapeDtypeStruct((4, TILE, TILE), jnp.bfloat16),
            jax.ShapeDtypeStruct((TILE, TILE), jnp.bfloat16),
        ]
        scratch += [pltpu.VMEM((TILE, TILE), jnp.bfloat16), pltpu.SemaphoreType.DMA(())]
        scratch += [pltpu.VMEM((2, TILE, TILE), jnp.float32), pltpu.SemaphoreType.DMA(())]
    operands = (in_hbm(inverse),) if head else parts
    return pl.pallas_call(
        functools.partial(factor_kernel, tuple(tiles), head),
        out_shape=out_shape,
        in_specs=[VMEM, HBM] + [HBM if head else VMEM] * len(operands),
        out_specs=[VMEM] * len(out_shape),
        scratch_shapes=scratch,
        compiler_params=pltpu.CompilerParams(vmem_limit_bytes=VMEM_LIMIT),
        cost_estimate=pl.CostEstimate(
            flops=12 * count * TILE**3, bytes_accessed=4 * count * TILE * 2 * TILE, transcendentals=0
        ),
        name="factor",
    )(mask, in_hbm(front), *operands)


def own_kernel(choices, sources, cols_dev, rows_out, span_front, mask, targets, me, front, *refs):
    blocks, (own, sends, panels, old, sems, old_sem) = refs[:sources], refs[sources:]
    tiles = front.shape[0] // TILE

    def copy(part, source):
        return pltpu.make_async_copy(blocks[source], panels.at[part], sems.at[part])

    old_copy = pltpu.make_async_copy(front.at[pl.ds((tiles - rows_out) * TILE, rows_out * TILE)], old, old_sem)
    old_copy.start()
    for part, options in enumerate(choices):
        for g, source in enumerate(options):
            pl.when(me[0] == g)(lambda part=part, source=source: copy(part, source).start())
    sends[...] = jnp.zeros_like(sends)
    lane = lax.broadcasted_iota(jnp.int32, (LABEL_ROWS, TILE), 1)
    count = cols_dev * rows_out
    labels = [targets[number] + 1 for number in range(count)]
    parents = [targets[number] // span_front for number in range(count)]
    ranks = [sum([(parents[m] == parents[n]).astype(jnp.int32) for m in range(n)], jnp.int32(0)) for n in range(count)]
    for parent in range(sends.shape[0]):
        digits = jnp.zeros((LABEL_ROWS, TILE), jnp.int32)
        for n in range(count):
            spot = jnp.where(parents[n] == parent, 2 * ranks[n], -2)
            digits = jnp.where(lane == spot, labels[n] // 32, digits)
            digits = jnp.where(lane == spot + 1, labels[n] % 32, digits)
        sends[parent, 2 * TILE :, :] = digits.astype(jnp.float32).astype(jnp.bfloat16)
    for part, options in enumerate(choices):
        copy(part, options[0]).wait()
    for c in range(cols_dev):
        own[:, c * TILE : (c + 1) * TILE] = panels[c].astype(jnp.float32).T.astype(jnp.bfloat16)
    old_copy.wait()
    for c in range(cols_dev):
        for r in range(rows_out):
            row, rows, panel = tiles - rows_out + r, slice(r * TILE, (r + 1) * TILE), panels.at[cols_dev + r]
            span = slice(c * TILE, (c + 1) * TILE)
            change = jnp.where(mask[row, c] > 0, dot(panel[...], own[:, span]), 0.0)
            tile = (old[rows, span].astype(jnp.float32) - change).astype(jnp.bfloat16)
            if c < 2:
                tile = jnp.where(me[0] == 0, panel[:, span], tile)
            number = c * rows_out + r
            place = pl.ds(pl.multiple_of(ranks[number] * TILE, TILE), TILE)
            sends[parents[number], place, :] = tile


def own_panels(mask, targets, me, front, blocks, choices, rows_out, n_front, span_front):
    width = front.shape[1]
    parts = len(choices)
    return pl.pallas_call(
        functools.partial(own_kernel, choices, len(blocks), width // TILE, rows_out, span_front),
        out_shape=[
            jax.ShapeDtypeStruct((2 * TILE, width), jnp.bfloat16),
            jax.ShapeDtypeStruct((n_front, 2 * TILE + LABEL_ROWS, TILE), jnp.bfloat16),
        ],
        in_specs=[SMEM, SMEM, SMEM, HBM] + [HBM] * len(blocks),
        out_specs=[VMEM, VMEM],
        scratch_shapes=[
            pltpu.VMEM((parts, TILE, 2 * TILE), jnp.bfloat16),
            pltpu.VMEM((rows_out * TILE, width), jnp.bfloat16),
            pltpu.SemaphoreType.DMA((parts,)),
            pltpu.SemaphoreType.DMA(()),
        ],
        compiler_params=pltpu.CompilerParams(vmem_limit_bytes=VMEM_LIMIT),
        cost_estimate=pl.CostEstimate(
            flops=2 * rows_out * TILE * width * 2 * TILE,
            bytes_accessed=4 * parts * TILE * 2 * TILE,
            transcendentals=0,
        ),
        name="own_panels",
    )(mask, targets, me, in_hbm(front), *[in_hbm(block) for block in blocks])


def relay_kernel(slots, labels, arrived, sends):
    n_grp = sends.shape[0]
    sends[...] = jnp.zeros_like(sends)
    for source in range(arrived.shape[0]):
        for rank in range(2):
            label = labels[source, rank]

            @pl.when(label > 0)
            def _():
                owner = (label - 1) // slots % n_grp
                slot = ((label - 1) % slots + 1).astype(jnp.float32)
                sends[owner, :TILE, :] = arrived[source, rank * TILE : (rank + 1) * TILE, :]
                sends[owner, TILE:, :] = jnp.full((LABEL_ROWS, TILE), slot, jnp.float32).astype(jnp.bfloat16)


def relay(labels, arrived, slots, n_grp):
    return pl.pallas_call(
        functools.partial(relay_kernel, slots),
        out_shape=jax.ShapeDtypeStruct((n_grp, TILE + LABEL_ROWS, TILE), jnp.bfloat16),
        in_specs=[SMEM, VMEM],
        out_specs=VMEM,
        compiler_params=pltpu.CompilerParams(vmem_limit_bytes=VMEM_LIMIT),
        cost_estimate=pl.CostEstimate(flops=0, bytes_accessed=4 * n_grp * TILE * TILE, transcendentals=0),
        name="relay",
    )(labels, arrived)


def sum_kernel(labels, arrived, out):
    out[...] = jnp.zeros_like(out)
    for source in range(arrived.shape[0]):
        label = labels[source]

        @pl.when(label > 0)
        def _():
            slot = label - 1
            out[slot] = out[slot] + arrived[source, :TILE, :].astype(jnp.float32)


def sum_parents(labels, arrived, slots):
    return pl.pallas_call(
        sum_kernel,
        out_shape=jax.ShapeDtypeStruct((slots, TILE, TILE), jnp.float32),
        in_specs=[SMEM, VMEM],
        out_specs=VMEM,
        compiler_params=pltpu.CompilerParams(vmem_limit_bytes=VMEM_LIMIT),
        cost_estimate=pl.CostEstimate(flops=0, bytes_accessed=8 * slots * TILE * TILE, transcendentals=0),
        name="sum_parents",
    )(labels, arrived)


def update_kernel(numbers, room, cols_dev, start, table, mask, me, own, front, *refs):
    count = len(numbers)
    blocks = refs[:count]
    out, panels, old, new, listed, panel_sems, in_sems, out_sems = refs[-8:]

    def place(row):
        return pl.ds(pl.multiple_of(row * TILE, TILE), TILE)

    def fetch(n, spot):
        return pltpu.make_async_copy(blocks[n], panels.at[spot], panel_sems.at[spot])

    def load(row, spot):
        return pltpu.make_async_copy(front.at[place(row)], old.at[spot], in_sems.at[spot])

    def store(row, spot):
        return pltpu.make_async_copy(new.at[spot], out.at[place(row)], out_sems.at[spot])

    spot = jnp.int32(0)
    for n, number in enumerate(numbers):
        row = table[me[0], number]

        def begin(n=n, row=row, spot=spot):
            listed[spot] = row
            fetch(n, spot).start()
            pl.when(spot < 4)(lambda: load(row, spot).start())

        pl.when(row > 0)(begin)
        spot = spot + (row > 0).astype(jnp.int32)
    total = spot
    listed[total] = 0
    if start:
        here = pl.ds(0, TILE)
        top_in = pltpu.make_async_copy(front.at[here], new.at[room], in_sems.at[room])
        top_out = pltpu.make_async_copy(new.at[room], out.at[here], out_sems.at[room])
        top_in.start()
        top_in.wait()
        top_out.start()

    @pl.loop(0, (total + 1) // 2)
    def _(pair):
        first = 2 * pair
        both = first + 1 < total

        def ready(spot):
            fetch(0, spot).wait()
            load(0, spot).wait()

        for ahead in (first + 4, first + 5):
            pl.when(ahead < total)(lambda ahead=ahead: load(listed[ahead], ahead).start())
        ready(first)
        pl.when(both)(lambda: ready(first + 1))
        panel = panels[pl.ds(first, 2)].reshape(2 * TILE, 2 * TILE)
        for c in range(cols_dev):
            span = slice(c * TILE, (c + 1) * TILE)
            change = dot(panel, own[:, span])
            for h in (0, 1):
                keep = mask[listed[first + h], c] > 0
                part = jnp.where(keep, change[h * TILE : (h + 1) * TILE], 0.0)
                before = old[first + h, :, span].astype(jnp.float32)
                new[first + h, :, span] = (before - part).astype(jnp.bfloat16)

        @pl.when(me[0] == 0)
        def _():
            for h in (0, 1):
                new[first + h, :, :TILE] = panels[first + h, :, :TILE]

                @pl.when(listed[first + h] > 1)
                def _():
                    new[first + h, :, TILE : 2 * TILE] = panels[first + h, :, TILE:]

        store(listed[first], first).start()
        pl.when(both)(lambda: store(listed[first + 1], first + 1).start())

    @pl.loop(0, total)
    def _(spot):
        store(0, spot).wait()

    if start:
        top_out.wait()


def update(table, mask, me, own, front, numbers, blocks, room, base=None):
    width = front.shape[1]
    count = len(numbers)
    operands = [table, mask, me, own, in_hbm(front), *[in_hbm(block) for block in blocks]]
    in_specs = [SMEM, SMEM, SMEM, VMEM, HBM] + [HBM] * count
    aliases = {}
    if base is not None:
        aliases = {len(operands): 0}
        operands.append(in_hbm(base))
        in_specs.append(HBM)
    return pl.pallas_call(
        functools.partial(update_kernel, tuple(numbers), room, width // TILE, base is None),
        out_shape=jax.ShapeDtypeStruct(front.shape, jnp.bfloat16),
        in_specs=in_specs,
        out_specs=HBM,
        scratch_shapes=[
            pltpu.VMEM((room, TILE, 2 * TILE), jnp.bfloat16),
            pltpu.VMEM((room, TILE, width), jnp.bfloat16),
            pltpu.VMEM((room + 1, TILE, width), jnp.bfloat16),
            pltpu.SMEM((room + 1,), jnp.int32),
            pltpu.SemaphoreType.DMA((room,)),
            pltpu.SemaphoreType.DMA((room + 1,)),
            pltpu.SemaphoreType.DMA((room + 1,)),
        ],
        input_output_aliases=aliases,
        compiler_params=pltpu.CompilerParams(vmem_limit_bytes=UPDATE_LIMIT),
        cost_estimate=pl.CostEstimate(
            flops=2 * room * TILE * width * 2 * TILE, bytes_accessed=4 * room * TILE * width, transcendentals=0
        ),
        name="update",
    )(*operands)


def after(values, *others):
    return lax.optimization_barrier((tuple(values), others))[0]


def one_of(g, members):
    result = g == members[0]
    for member in members[1:]:
        result = result | (g == member)
    return result


def shards(front_in, panel_inverse, tile_mask, tile_map):
    front = front_in[0]
    width = front.shape[1]
    tiles = front.shape[0] // TILE
    cols_dev = width // TILE
    inverse = panel_inverse[0]
    mask = tile_mask[0]
    targets = tile_map[0, 0]
    contrib = targets.shape[0]
    rows_out = contrib // cols_dev
    n_grp = lax.axis_size("grp")
    n_front = lax.axis_size("front")
    slots_dev = n_grp // 2
    g = lax.axis_index("grp")
    me = jnp.reshape(g, (1,)).astype(jnp.int32)
    root = g == 0

    perms, rules = routes(n_grp)
    lists = stream_plan(perms, rules, n_grp, tiles, cols_dev, rows_out)
    if n_grp == 8:
        lists = [lists[0] + lists[1][-1:], lists[1] + lists[0][-2 * CHAINS :]]
    got = travel(perms, rules, lists, n_grp, tiles)
    events = len(got)
    longest = max(len(lists[0]), len(lists[1]))

    order = [(e, lists[s][e]) for e in range(longest) for s in (0, 1) if e < len(lists[s])]
    order = [(e, tile) for n, (e, tile) in enumerate(order) if tile not in [other for _, other in order[:n]]]
    order.append((longest, 0))
    cuts = list(range(0, len(order) - 2, 4)) + [len(order)]
    made, parts, where_made = [], None, {}

    def make(e, turn):
        nonlocal parts
        while len(made) < len(cuts) - 1:
            begin, end = cuts[len(made)], cuts[len(made) + 1]
            if order[begin][0] > max(0, e + 1 if begin < 8 else e + 2):
                break
            names = [tile for _, tile in order[begin:end]]
            for n, tile in enumerate(names):
                where_made[tile] = (len(made), n)
            if parts is None:
                *made_now, parts, one = factor(front, mask, names, inverse=inverse)
                parts = (parts, one)
            else:
                made_now = factor(front, mask, names, parts=after(parts, *turn))
            made.append(made_now)

    make(-2, ())
    odd = [[n for n in range(n_grp) if rules[s][n] != rules[s][0]] for s in (0, 1)]
    others = [one_of(g, odd[s]) if odd[s] else None for s in (0, 1)]
    scalars = [value for value in (root, *others) if value is not None]
    table = []
    for n in range(n_grp):
        line = []
        for now in got:
            for arrival in now:
                line.append(arrival[n] if arrival[n] not in line else 0)
        table.append(line)
    rows = jnp.asarray(table, jnp.int32)
    used = [[any(line[2 * e + s] for line in table) for s in (0, 1)] for e in range(events)]
    for e in reversed(range(events - CHAINS)):
        for s in (0, 1):
            used[e][s] = used[e][s] or any(used[e + CHAINS])

    needed = [
        [n * cols_dev + c for c in range(cols_dev)] + [tiles - rows_out + r for r in range(rows_out)]
        for n in range(n_grp)
    ]
    ready = max(table[n].index(tile) // 2 for n in range(1, n_grp) for tile in needed[n])

    def own_part():
        blocks, names = [], {}

        def choice(tile, n):
            if n == 0:
                name = (-1, tile)
                which, place = where_made[tile]
                block = made[which][place]
            else:
                name = divmod(table[n].index(tile), 2)
                block = held[name[0]][name[1]]
            if name not in names:
                names[name] = len(blocks)
                blocks.append(block)
            return names[name]

        choices = [[choice(needed[n][part], n) for n in range(n_grp)] for part in range(cols_dev + rows_out)]
        return own_panels(mask, targets, me, front, blocks, choices, rows_out, n_front, n_grp * slots_dev)

    def exchange(blocks, axis):
        return lax.all_to_all(blocks, axis, split_axis=0, concat_axis=0, tiled=True)

    def relayed(arrived):
        digits = arrived[:, 2 * TILE, :4].astype(jnp.int32).reshape(n_front, 2, 2)
        return relay(digits[..., 0] * 32 + digits[..., 1], arrived, slots_dev, n_grp)

    held, turn, result = [], (), None

    def step(begin, end, *waits):
        nonlocal result
        numbers = [n for n in range(2 * begin, 2 * end) if any(line[n] for line in table)]
        here = after((me,), *waits)[0]
        blocks = [held[n // 2][n % 2] for n in numbers]
        result = update(rows, mask, here, own, front, numbers, blocks, 2 * (end - begin), base=result)

    for e in range(events):
        values = []
        for s in (0, 1):
            value = None
            if e >= CHAINS:
                value = held[e - CHAINS][rules[s][0]]
                if others[s] is not None:
                    value = jnp.where(others[s], held[e - CHAINS][1 - rules[s][0]], value)
            if e < len(lists[s]):
                which, n = where_made[lists[s][e]]
                value = made[which][n] if value is None else jnp.where(root, made[which][n], value)
            values.append(value)
        turn = after(values, *turn, *(scalars if e == 0 else ()))
        held.append([lax.ppermute(turn[s], "grp", perms[s]) if used[e][s] else turn[s] for s in (0, 1)])
        make(e, turn)
        if CHAINS <= e + 1 < events:
            held[e + 1 - CHAINS] = list(after(held[e + 1 - CHAINS], *turn))
        late = e - ready - CHAINS
        if late == 0:
            own, sends = own_part()
            turn = (*turn, own)
        if late == 1:
            arrived = exchange(after((sends,), *turn)[0], "front")
        if late == 4:
            step(0, 4, *turn)
            turn = (*turn, result)
    passed = relayed(after((arrived,), *turn, *held[-3])[0])
    arrived = exchange(passed, "grp")
    last = events - 6
    step(last, events, passed)
    for begin in range(4, last, 8):
        step(begin, min(begin + 8, last), passed)
    slots_here = after((arrived,), result)[0]
    parent_tiles = sum_parents(slots_here[:, TILE, 0].astype(jnp.int32), slots_here, slots_dev)
    return (result[None], parent_tiles)


def solution(mesh):
    in_specs = (
        P("front", None, "grp"),
        P("front", None, None, None),
        P("front", None, "grp"),
        P("front", "grp", None),
    )
    out_specs = (P("front", None, "grp"), P(("front", "grp"), None, None))
    return jax.shard_map(shards, mesh=mesh, in_specs=in_specs, out_specs=out_specs, check_vma=False)
```

```python
import functools

import jax
import jax.numpy as jnp
from jax import lax
from jax.experimental import pallas as pl
from jax.experimental.pallas import tpu as pltpu
from jax.sharding import PartitionSpec as P

TILE = 256
CHAINS = 2
LABEL_ROWS = 16
VMEM_LIMIT = 16 * 1024 * 1024
UPDATE_LIMIT = 32 * 1024 * 1024
HBM = pl.BlockSpec(memory_space=pltpu.HBM)
VMEM = pl.BlockSpec(memory_space=pltpu.VMEM)
SMEM = pl.BlockSpec(memory_space=pltpu.SMEM)


def ring_order(n_grp):
    depth = 4 if n_grp % 4 == 0 and n_grp >= 8 else 1
    width = n_grp // depth
    if depth == 1:
        return list(range(n_grp))
    order = [z * width for z in range(depth)]
    for number, z in enumerate(reversed(range(depth))):
        ys = range(1, width) if number % 2 == 0 else range(width - 1, 0, -1)
        order += [z * width + y for y in ys]
    return order


def routes(n_grp):
    if n_grp == 8:
        climb = [(g, (g + 2) % n_grp) for g in range(n_grp)]
        cross = [(g, g ^ 1) for g in range(n_grp)]
        rules = [[0] * n_grp, [0] * n_grp]
        rules[0][1] = rules[0][n_grp - 1] = rules[1][1] = 1
        return [climb, cross], rules
    cycle = ring_order(n_grp)
    ring = [(g, cycle[(d + 1) % n_grp]) for d, g in enumerate(cycle)]
    return [ring, [(b, a) for a, b in ring]], [[0] * n_grp, [1] * n_grp]


def travel(perms, rules, lists, n_grp, tiles):
    got = []
    missing = {(g, tile) for g in range(n_grp) for tile in range(1, tiles)}
    while missing:
        e = len(got)
        now = []
        for s in (0, 1):
            arrival = [0] * n_grp
            for g, target in perms[s]:
                if g == 0 and e < len(lists[s]):
                    arrival[target] = lists[s][e]
                elif e >= CHAINS:
                    arrival[target] = got[e - CHAINS][rules[s][g]][g]
            now.append(arrival)
            missing -= set(enumerate(arrival))
        got.append(now)
    return got


def delays(perms, rules, n_grp):
    result = [[None] * n_grp, [None] * n_grp]
    for s in (0, 1):
        lists = [[], []]
        lists[s] = [1]
        for e, now in enumerate(travel(perms, rules, lists, n_grp, 2)):
            for arrival in now:
                for g in range(n_grp):
                    if arrival[g] and result[s][g] is None:
                        result[s][g] = e
    return result


def stream_plan(perms, rules, n_grp, tiles, cols_dev, rows_out):
    hops = delays(perms, rules, n_grp)
    picks = [[], []]
    bottom = [tiles - 1 - r for r in range(rows_out)]
    heads = [bottom[0::2], bottom[1::2]]

    def shorter():
        return 0 if len(heads[0] + picks[0]) <= len(heads[1] + picks[1]) else 1

    rest = [(n // cols_dev, n) for n in range(1, tiles) if n not in bottom]
    for g, tile in rest:
        if g and hops[0][g] != hops[1][g]:
            picks[0 if hops[0][g] < hops[1][g] else 1].append((g, tile))
    for g, tile in rest:
        if g and hops[0][g] == hops[1][g]:
            picks[shorter()].append((g, tile))
    for s in (0, 1):
        picks[s].sort(key=lambda item: (-hops[s][item[0]], item[1]))
    for g, tile in rest:
        if g == 0:
            picks[shorter()].append((g, tile))
    return [heads[s] + [tile for _, tile in picks[s]] for s in (0, 1)]


def in_hbm(x):
    return pltpu.with_memory_space_constraint(x, pltpu.HBM)


def split2(x):
    hi = x.astype(jnp.bfloat16)
    return hi, (x - hi.astype(jnp.float32)).astype(jnp.bfloat16)


def dot(a, b):
    return jnp.dot(a, b, preferred_element_type=jnp.float32)


def factor_kernel(tiles, head, mask, front, *refs):
    count = len(tiles)
    if head:
        source, outs, rest = refs[0], refs[1 : count + 1], refs[count + 1 :]
        parts, one, blocks, sems, top, top_sem, inverse, inverse_sem = rest
        inverse_copy = pltpu.make_async_copy(source, inverse, inverse_sem)
        inverse_copy.start()
    else:
        parts, one, outs, (blocks, sems) = refs[0], refs[1], refs[2 : count + 2], refs[count + 2 :]
    copies = [
        pltpu.make_async_copy(
            front.at[pl.ds(tile * TILE, TILE), pl.ds(0, 2 * TILE)], blocks.at[n], sems.at[n]
        )
        for n, tile in enumerate(tiles)
    ]
    if head:
        top_copy = pltpu.make_async_copy(front.at[pl.ds(TILE, TILE), pl.ds(0, TILE)], top, top_sem)
        top_copy.start()
    for copy in copies:
        copy.start()

    def first_of(x):
        return (dot(x, parts[1]) + dot(x, parts[0])).astype(jnp.bfloat16)

    if head:
        inverse_copy.wait()
        for which in range(2):
            hi, low = split2(inverse[which].T)
            parts[2 * which] = hi
            parts[2 * which + 1] = low
        top_copy.wait()
        one[...] = first_of(top[...]).astype(jnp.float32).T.astype(jnp.bfloat16)
    for begin in range(0, len(tiles), 2):
        group = list(range(begin, min(begin + 2, len(tiles))))
        for n in group:
            copies[n].wait()
        firsts = first_of(jnp.concatenate([blocks[n, :, :TILE] for n in group], axis=0))
        updates = dot(firsts, one[...])
        works = []
        for place, n in enumerate(group):
            keep = mask[tiles[n] : tiles[n] + 1, 1:2] > 0
            update = updates[place * TILE : (place + 1) * TILE]
            works.append(blocks[n, :, TILE:].astype(jnp.float32) - jnp.where(keep, update, 0.0))
        high, low = split2(jnp.concatenate(works, axis=0))
        seconds = (dot(low, parts[2]) + dot(high, parts[3]) + dot(high, parts[2])).astype(jnp.bfloat16)
        for place, n in enumerate(group):
            span = slice(place * TILE, (place + 1) * TILE)
            empty = jnp.zeros((TILE, TILE), jnp.bfloat16)
            outs[n][:, :TILE] = firsts[span] if tiles[n] > 0 else empty
            outs[n][:, TILE:] = seconds[span] if tiles[n] > 1 else empty


def factor(front, mask, tiles, inverse=None, parts=None):
    head = parts is None
    count = len(tiles)
    out_shape = [jax.ShapeDtypeStruct((TILE, 2 * TILE), jnp.bfloat16)] * count
    scratch = [pltpu.VMEM((count, TILE, 2 * TILE), jnp.bfloat16), pltpu.SemaphoreType.DMA((count,))]
    if head:
        out_shape += [
            jax.ShapeDtypeStruct((4, TILE, TILE), jnp.bfloat16),
            jax.ShapeDtypeStruct((TILE, TILE), jnp.bfloat16),
        ]
        scratch += [pltpu.VMEM((TILE, TILE), jnp.bfloat16), pltpu.SemaphoreType.DMA(())]
        scratch += [pltpu.VMEM((2, TILE, TILE), jnp.float32), pltpu.SemaphoreType.DMA(())]
    operands = (in_hbm(inverse),) if head else parts
    return pl.pallas_call(
        functools.partial(factor_kernel, tuple(tiles), head),
        out_shape=out_shape,
        in_specs=[VMEM, HBM] + [HBM if head else VMEM] * len(operands),
        out_specs=[VMEM] * len(out_shape),
        scratch_shapes=scratch,
        compiler_params=pltpu.CompilerParams(vmem_limit_bytes=VMEM_LIMIT),
        cost_estimate=pl.CostEstimate(
            flops=12 * count * TILE**3, bytes_accessed=4 * count * TILE * 2 * TILE, transcendentals=0
        ),
        name="factor",
    )(mask, in_hbm(front), *operands)


def own_kernel(choices, sources, cols_dev, rows_out, span_front, mask, targets, me, front, *refs):
    blocks, (own, sends, panels, old, sems, old_sem) = refs[:sources], refs[sources:]
    tiles = front.shape[0] // TILE

    def copy(part, source):
        return pltpu.make_async_copy(blocks[source], panels.at[part], sems.at[part])

    old_copy = pltpu.make_async_copy(front.at[pl.ds((tiles - rows_out) * TILE, rows_out * TILE)], old, old_sem)
    old_copy.start()
    for part, options in enumerate(choices):
        for g, source in enumerate(options):
            pl.when(me[0] == g)(lambda part=part, source=source: copy(part, source).start())
    sends[...] = jnp.zeros_like(sends)
    lane = lax.broadcasted_iota(jnp.int32, (LABEL_ROWS, TILE), 1)
    count = cols_dev * rows_out
    labels = [targets[number] + 1 for number in range(count)]
    parents = [targets[number] // span_front for number in range(count)]
    ranks = [sum([(parents[m] == parents[n]).astype(jnp.int32) for m in range(n)], jnp.int32(0)) for n in range(count)]
    for parent in range(sends.shape[0]):
        digits = jnp.zeros((LABEL_ROWS, TILE), jnp.int32)
        for n in range(count):
            spot = jnp.where(parents[n] == parent, 2 * ranks[n], -2)
            digits = jnp.where(lane == spot, labels[n] // 32, digits)
            digits = jnp.where(lane == spot + 1, labels[n] % 32, digits)
        sends[parent, 2 * TILE :, :] = digits.astype(jnp.float32).astype(jnp.bfloat16)
    for part, options in enumerate(choices):
        copy(part, options[0]).wait()
    for c in range(cols_dev):
        own[:, c * TILE : (c + 1) * TILE] = panels[c].astype(jnp.float32).T.astype(jnp.bfloat16)
    old_copy.wait()
    for c in range(cols_dev):
        for r in range(rows_out):
            row, rows, panel = tiles - rows_out + r, slice(r * TILE, (r + 1) * TILE), panels.at[cols_dev + r]
            span = slice(c * TILE, (c + 1) * TILE)
            change = jnp.where(mask[row, c] > 0, dot(panel[...], own[:, span]), 0.0)
            tile = (old[rows, span].astype(jnp.float32) - change).astype(jnp.bfloat16)
            if c < 2:
                tile = jnp.where(me[0] == 0, panel[:, span], tile)
            number = c * rows_out + r
            place = pl.ds(pl.multiple_of(ranks[number] * TILE, TILE), TILE)
            sends[parents[number], place, :] = tile


def own_panels(mask, targets, me, front, blocks, choices, rows_out, n_front, span_front):
    width = front.shape[1]
    parts = len(choices)
    return pl.pallas_call(
        functools.partial(own_kernel, choices, len(blocks), width // TILE, rows_out, span_front),
        out_shape=[
            jax.ShapeDtypeStruct((2 * TILE, width), jnp.bfloat16),
            jax.ShapeDtypeStruct((n_front, 2 * TILE + LABEL_ROWS, TILE), jnp.bfloat16),
        ],
        in_specs=[SMEM, SMEM, SMEM, HBM] + [HBM] * len(blocks),
        out_specs=[VMEM, VMEM],
        scratch_shapes=[
            pltpu.VMEM((parts, TILE, 2 * TILE), jnp.bfloat16),
            pltpu.VMEM((rows_out * TILE, width), jnp.bfloat16),
            pltpu.SemaphoreType.DMA((parts,)),
            pltpu.SemaphoreType.DMA(()),
        ],
        compiler_params=pltpu.CompilerParams(vmem_limit_bytes=VMEM_LIMIT),
        cost_estimate=pl.CostEstimate(
            flops=2 * rows_out * TILE * width * 2 * TILE,
            bytes_accessed=4 * parts * TILE * 2 * TILE,
            transcendentals=0,
        ),
        name="own_panels",
    )(mask, targets, me, in_hbm(front), *[in_hbm(block) for block in blocks])


def relay_kernel(slots, labels, arrived, sends):
    n_grp = sends.shape[0]
    sends[...] = jnp.zeros_like(sends)
    for source in range(arrived.shape[0]):
        for rank in range(2):
            label = labels[source, rank]

            @pl.when(label > 0)
            def _():
                owner = (label - 1) // slots % n_grp
                slot = ((label - 1) % slots + 1).astype(jnp.float32)
                sends[owner, :TILE, :] = arrived[source, rank * TILE : (rank + 1) * TILE, :]
                sends[owner, TILE:, :] = jnp.full((LABEL_ROWS, TILE), slot, jnp.float32).astype(jnp.bfloat16)


def relay(labels, arrived, slots, n_grp):
    return pl.pallas_call(
        functools.partial(relay_kernel, slots),
        out_shape=jax.ShapeDtypeStruct((n_grp, TILE + LABEL_ROWS, TILE), jnp.bfloat16),
        in_specs=[SMEM, VMEM],
        out_specs=VMEM,
        compiler_params=pltpu.CompilerParams(vmem_limit_bytes=VMEM_LIMIT),
        cost_estimate=pl.CostEstimate(flops=0, bytes_accessed=4 * n_grp * TILE * TILE, transcendentals=0),
        name="relay",
    )(labels, arrived)


def sum_kernel(labels, arrived, out):
    out[...] = jnp.zeros_like(out)
    for source in range(arrived.shape[0]):
        label = labels[source]

        @pl.when(label > 0)
        def _():
            slot = label - 1
            out[slot] = out[slot] + arrived[source, :TILE, :].astype(jnp.float32)


def sum_parents(labels, arrived, slots):
    return pl.pallas_call(
        sum_kernel,
        out_shape=jax.ShapeDtypeStruct((slots, TILE, TILE), jnp.float32),
        in_specs=[SMEM, VMEM],
        out_specs=VMEM,
        compiler_params=pltpu.CompilerParams(vmem_limit_bytes=VMEM_LIMIT),
        cost_estimate=pl.CostEstimate(flops=0, bytes_accessed=8 * slots * TILE * TILE, transcendentals=0),
        name="sum_parents",
    )(labels, arrived)


def update_kernel(numbers, room, cols_dev, start, table, mask, me, own, front, *refs):
    count = len(numbers)
    blocks = refs[:count]
    out, panels, old, new, listed, panel_sems, in_sems, out_sems = refs[-8:]

    def place(row):
        return pl.ds(pl.multiple_of(row * TILE, TILE), TILE)

    def fetch(n, spot):
        return pltpu.make_async_copy(blocks[n], panels.at[spot], panel_sems.at[spot])

    def load(row, spot):
        return pltpu.make_async_copy(front.at[place(row)], old.at[spot], in_sems.at[spot])

    def store(row, spot):
        return pltpu.make_async_copy(new.at[spot], out.at[place(row)], out_sems.at[spot])

    spot = jnp.int32(0)
    for n, number in enumerate(numbers):
        row = table[me[0], number]

        def begin(n=n, row=row, spot=spot):
            listed[spot] = row
            fetch(n, spot).start()
            pl.when(spot < 4)(lambda: load(row, spot).start())

        pl.when(row > 0)(begin)
        spot = spot + (row > 0).astype(jnp.int32)
    total = spot
    listed[total] = 0
    if start:
        here = pl.ds(0, TILE)
        top_in = pltpu.make_async_copy(front.at[here], new.at[room], in_sems.at[room])
        top_out = pltpu.make_async_copy(new.at[room], out.at[here], out_sems.at[room])
        top_in.start()
        top_in.wait()
        top_out.start()

    @pl.loop(0, (total + 1) // 2)
    def _(pair):
        first = 2 * pair
        both = first + 1 < total

        def ready(spot):
            fetch(0, spot).wait()
            load(0, spot).wait()

        for ahead in (first + 4, first + 5):
            pl.when(ahead < total)(lambda ahead=ahead: load(listed[ahead], ahead).start())
        ready(first)
        pl.when(both)(lambda: ready(first + 1))
        panel = panels[pl.ds(first, 2)].reshape(2 * TILE, 2 * TILE)
        for c in range(cols_dev):
            span = slice(c * TILE, (c + 1) * TILE)
            change = dot(panel, own[:, span])
            for h in (0, 1):
                keep = mask[listed[first + h], c] > 0
                part = jnp.where(keep, change[h * TILE : (h + 1) * TILE], 0.0)
                before = old[first + h, :, span].astype(jnp.float32)
                new[first + h, :, span] = (before - part).astype(jnp.bfloat16)

        @pl.when(me[0] == 0)
        def _():
            for h in (0, 1):
                new[first + h, :, :TILE] = panels[first + h, :, :TILE]

                @pl.when(listed[first + h] > 1)
                def _():
                    new[first + h, :, TILE : 2 * TILE] = panels[first + h, :, TILE:]

        store(listed[first], first).start()
        pl.when(both)(lambda: store(listed[first + 1], first + 1).start())

    @pl.loop(0, total)
    def _(spot):
        store(0, spot).wait()

    if start:
        top_out.wait()


def update(table, mask, me, own, front, numbers, blocks, room, base=None):
    width = front.shape[1]
    count = len(numbers)
    operands = [table, mask, me, own, in_hbm(front), *[in_hbm(block) for block in blocks]]
    in_specs = [SMEM, SMEM, SMEM, VMEM, HBM] + [HBM] * count
    aliases = {}
    if base is not None:
        aliases = {len(operands): 0}
        operands.append(in_hbm(base))
        in_specs.append(HBM)
    return pl.pallas_call(
        functools.partial(update_kernel, tuple(numbers), room, width // TILE, base is None),
        out_shape=jax.ShapeDtypeStruct(front.shape, jnp.bfloat16),
        in_specs=in_specs,
        out_specs=HBM,
        scratch_shapes=[
            pltpu.VMEM((room, TILE, 2 * TILE), jnp.bfloat16),
            pltpu.VMEM((room, TILE, width), jnp.bfloat16),
            pltpu.VMEM((room + 1, TILE, width), jnp.bfloat16),
            pltpu.SMEM((room + 1,), jnp.int32),
            pltpu.SemaphoreType.DMA((room,)),
            pltpu.SemaphoreType.DMA((room + 1,)),
            pltpu.SemaphoreType.DMA((room + 1,)),
        ],
        input_output_aliases=aliases,
        compiler_params=pltpu.CompilerParams(vmem_limit_bytes=UPDATE_LIMIT),
        cost_estimate=pl.CostEstimate(
            flops=2 * room * TILE * width * 2 * TILE, bytes_accessed=4 * room * TILE * width, transcendentals=0
        ),
        name="update",
    )(*operands)


def after(values, *others):
    return lax.optimization_barrier((tuple(values), others))[0]


def one_of(g, members):
    result = g == members[0]
    for member in members[1:]:
        result = result | (g == member)
    return result


def shards(front_in, panel_inverse, tile_mask, tile_map):
    front = front_in[0]
    width = front.shape[1]
    tiles = front.shape[0] // TILE
    cols_dev = width // TILE
    inverse = panel_inverse[0]
    mask = tile_mask[0]
    targets = tile_map[0, 0]
    contrib = targets.shape[0]
    rows_out = contrib // cols_dev
    n_grp = lax.axis_size("grp")
    n_front = lax.axis_size("front")
    slots_dev = n_grp // 2
    g = lax.axis_index("grp")
    me = jnp.reshape(g, (1,)).astype(jnp.int32)
    root = g == 0

    perms, rules = routes(n_grp)
    lists = stream_plan(perms, rules, n_grp, tiles, cols_dev, rows_out)
    if n_grp == 8:
        lists = [lists[0] + lists[1][-1:], lists[1] + lists[0][-2 * CHAINS :]]
    got = travel(perms, rules, lists, n_grp, tiles)
    events = len(got)
    longest = max(len(lists[0]), len(lists[1]))

    order = [(e, lists[s][e]) for e in range(longest) for s in (0, 1) if e < len(lists[s])]
    order = [(e, tile) for n, (e, tile) in enumerate(order) if tile not in [other for _, other in order[:n]]]
    order.append((longest, 0))
    cuts = list(range(0, len(order) - 2, 4)) + [len(order)]
    made, parts, where_made = [], None, {}

    def make(e, turn):
        nonlocal parts
        while len(made) < len(cuts) - 1:
            begin, end = cuts[len(made)], cuts[len(made) + 1]
            if order[begin][0] > max(0, e + 1 if begin < 8 else e + 2):
                break
            names = [tile for _, tile in order[begin:end]]
            for n, tile in enumerate(names):
                where_made[tile] = (len(made), n)
            if parts is None:
                *made_now, parts, one = factor(front, mask, names, inverse=inverse)
                parts = (parts, one)
            else:
                made_now = factor(front, mask, names, parts=after(parts, *turn))
            made.append(made_now)

    make(-2, ())
    odd = [[n for n in range(n_grp) if rules[s][n] != rules[s][0]] for s in (0, 1)]
    others = [one_of(g, odd[s]) if odd[s] else None for s in (0, 1)]
    scalars = [value for value in (root, *others) if value is not None]
    table = []
    for n in range(n_grp):
        line = []
        for now in got:
            for arrival in now:
                line.append(arrival[n] if arrival[n] not in line else 0)
        table.append(line)
    rows = jnp.asarray(table, jnp.int32)
    used = [[any(line[2 * e + s] for line in table) for s in (0, 1)] for e in range(events)]
    for e in reversed(range(events - CHAINS)):
        for s in (0, 1):
            used[e][s] = used[e][s] or any(used[e + CHAINS])

    needed = [
        [n * cols_dev + c for c in range(cols_dev)] + [tiles - rows_out + r for r in range(rows_out)]
        for n in range(n_grp)
    ]
    ready = max(table[n].index(tile) // 2 for n in range(1, n_grp) for tile in needed[n])

    def own_part():
        blocks, names = [], {}

        def choice(tile, n):
            if n == 0:
                name = (-1, tile)
                which, place = where_made[tile]
                block = made[which][place]
            else:
                name = divmod(table[n].index(tile), 2)
                block = held[name[0]][name[1]]
            if name not in names:
                names[name] = len(blocks)
                blocks.append(block)
            return names[name]

        choices = [[choice(needed[n][part], n) for n in range(n_grp)] for part in range(cols_dev + rows_out)]
        return own_panels(mask, targets, me, front, blocks, choices, rows_out, n_front, n_grp * slots_dev)

    def exchange(blocks, axis):
        return lax.all_to_all(blocks, axis, split_axis=0, concat_axis=0, tiled=True)

    def relayed(arrived):
        digits = arrived[:, 2 * TILE, :4].astype(jnp.int32).reshape(n_front, 2, 2)
        return relay(digits[..., 0] * 32 + digits[..., 1], arrived, slots_dev, n_grp)

    held, turn, result, done = [], (), None, 0

    def step(count, *waits):
        nonlocal result, done
        numbers = [n for n in range(2 * done, 2 * (done + count)) if any(line[n] for line in table)]
        done += count
        here = after((me,), *waits)[0] if waits else me
        blocks = [held[n // 2][n % 2] for n in numbers]
        result = update(rows, mask, here, own, front, numbers, blocks, 2 * count, base=result)

    for e in range(events):
        values = []
        for s in (0, 1):
            value = None
            if e >= CHAINS:
                value = held[e - CHAINS][rules[s][0]]
                if others[s] is not None:
                    value = jnp.where(others[s], held[e - CHAINS][1 - rules[s][0]], value)
            if e < len(lists[s]):
                which, n = where_made[lists[s][e]]
                value = made[which][n] if value is None else jnp.where(root, made[which][n], value)
            values.append(value)
        turn = after(values, *turn, *(scalars if e == 0 else ()))
        held.append([lax.ppermute(turn[s], "grp", perms[s]) if used[e][s] else turn[s] for s in (0, 1)])
        make(e, turn)
        if CHAINS <= e + 1 < events:
            held[e + 1 - CHAINS] = list(after(held[e + 1 - CHAINS], *turn))
        late = e - ready - CHAINS
        if late == 0:
            own, sends = own_part()
            turn = (*turn, own)
        if late == 1:
            arrived = exchange(after((sends,), *turn)[0], "front")
        if late == 4:
            step(4, *turn)
            turn = (*turn, result)
    passed = relayed(after((arrived,), *turn, *held[-2])[0])
    arrived = exchange(passed, "grp")
    while done < events:
        step(min(8, events - done), passed)
    slots_here = after((arrived,), result)[0]
    parent_tiles = sum_parents(slots_here[:, TILE, 0].astype(jnp.int32), slots_here, slots_dev)
    return (result[None], parent_tiles)


def solution(mesh):
    in_specs = (
        P("front", None, "grp"),
        P("front", None, None, None),
        P("front", None, "grp"),
        P("front", "grp", None),
    )
    out_specs = (P("front", None, "grp"), P(("front", "grp"), None, None))
    return jax.shard_map(shards, mesh=mesh, in_specs=in_specs, out_specs=out_specs, check_vma=False)
```
